32 devices in a mesh: grp: 8 (over y, x, core), tp: 4 (over z).
Axes of the slice: x: 2, y: 2, z: 4, core: 2. Of those that a mesh axis runs over, the one named last changes fastest.
Arguments:
- comp_queries: bfloat16 [2048, 8192], P('grp', 'tp'), may hold values from -6 to 6
- comp_keys: bfloat16 [2048, 1024], P('grp', 'tp'), may hold values from -6 to 6
- comp_values: bfloat16 [2048, 1024], P('grp', 'tp'), may hold values from -6 to 6
- prompt_keys: bfloat16 [768, 1024], P('grp', 'tp'), may hold values from -6 to 6
- prompt_values: bfloat16 [768, 1024], P('grp', 'tp'), may hold values from -6 to 6
- query_gain: float32 [128], replicated, may hold values from 0.5 to 6
- key_gain: float32 [128], replicated, may hold values from 0.5 to 6
- out_grad: bfloat16 [2048, 8192], P('grp', 'tp'), may hold values from -18 to 18
- live_counts: int32 [8], P('grp'), may hold values from 1 to 4, as said below
- slot_prompts: int32 [32], P('grp'), may hold values from 0 to 1, as said below
Outputs:
- attended: bfloat16 [2048, 8192], P('grp', 'tp')
- query_grads: bfloat16 [2048, 8192], P('grp', 'tp')
- comp_key_grads: bfloat16 [2048, 1024], P('grp', 'tp')
- comp_value_grads: bfloat16 [2048, 1024], P('grp', 'tp')
- prompt_key_grads: float32 [768, 1024], P('grp', 'tp')
- prompt_value_grads: float32 [768, 1024], P('grp', 'tp')
- query_gain_grad: float32 [128], replicated
- key_gain_grad: float32 [128], replicated
The draws below stay inside these ranges and needn't reach their ends.
Inputs may be any that keep to these rules, and one draw needn't show every extreme that they name: Slot j of index s of grp is live exactly when j < live_counts[s]; some index has all 4 live and some has one. `slot_prompts`: the first slot of every index of grp is live; every prompt is named by some first slot.
All inputs are finite; a program needn't handle non-finite values.
Results may differ from the reference program's by a relative error of at most 0.033.
The reference program's roundings to bfloat16 on the way count: a program that leaves them out, or rounds other values in their place, can miss the bound.
Values may be sent and summed in bfloat16 or wider, within the bound.
No kernel may reach another device: no remote copies, remote signals or barrier semaphores. Data moves between devices by JAX's collectives and lax.ppermute only.
A program may use at most 64 MiB of HBM per device.

```python
import math
import jax
import jax.numpy as jnp
from jax import lax

H = 64
KVH = 8
HD = 128
PL = 384
CL = 64
SLOTS = 4
COMP_DEVS = 8
PROMPTS = 2
COMPLETIONS = 32
CTOKENS = 2048
POOL = 768


def draw_comp_queries(key, part):
    key = jax.random.fold_in(key, 11)
    return jnp.clip(jax.random.normal(key, (CTOKENS, H * HD), jnp.float32), -6.0, 6.0).astype(jnp.bfloat16)


def draw_prompt_keys(key, part):
    key = jax.random.fold_in(key, 13)
    return jnp.clip(jax.random.normal(key, (POOL, KVH * HD), jnp.float32), -6.0, 6.0).astype(jnp.bfloat16)


def gain_draw(key):
    return jnp.exp(jax.random.uniform(key, (HD,), jnp.float32, -0.69, 0.69))


def draw_query_gain(key, part):
    key = jax.random.fold_in(key, 17)
    return gain_draw(key)


def draw_key_gain(key, part):
    key = jax.random.fold_in(key, 19)
    return gain_draw(key)


def draw_out_grad(key, part):
    key = jax.random.fold_in(key, 23)
    rising = jnp.arange(CTOKENS).astype(jnp.float32) / CTOKENS
    noise_part = jnp.clip(jax.random.normal(key, (CTOKENS, H * HD), jnp.float32), -6.0, 6.0)
    return (noise_part * (1.0 + 2.0 * rising)[:, None]).astype(jnp.bfloat16)


def draw_live_counts(key, part):
    key = jax.random.fold_in(key, 29)
    subkeys = jax.random.split(key, 3)
    values = jax.random.randint(subkeys[0], (COMP_DEVS,), 1, SLOTS + 1)
    busiest = jax.random.randint(subkeys[1], (), 0, COMP_DEVS)
    lightest = (busiest + jax.random.randint(subkeys[2], (), 1, COMP_DEVS)) % COMP_DEVS
    position = jnp.arange(COMP_DEVS)
    values = jnp.where(position == busiest, SLOTS, values)
    return jnp.where(position == lightest, 1, values).astype(jnp.int32)


def draw_slot_prompts(key, part):
    key = jax.random.fold_in(key, 31)
    subkeys = jax.random.split(key, 2)
    shuffled = jax.random.permutation(subkeys[0], COMP_DEVS) % PROMPTS
    others = jax.random.randint(subkeys[1], (COMP_DEVS, SLOTS), 0, PROMPTS)
    column = jnp.arange(SLOTS)[None, :]
    return jnp.where(column == 0, shuffled[:, None], others).reshape(COMPLETIONS).astype(jnp.int32)


def levels(stream_key, shape, shards, least, largest):
    loudness, own = 1.0, jax.random.fold_in(stream_key, 6)
    for axis_at, shards_of in shards:
        heights = jnp.exp(jax.random.uniform(jax.random.fold_in(own, axis_at), (shards_of,), jnp.float32, least / len(shards), largest / len(shards)))
        loudness = loudness * jnp.repeat(heights, shape[axis_at] // shards_of).reshape([-1 if axis == axis_at else 1 for axis in range(len(shape))])
    return loudness


def gaussian(own_key, shape, width, limit, cuts=(), held_as=jnp.bfloat16):
    entries = jax.random.normal(own_key, shape, jnp.float32) * width
    if len(cuts) > 0:
        entries = levels(own_key, shape, cuts, -0.22, 0.18) * entries
    return jnp.clip(entries, min=-limit, max=limit).astype(held_as)


def setup_inputs(seed: int = 0) -> dict:
    key_of = jax.random.split(jax.random.key(seed), 11)
    return {
        "comp_queries": draw_comp_queries(jax.random.fold_in(key_of[10], 71), 0),
        "comp_keys": gaussian(key_of[1], (CTOKENS, KVH * HD), 1.0, 6.0, ((0, 8), (1, 4))),
        "comp_values": gaussian(key_of[2], (CTOKENS, KVH * HD), 1.0, 6.0, ((0, 8), (1, 4))),
        "prompt_keys": draw_prompt_keys(jax.random.fold_in(key_of[10], 71), 0),
        "prompt_values": gaussian(key_of[4], (POOL, KVH * HD), 1.0, 6.0, ((0, 8), (1, 4))),
        "query_gain": draw_query_gain(jax.random.fold_in(key_of[10], 71), 0),
        "key_gain": draw_key_gain(jax.random.fold_in(key_of[10], 71), 0),
        "out_grad": draw_out_grad(jax.random.fold_in(key_of[10], 71), 0),
        "live_counts": draw_live_counts(jax.random.fold_in(key_of[10], 71), 0),
        "slot_prompts": draw_slot_prompts(jax.random.fold_in(key_of[10], 71), 0),
    }


epsilon = 1e-06

def normalize(raw_rows, gain_row):
    values = raw_rows.astype(jnp.float32)
    reciprocal = lax.rsqrt(lax.optimization_barrier(jnp.mean(values * values, axis=-1, keepdims=True)) + epsilon)
    unit_rows = values * reciprocal
    return (unit_rows * gain_row, unit_rows, reciprocal)

def norm_back(upstream, unit_rows, reciprocal, gain_row):
    scaled = upstream * gain_row
    return reciprocal * (scaled - unit_rows * lax.optimization_barrier(jnp.mean(unit_rows * scaled, axis=-1, keepdims=True)))

def product(form, left, right):
    return jnp.einsum(form, left.astype(jnp.float32), right.astype(jnp.float32), precision=lax.Precision.HIGHEST)

def to_half(values):
    return lax.optimization_barrier(values.astype(jnp.bfloat16)).astype(jnp.float32)

def block_scores(queries, key_block):
    score_scale = 1.0 / math.sqrt(queries.shape[-1])
    return product('qkgd,nkd->kgqn', queries, key_block) * score_scale

def back_block(queries, grads_out, log_total, row_delta, key_block, value_block, allowed):
    score_scale = 1.0 / math.sqrt(queries.shape[-1])
    scores = block_scores(queries, key_block)
    probability = jnp.where(allowed, jnp.exp(scores - log_total[..., None]), 0.0)
    value_grad = product('kgqn,qkgd->nkd', to_half(probability), grads_out)
    prob_grad = product('qkgd,nkd->kgqn', grads_out, value_block)
    score_grad = to_half(probability * (prob_grad - row_delta[..., None]))
    query_grad = product('kgqn,nkd->qkgd', score_grad, key_block) * score_scale
    key_grad = product('kgqn,qkgd->nkd', score_grad, queries) * score_scale
    return (query_grad, key_grad, value_grad)

def reference(comp_queries, comp_keys, comp_values, prompt_keys, prompt_values, query_gain, key_gain, out_grad, live_counts, slot_prompts):
    group_size = H // KVH
    prompt_norm, prompt_unit, prompt_recip = normalize(prompt_keys.reshape(POOL, KVH, HD), key_gain)
    prompt_half = prompt_norm.astype(jnp.bfloat16)
    prompt_value_rows = prompt_values.reshape(POOL, KVH, HD)
    live_mask = jnp.arange(COMPLETIONS) % SLOTS < jnp.repeat(live_counts, SLOTS, total_repeat_length=COMPLETIONS)
    causal = jnp.arange(CL)[:, None] >= jnp.arange(CL)[None, :]
    allowed = jnp.concatenate([jnp.ones((CL, PL), bool), causal], axis=1)

    def scan_step(carried, scan_item):
        pool_key_grad, pool_value_grad, query_part, key_part = carried
        raw_queries, raw_keys, own_values, grads_out, prompt_no, alive = scan_item
        query_norm, query_unit, query_recip = normalize(raw_queries, query_gain)
        queries = query_norm.astype(jnp.bfloat16)
        key_norm, key_unit, key_recip = normalize(raw_keys, key_gain)
        own_keys = key_norm.astype(jnp.bfloat16)
        first_row = (prompt_no * PL).astype(jnp.int32)
        key_block = jnp.concatenate([lax.dynamic_slice_in_dim(prompt_half, first_row, PL, 0), own_keys], axis=0)
        value_block = jnp.concatenate([lax.dynamic_slice_in_dim(prompt_value_rows, first_row, PL, 0), own_values], axis=0)
        scores = jnp.where(allowed, block_scores(queries, key_block), -jnp.inf)
        row_high = lax.optimization_barrier(jnp.max(scores, axis=-1))
        weights = jnp.exp(scores - row_high[..., None])
        sum_total = lax.optimization_barrier(jnp.sum(weights, axis=-1))
        attended_rows = product('kgqn,nkd->kgqd', weights, value_block) / sum_total[..., None]
        log_total = row_high + jnp.log(sum_total)
        out_half = jnp.where(alive, jnp.transpose(attended_rows, (2, 0, 1, 3)), 0.0).astype(jnp.bfloat16)
        row_delta = jnp.transpose(lax.optimization_barrier(jnp.sum(grads_out.astype(jnp.float32) * out_half.astype(jnp.float32), axis=-1)), (1, 2, 0))
        query_grad, key_grad, value_grad = back_block(queries, grads_out, log_total, row_delta, key_block, value_block, allowed)
        query_grad = jnp.where(alive, query_grad, 0.0)
        key_grad = jnp.where(alive, key_grad, 0.0)
        value_grad = jnp.where(alive, value_grad, 0.0)
        prior_keys = lax.dynamic_slice_in_dim(pool_key_grad, first_row, PL, 0)
        pool_key_grad = lax.dynamic_update_slice_in_dim(pool_key_grad, prior_keys + key_grad[:PL], first_row, 0)
        prior_values = lax.dynamic_slice_in_dim(pool_value_grad, first_row, PL, 0)
        pool_value_grad = lax.dynamic_update_slice_in_dim(pool_value_grad, prior_values + value_grad[:PL], first_row, 0)
        query_part = query_part + lax.optimization_barrier(jnp.sum(query_grad * query_unit, axis=(0, 1, 2)))
        key_part = key_part + lax.optimization_barrier(jnp.sum(key_grad[PL:] * key_unit, axis=(0, 1)))
        query_out = norm_back(query_grad, query_unit, query_recip, query_gain).astype(jnp.bfloat16)
        key_out = norm_back(key_grad[PL:], key_unit, key_recip, key_gain).astype(jnp.bfloat16)
        value_out = value_grad[PL:].astype(jnp.bfloat16)
        return ((pool_key_grad, pool_value_grad, query_part, key_part), (out_half, query_out, key_out, value_out))
    start = (jnp.zeros((POOL, KVH, HD), jnp.float32), jnp.zeros((POOL, KVH, HD), jnp.float32), jnp.zeros((HD,), jnp.float32), jnp.zeros((HD,), jnp.float32))
    scan_items = (comp_queries.reshape(COMPLETIONS, CL, KVH, group_size, HD), comp_keys.reshape(COMPLETIONS, CL, KVH, HD), comp_values.reshape(COMPLETIONS, CL, KVH, HD), out_grad.reshape(COMPLETIONS, CL, KVH, group_size, HD), slot_prompts, live_mask)
    finals, stacked = lax.scan(scan_step, start, scan_items)
    pool_key_grad, pool_value_grad, query_part, key_part = finals
    out_half, query_out, key_out, value_out = stacked
    key_part = key_part + lax.optimization_barrier(jnp.sum(pool_key_grad * prompt_unit, axis=(0, 1)))
    prompt_key_grads = norm_back(pool_key_grad, prompt_unit, prompt_recip, key_gain).reshape(POOL, KVH * HD)
    prompt_value_grads = pool_value_grad.reshape(POOL, KVH * HD)
    return (out_half.reshape(CTOKENS, H * HD), query_out.reshape(CTOKENS, H * HD), key_out.reshape(CTOKENS, KVH * HD), value_out.reshape(CTOKENS, KVH * HD), prompt_key_grads, prompt_value_grads, query_part, key_part)
```

```python
import math

import jax
import jax.numpy as jnp
from jax import lax
from jax.experimental import pallas as pl
from jax.experimental.pallas import tpu as pltpu
from jax.sharding import PartitionSpec as P

PL = 384
CL = 64
EPS = 1e-06
TAIL = 16
VMEM_LIMIT = 48 * 1024 * 1024
F32 = jnp.float32
BF16 = jnp.bfloat16


def dot(left, right):
    return jnp.dot(left, right, preferred_element_type=F32)


def dot_nt(left, right):
    return lax.dot_general(left, right, (((1,), (1,)), ((), ())), preferred_element_type=F32)


def unit(raw):
    recip = lax.rsqrt(jnp.mean(raw * raw, axis=-1, keepdims=True) + EPS)
    return raw * recip, recip


def norm_back(upstream, unit_rows, recip, gain):
    scaled = upstream * gain
    return recip * (scaled - unit_rows * jnp.mean(unit_rows * scaled, axis=-1, keepdims=True))


def attention_kernel(
    live_ref, prompt_ref,
    q_ref, do_ref, ck_ref, cv_ref, pool_ref, qg_ref, kg_ref,
    att_ref, dq_ref, dk_ref, dv_ref, send_ref,
    acc, pool_unit, pool_keys, pool_keys_t, pool_values_t, qgain_col, qpart, kpart,
):
    slot = pl.program_id(0)
    size = qg_ref.shape[1]
    heads = ck_ref.shape[1] // size
    width = heads * size
    group = q_ref.shape[1] // width
    score_scale = 1.0 / math.sqrt(size)
    chunk_heads = min(group, 4)
    chunk = chunk_heads * CL

    @pl.when(slot == 0)
    def _():
        qgain_col[...] = jnp.broadcast_to(qg_ref[...], (size, size)).T
        qpart[...] = jnp.zeros_like(qpart)
        kpart[...] = jnp.zeros_like(kpart)
        acc[...] = jnp.zeros_like(acc)
        for head in range(heads):
            columns = slice(head * size, (head + 1) * size)
            unit_rows, _ = unit(pool_ref[:, columns].astype(F32))
            pool_unit[:, columns] = unit_rows
            keys = (unit_rows * kg_ref[...]).astype(BF16)
            pool_keys[:, columns] = keys
            pool_keys_t[columns, :] = keys.T
            pool_values_t[columns, :] = pool_ref[:, width + head * size:width + (head + 1) * size].T

    alive = slot < live_ref[0]

    @pl.when(jnp.logical_not(alive))
    def _():
        for ref in (att_ref, dq_ref, dk_ref, dv_ref):
            ref[...] = jnp.zeros_like(ref)

    @pl.when(alive)
    def _():
        first = pl.multiple_of(prompt_ref[slot] * PL, PL)
        rows = pl.ds(first, PL)
        gain_col = jnp.concatenate([qgain_col[...]] * (chunk // size), axis=1)

        def load_head(head):
            columns = slice(head * size, (head + 1) * size)
            own_unit, own_recip = unit(ck_ref[:, columns].astype(F32))
            own_keys = (own_unit * kg_ref[...]).astype(BF16)
            own_values = cv_ref[:, columns]
            keys = jnp.concatenate([pool_keys[rows, columns], own_keys], axis=0)
            values = jnp.concatenate(
                [pool_ref[rows, width + head * size:width + (head + 1) * size], own_values], axis=0
            )
            keys_t = jnp.concatenate([pool_keys_t[columns, rows], own_keys.T], axis=1)
            values_t = jnp.concatenate([pool_values_t[columns, rows], own_values.T], axis=1)
            values_t = jnp.concatenate([values_t, jnp.ones((16, PL + CL), BF16)], axis=0)
            return own_unit, own_recip, keys, values, keys_t, values_t

        def places(head, at):
            start = (head * group + at * chunk_heads) * size
            return [slice(start + g * size, start + (g + 1) * size) for g in range(chunk_heads)]

        def stack(ref, where):
            return jnp.concatenate([ref[:, place] for place in where], axis=0)

        def unstack(ref, where, values):
            for g, place in enumerate(where):
                ref[:, place] = values[g * CL:(g + 1) * CL]

        def begin(state):
            raw_t = stack(q_ref, state["where"]).T.astype(F32)
            state["recip"] = lax.rsqrt(jnp.mean(raw_t * raw_t, axis=0, keepdims=True) + EPS)
            state["unit"] = raw_t * state["recip"]
            state["queries"] = (state["unit"] * gain_col).astype(BF16)
            state["scores"] = dot(state["head"][2], state["queries"])

        def weigh(state):
            scores = state.pop("scores")
            own = scores[PL:]
            key_no = lax.broadcasted_iota(jnp.int32, own.shape, 0)
            token_no = lax.broadcasted_iota(jnp.int32, own.shape, 1) % CL
            own = jnp.where(key_no <= token_no, own, -jnp.inf)
            scores = jnp.concatenate([scores[:PL], own], axis=0)
            high = jnp.max(scores, axis=0, keepdims=True)
            state["weights"] = jnp.exp2((scores - high) * (score_scale * math.log2(math.e)))
            state["half"] = state["weights"].astype(BF16)
            state["summed"] = dot(state["head"][5], state["half"])

        def attend(state):
            summed = state.pop("summed")
            inverse = 1.0 / summed[size:size + 1]
            attended = (summed[:size] * inverse).astype(BF16)
            unstack(att_ref, state["where"], attended.T)
            grads = (stack(do_ref, state["where"]).T.astype(F32) * inverse).astype(BF16)
            state["grads"] = grads
            state["delta"] = jnp.sum(grads.astype(F32) * attended.astype(F32), axis=0, keepdims=True)
            state["prob_grad"] = dot(state["head"][3], grads)

        def back(state):
            state["value_grad"] = dot_nt(state.pop("half"), state.pop("grads"))
            score_grad = (state.pop("weights") * (state.pop("prob_grad") - state.pop("delta"))).astype(BF16)
            state["query_grad"] = dot(state["head"][4], score_grad)
            state["key_grad"] = dot_nt(score_grad, state.pop("queries"))

        def end(state):
            query_grad = state.pop("query_grad") * score_scale
            query_unit = state.pop("unit")
            part = query_grad * query_unit
            for at in range(0, chunk, size):
                qpart[...] += part[:, at:at + size]
            mean = jnp.mean(part * gain_col, axis=0, keepdims=True)
            query_out = state.pop("recip") * (query_grad * gain_col - query_unit * mean)
            unstack(dq_ref, state["where"], query_out.astype(BF16).T)

        loaded = [load_head(head) for head in range(heads)]
        states = [
            {"head": loaded[head], "where": places(head, at)}
            for head in range(heads)
            for at in range(group // chunk_heads)
        ]
        stages = (begin, weigh, attend, back, end)
        for tick in range(len(states) + len(stages) - 1):
            for number in range(len(stages)):
                if 0 <= tick - number < len(states):
                    stages[number](states[tick - number])

        per_head = group // chunk_heads
        for head in range(heads):
            own_unit, own_recip = loaded[head][:2]
            mine = states[head * per_head:(head + 1) * per_head]
            key_grad = sum(state["key_grad"] for state in mine) * score_scale
            value_grad = sum(state["value_grad"] for state in mine)
            start = 2 * head * size
            acc[rows, start:start + size] += key_grad[:PL]
            acc[rows, start + size:start + 2 * size] += value_grad[:PL]
            own_grad = key_grad[PL:]
            kpart[...] += jnp.sum(own_grad * own_unit, axis=0, keepdims=True)
            columns = slice(head * size, (head + 1) * size)
            dk_ref[:, columns] = norm_back(own_grad, own_unit, own_recip, kg_ref[...]).astype(BF16)
            dv_ref[:, columns] = value_grad[PL:].astype(BF16)

    @pl.when(slot == pl.num_programs(0) - 1)
    def _():
        key_part = kpart[...]
        for head in range(heads):
            terms = acc[:, 2 * head * size:(2 * head + 1) * size] * pool_unit[:, head * size:(head + 1) * size]
            key_part = key_part + jnp.sum(terms, axis=0, keepdims=True)
        query_part = jnp.sum(qpart[...].T, axis=0, keepdims=True)
        tail = []
        for part in (query_part, key_part):
            upper = part.astype(BF16).astype(F32)
            tail += [upper, part - upper]
        row = jnp.concatenate(tail + [jnp.zeros((1, 2 * width - 4 * size), F32)] * (2 * width > 4 * size), axis=1)
        row = jnp.broadcast_to(row, (TAIL, 2 * width))
        row = jnp.where(lax.broadcasted_iota(jnp.int32, row.shape, 0) == 0, row, 0.0).astype(BF16)
        blocks = send_ref.shape[0]
        shard = (send_ref.shape[1] - TAIL) if blocks > 1 else acc.shape[0]
        for at in range(blocks):
            send_ref[at, :shard, :] = acc[at * shard:(at + 1) * shard, :].astype(BF16)
            send_ref[at, shard:, :] = row


def attention(live_counts, slot_prompts, queries, out_grad, keys, values, pool, query_gain, key_gain, blocks):
    size = query_gain.shape[0]
    slots = slot_prompts.shape[0]
    width = keys.shape[1]
    pool_rows = pool.shape[0]
    smem = pl.BlockSpec(memory_space=pltpu.SMEM)
    token = pl.BlockSpec((CL, queries.shape[1]), lambda j: (j, 0))
    own = pl.BlockSpec((CL, width), lambda j: (j, 0))
    gain = pl.BlockSpec((1, size), lambda j: (0, 0))
    send = (blocks, pool_rows // blocks + TAIL, 2 * width)
    return pl.pallas_call(
        attention_kernel,
        grid=(slots,),
        in_specs=[smem, smem, token, token, own, own, pl.BlockSpec(pool.shape, lambda j: (0, 0)), gain, gain],
        out_specs=[token, token, own, own, pl.BlockSpec(send, lambda j: (0, 0, 0))],
        out_shape=[
            jax.ShapeDtypeStruct(queries.shape, BF16),
            jax.ShapeDtypeStruct(queries.shape, BF16),
            jax.ShapeDtypeStruct(keys.shape, BF16),
            jax.ShapeDtypeStruct(keys.shape, BF16),
            jax.ShapeDtypeStruct(send, BF16),
        ],
        scratch_shapes=[
            pltpu.VMEM((pool_rows, 2 * width), F32),
            pltpu.VMEM((pool_rows, width), F32),
            pltpu.VMEM((pool_rows, width), BF16),
            pltpu.VMEM((width, pool_rows), BF16),
            pltpu.VMEM((width, pool_rows), BF16),
            pltpu.VMEM((size, size), F32),
            pltpu.VMEM((size, size), F32),
            pltpu.VMEM((1, size), F32),
        ],
        compiler_params=pltpu.CompilerParams(vmem_limit_bytes=VMEM_LIMIT),
        name="attention",
    )(
        live_counts, slot_prompts, queries, out_grad, keys, values, pool,
        query_gain.reshape(1, size), key_gain.reshape(1, size),
    )


def finish_kernel(parts_ref, raw_ref, kg_ref, key_ref, value_ref):
    size = kg_ref.shape[1]
    shard = raw_ref.shape[0]
    total = parts_ref[0, :shard, :].astype(F32)
    for at in range(1, parts_ref.shape[0]):
        total = total + parts_ref[at, :shard, :].astype(F32)
    for head in range(raw_ref.shape[1] // size):
        columns = slice(head * size, (head + 1) * size)
        unit_rows, recip = unit(raw_ref[:, columns].astype(F32))
        at = 2 * head * size
        key_ref[:, columns] = norm_back(total[:, at:at + size], unit_rows, recip, kg_ref[...])
        value_ref[:, columns] = total[:, at + size:at + 2 * size]


def finish(parts, raw, key_gain):
    shape = jax.ShapeDtypeStruct(raw.shape, F32)
    return pl.pallas_call(
        finish_kernel,
        out_shape=[shape, shape],
        compiler_params=pltpu.CompilerParams(vmem_limit_bytes=VMEM_LIMIT),
        cost_estimate=pl.CostEstimate(flops=20 * raw.size, bytes_accessed=2 * parts.size, transcendentals=0),
        name="finish",
    )(parts, raw, key_gain.reshape(1, -1))


def sum_over(values, axis):
    count = lax.axis_size(axis)
    terms = [values] + [
        lax.ppermute(values, axis, [(i, i ^ step) for i in range(count)]) for step in range(1, count)
    ]
    while len(terms) > 1:
        terms = [left + right for left, right in zip(terms[::2], terms[1::2])]
    return terms[0]


def local(
    comp_queries, comp_keys, comp_values, prompt_keys, prompt_values,
    query_gain, key_gain, out_grad, live_counts, slot_prompts,
):
    grp = lax.axis_size("grp")
    shard, width = prompt_keys.shape
    size = query_gain.shape[0]
    mine = jnp.concatenate([prompt_keys, prompt_values], axis=1)
    copies = jnp.broadcast_to(mine, (grp,) + mine.shape)
    pool = lax.all_to_all(copies, "grp", 0, 0, tiled=True).reshape(grp * shard, 2 * width)
    blocks = grp if shard % TAIL == 0 else 1
    attended, query_grads, key_grads, value_grads, send = attention(
        live_counts, slot_prompts, comp_queries, out_grad, comp_keys, comp_values, pool,
        query_gain, key_gain, blocks,
    )
    if blocks == 1:
        tail = jnp.broadcast_to(send[:, grp * shard:], (grp, TAIL, 2 * width))
        send = jnp.concatenate([send[0, :grp * shard].reshape(grp, shard, 2 * width), tail], axis=1)
    parts = lax.all_to_all(send, "grp", 0, 0, tiled=True)
    gains = jnp.sum(parts[:, shard, :4 * size].astype(F32).reshape(grp, 2, 2, size), axis=(0, 2))
    gains = sum_over(gains, "tp")
    prompt_key_grads, prompt_value_grads = finish(parts, prompt_keys, key_gain)
    return (
        attended, query_grads, key_grads, value_grads,
        prompt_key_grads, prompt_value_grads, gains[0], gains[1],
    )


def solution(mesh):
    split, whole = P("grp", "tp"), P()
    return jax.shard_map(
        local,
        mesh=mesh,
        in_specs=(split, split, split, split, split, whole, whole, split, P("grp"), P("grp")),
        out_specs=(split, split, split, split, split, split, whole, whole),
        check_vma=False,
    )
```

```python
import functools
import math

import jax
import jax.numpy as jnp
from jax import lax
from jax.experimental import pallas as pl
from jax.experimental.pallas import tpu as pltpu
from jax.sharding import PartitionSpec as P

PL = 384
CL = 64
EPS = 1e-06
TAIL = 16
CHUNK = 256
VMEM_LIMIT = 24 * 1024 * 1024
F32 = jnp.float32
BF16 = jnp.bfloat16
SMEM_SPEC = pl.BlockSpec(memory_space=pltpu.SMEM)
VMEM_SPEC = pl.BlockSpec(memory_space=pltpu.VMEM)
HBM_SPEC = pl.BlockSpec(memory_space=pltpu.HBM)


def dot(left, right):
    return jnp.dot(left, right, preferred_element_type=F32)


def dot_nt(left, right):
    return lax.dot_general(left, right, (((1,), (1,)), ((), ())), preferred_element_type=F32)


def unit(raw):
    recip = lax.rsqrt(jnp.mean(raw * raw, axis=-1, keepdims=True) + EPS)
    return raw * recip, recip


def norm_back(upstream, unit_rows, recip, gain):
    scaled = upstream * gain
    return recip * (scaled - unit_rows * jnp.mean(unit_rows * scaled, axis=-1, keepdims=True))


def halves(row):
    upper = row.astype(BF16)
    return [upper, (row - upper.astype(F32)).astype(BF16)]


def gain_rows(term, wide):
    row = jnp.concatenate([part.astype(F32) for part in halves(term)], axis=1)
    if wide > row.shape[1]:
        row = jnp.concatenate([row, jnp.zeros((1, wide - row.shape[1]), F32)], axis=1)
    rows = jnp.broadcast_to(row, (TAIL, wide))
    return jnp.where(lax.broadcasted_iota(jnp.int32, rows.shape, 0) == 0, rows, 0.0).astype(BF16)


def gain_term(rows, size):
    row = rows.astype(F32)[0:1]
    return row[:, :size] + row[:, size:2 * size]


def params(limit=VMEM_LIMIT):
    return pltpu.CompilerParams(vmem_limit_bytes=limit)


def cost(flops, size):
    return pl.CostEstimate(flops=flops, bytes_accessed=size, transcendentals=0)


def gains_kernel(qg_ref, kg_ref, query_col_ref, key_row_ref):
    size = qg_ref.shape[1]
    column = jnp.broadcast_to(qg_ref[...], (size, size)).T
    for at in range(0, query_col_ref.shape[1], size):
        query_col_ref[:, at:at + size] = column
    key_row_ref[...] = jnp.broadcast_to(kg_ref[...], key_row_ref.shape)


def spread_gains(query_gain, key_gain, lanes):
    size = query_gain.shape[0]
    return pl.pallas_call(
        gains_kernel,
        in_specs=[VMEM_SPEC] * 2,
        out_specs=[VMEM_SPEC] * 2,
        out_shape=[jax.ShapeDtypeStruct((size, lanes), F32), jax.ShapeDtypeStruct((8, size), F32)],
        compiler_params=params(),
        cost_estimate=cost(4 * 10**9, 10**6),
        name="spread_gains",
    )(query_gain.reshape(1, size), key_gain.reshape(1, size))


def pack_kernel(keys_ref, values_ref, kg_ref, out_ref):
    size, width = kg_ref.shape[1], keys_ref.shape[1]
    for head in range(width // size):
        columns = slice(head * size, (head + 1) * size)
        unit_rows, _ = unit(keys_ref[:, columns].astype(F32))
        out_ref[:, columns] = (unit_rows * kg_ref[0:1, :]).astype(BF16)
    out_ref[:, width:] = values_ref[...]


def pack(keys, values, key_row):
    return pl.pallas_call(
        pack_kernel,
        in_specs=[VMEM_SPEC] * 3,
        out_specs=VMEM_SPEC,
        out_shape=jax.ShapeDtypeStruct((keys.shape[0], 2 * keys.shape[1]), BF16),
        compiler_params=params(),
        cost_estimate=cost(4 * 10**9, 10**6),
        name="pack",
    )(keys, values, key_row)


def head_columns(head, group, size):
    return [slice((head * group + g) * size, (head * group + g + 1) * size) for g in range(group)]


def slot_rows(slot):
    return pl.ds(pl.multiple_of(slot * CL, CL), CL)


def prepare_kernel(live_ref, q_ref, do_ref, col_ref, raw_ref, recip_ref, queries_ref, grads_ref):
    size = col_ref.shape[0]
    heads = raw_ref.shape[1] // size
    group = q_ref.shape[1] // raw_ref.shape[1]

    def live(slot, carry):
        for head in range(heads):
            places = head_columns(head, group, size)
            rows = slice(head * size, (head + 1) * size)
            half = jnp.concatenate([q_ref[slot_rows(slot), place] for place in places], axis=0).T
            raw_ref[slot, rows, :] = half
            raw = half.astype(F32)
            recip = lax.rsqrt(jnp.mean(raw * raw, axis=0, keepdims=True) + EPS)
            recip_ref[slot, head:head + 1, :] = recip
            queries_ref[slot, rows, :] = (raw * recip * col_ref[...]).astype(BF16)
            grads_ref[slot, rows, :] = jnp.concatenate([do_ref[slot_rows(slot), place] for place in places], axis=0).T
        return carry

    lax.fori_loop(0, live_ref[0], live, 0)


def prepare(live_counts, queries, out_grad, query_col, slots, width):
    lanes = query_col.shape[1]
    turned = jax.ShapeDtypeStruct((slots, width, lanes), BF16)
    return pl.pallas_call(
        prepare_kernel,
        in_specs=[SMEM_SPEC] + [VMEM_SPEC] * 3,
        out_specs=[VMEM_SPEC] * 4,
        out_shape=[turned, jax.ShapeDtypeStruct((slots, 8, lanes), F32), turned, turned],
        compiler_params=params(),
        cost_estimate=cost(2 * 10**9, 6 * queries.size),
        name="prepare",
    )(live_counts, queries, out_grad, query_col)


def attention_kernel(*refs, parts, heads):
    live_ref, prompt_ref, me_ref, queries_ref, grads_ref, ck_ref, cv_ref, kg_ref = refs[:8]
    pieces, refs = refs[8:8 + parts], refs[8 + parts:]
    att_ref, ds_ref, pool_keys, own_keys_ref, dk_ref, dv_ref, keep_ref, send_ref = refs[:8]
    acc, pool_values, pool_values_t, term = refs[8:]
    size = kg_ref.shape[1]
    width = heads * size
    slots, _, lanes = queries_ref.shape
    per_head = lanes // CHUNK
    score_scale = 1.0 / math.sqrt(size)
    shard = pieces[0].shape[0]
    gain = kg_ref[0:1, :]

    def piece_rows(piece_no):
        return pl.ds(pl.multiple_of((me_ref[0] ^ piece_no) * shard, shard), shard)

    term[...] = jnp.zeros_like(term)
    acc[...] = jnp.zeros_like(acc)
    for piece_no, piece in enumerate(pieces):
        pool_keys[piece_rows(piece_no), :] = piece[:, :width]
        pool_values[piece_rows(piece_no), :] = piece[:, width:]
    for head in range(heads):
        columns = slice(head * size, (head + 1) * size)
        pool_values_t[columns, :] = pool_values[:, columns].T

    def dead(slot, carry):
        dk_ref[slot_rows(slot), :] = jnp.zeros((CL, width), BF16)
        dv_ref[slot_rows(slot), :] = jnp.zeros((CL, width), BF16)
        return carry

    def live(slot, carry):
        rows = pl.ds(pl.multiple_of(prompt_ref[slot] * PL, PL), PL)

        def load_head(head):
            columns = slice(head * size, (head + 1) * size)
            own_unit, own_recip = unit(ck_ref[slot_rows(slot), columns].astype(F32))
            own_keys = (own_unit * gain).astype(BF16)
            own_keys_ref[slot_rows(slot), columns] = own_keys
            own_values = cv_ref[slot_rows(slot), columns]
            keys = jnp.concatenate([pool_keys[rows, columns], own_keys], axis=0)
            values = jnp.concatenate([pool_values[rows, columns], own_values], axis=0)
            values_t = jnp.concatenate([pool_values_t[columns, rows], own_values.T], axis=1)
            values_t = jnp.concatenate([values_t, jnp.ones((TAIL, PL + CL), BF16)], axis=0)
            return own_unit, own_recip, keys, values, values_t

        def begin(state):
            state["queries"] = queries_ref[slot, state["rows"], state["lanes"]]
            state["scores"] = dot(state["head"][2], state["queries"])

        def weigh(state):
            scores = state.pop("scores")
            own = scores[PL:]
            key_no = lax.broadcasted_iota(jnp.int32, own.shape, 0)
            token_no = lax.broadcasted_iota(jnp.int32, own.shape, 1) % CL
            own = jnp.where(key_no <= token_no, own, -jnp.inf)
            scores = jnp.concatenate([scores[:PL], own], axis=0)
            high = jnp.max(scores, axis=0, keepdims=True)
            state["weights"] = jnp.exp2((scores - high) * (score_scale * math.log2(math.e)))
            state["half"] = state["weights"].astype(BF16)
            state["summed"] = dot(state["head"][4], state["half"])

        def attend(state):
            summed = state.pop("summed")
            inverse = 1.0 / summed[size:size + 1]
            attended = (summed[:size] * inverse).astype(BF16)
            att_ref[slot, state["rows"], state["lanes"]] = attended
            grads = (grads_ref[slot, state["rows"], state["lanes"]].astype(F32) * inverse).astype(BF16)
            state["grads"] = grads
            state["delta"] = jnp.sum(grads.astype(F32) * attended.astype(F32), axis=0, keepdims=True)
            state["prob_grad"] = dot(state["head"][3], grads)

        def back(state):
            state["value_grad"] = dot_nt(state.pop("half"), state.pop("grads"))
            score_grad = (state.pop("weights") * (state.pop("prob_grad") - state.pop("delta"))).astype(BF16)
            ds_ref[slot, state["head_no"], :, state["lanes"]] = score_grad
            state["key_grad"] = dot_nt(score_grad, state.pop("queries"))

        loaded = [load_head(head) for head in range(heads)]
        states = [
            {
                "head": loaded[head],
                "head_no": head,
                "rows": slice(head * size, (head + 1) * size),
                "lanes": slice(at * CHUNK, (at + 1) * CHUNK),
            }
            for head in range(heads)
            for at in range(per_head)
        ]
        stages = (begin, weigh, attend, back)
        for tick in range(len(states) + len(stages) - 1):
            for number in range(len(stages)):
                if 0 <= tick - number < len(states):
                    stages[number](states[tick - number])

        for head in range(heads):
            own_unit, own_recip, keys = loaded[head][:3]
            mine = states[head * per_head:(head + 1) * per_head]
            key_grad = sum(state["key_grad"] for state in mine) * score_scale
            value_grad = sum(state["value_grad"] for state in mine)
            columns = slice(head * size, (head + 1) * size)
            acc[rows, columns] += key_grad[:PL]
            acc[rows, width + head * size:width + (head + 1) * size] += value_grad[:PL]
            own_grad = key_grad[PL:]
            term[...] += jnp.sum(own_grad * keys[PL:].astype(F32), axis=0, keepdims=True)
            dk_ref[slot_rows(slot), columns] = norm_back(own_grad, own_unit, own_recip, gain).astype(BF16)
            dv_ref[slot_rows(slot), columns] = value_grad[PL:].astype(BF16)
        return carry

    lax.fori_loop(0, live_ref[0], live, 0)
    lax.fori_loop(live_ref[0], slots, dead, 0)

    total = term[...]
    for head in range(heads):
        columns = slice(head * size, (head + 1) * size)
        total = total + jnp.sum(acc[:, columns] * pool_keys[:, columns].astype(F32), axis=0, keepdims=True)
    if parts == 1:
        keep_ref[...] = acc[...]
        send_ref[...] = jnp.concatenate([total, jnp.zeros((7, size), F32)], axis=0)
    else:
        for piece_no in range(parts):
            place = slice(piece_no // 2 * shard, (piece_no // 2 + 1) * shard)
            if piece_no % 2 == 0:
                keep_ref[place, :] = acc[piece_rows(piece_no), :]
            else:
                send_ref[place, :] = acc[piece_rows(piece_no), :].astype(BF16)
        tail = gain_rows(total, 2 * width)
        send_ref[parts // 2 * shard:, :] = tail
        keep_ref[parts // 2 * shard:, :] = tail.astype(F32)


def attention(live_counts, slot_prompts, me, queries, grads, keys, values, key_row, pieces):
    size = key_row.shape[1]
    slots, width, lanes = queries.shape
    heads = width // size
    parts = len(pieces)
    pool_rows = parts * pieces[0].shape[0]
    own = jax.ShapeDtypeStruct(keys.shape, BF16)
    out_shape = [
        jax.ShapeDtypeStruct(queries.shape, BF16),
        jax.ShapeDtypeStruct((slots, heads, PL + CL, lanes), BF16),
        jax.ShapeDtypeStruct((pool_rows, width), BF16),
        own, own, own,
    ]
    if parts > 1:
        half = (pool_rows // 2 + TAIL, 2 * width)
        out_shape += [jax.ShapeDtypeStruct(half, F32), jax.ShapeDtypeStruct(half, BF16)]
    else:
        out_shape += [jax.ShapeDtypeStruct((pool_rows, 2 * width), F32), jax.ShapeDtypeStruct((8, size), F32)]
    return pl.pallas_call(
        functools.partial(attention_kernel, parts=parts, heads=heads),
        in_specs=[SMEM_SPEC] * 3 + [VMEM_SPEC] * (5 + parts),
        out_specs=[VMEM_SPEC] * 8,
        out_shape=out_shape,
        scratch_shapes=[
            pltpu.VMEM((pool_rows, 2 * width), F32),
            pltpu.VMEM((pool_rows, width), BF16),
            pltpu.VMEM((width, pool_rows), BF16),
            pltpu.VMEM((1, size), F32),
        ],
        compiler_params=params(),
        cost_estimate=cost(3 * 10**9, 10**7),
        name="attention",
    )(live_counts, slot_prompts, me, queries, grads, keys, values, key_row, *pieces)


def post_kernel(
    live_ref, prompt_ref, att_t_ref, ds_ref, pool_keys, own_keys_ref, raw_ref, recip_ref, col_ref,
    att_ref, dq_ref, att_out, dq_out, sems,
):
    slots, width, lanes = raw_ref.shape
    size = col_ref.shape[0]
    heads = width // size
    group = att_ref.shape[1] // width
    score_scale = 1.0 / math.sqrt(size)

    def copy_out(slot, which):
        source, target = ((att_out, att_ref), (dq_out, dq_ref))[which]
        return pltpu.make_async_copy(source.at[slot], target.at[slot_rows(slot), :], sems.at[which, slot])

    def dead(slot, carry):
        att_out[slot] = jnp.zeros(att_out.shape[1:], BF16)
        dq_out[slot] = jnp.zeros(dq_out.shape[1:], BF16)
        for which in range(2):
            copy_out(slot, which).start()
        return carry

    def live(slot, carry):
        rows = pl.ds(pl.multiple_of(prompt_ref[slot] * PL, PL), PL)
        for head in range(heads):
            columns = slice(head * size, (head + 1) * size)
            keys_t = jnp.concatenate([pool_keys[rows, columns], own_keys_ref[slot_rows(slot), columns]], axis=0).T
            query_grad = dot(keys_t, ds_ref[slot, head]) * score_scale
            recip = recip_ref[slot, head:head + 1, :]
            query_unit = raw_ref[slot, columns, :].astype(F32) * recip
            scaled = query_grad * col_ref[...]
            mean = jnp.mean(query_unit * scaled, axis=0, keepdims=True)
            query_out = (recip * (scaled - query_unit * mean)).astype(BF16).T
            attended = att_t_ref[slot, columns, :].T
            for g, place in enumerate(head_columns(head, group, size)):
                att_out[slot, :, place] = attended[g * CL:(g + 1) * CL]
                dq_out[slot, :, place] = query_out[g * CL:(g + 1) * CL]
        for which in range(2):
            copy_out(slot, which).start()
        return carry

    lax.fori_loop(live_ref[0], slots, dead, 0)
    lax.fori_loop(0, live_ref[0], live, 0)
    for slot in range(slots):
        for which in range(2):
            copy_out(slot, which).wait()


def post(live_counts, slot_prompts, att_t, score_grads, pool_keys, own_keys, raw, recip, query_col, shape):
    slots = raw.shape[0]
    out = jax.ShapeDtypeStruct(shape, BF16)
    slab = pltpu.VMEM((slots, CL, shape[1]), BF16)
    return pl.pallas_call(
        post_kernel,
        in_specs=[SMEM_SPEC] * 2 + [VMEM_SPEC] * 7,
        out_specs=[HBM_SPEC] * 2,
        out_shape=[out, out],
        scratch_shapes=[slab, slab, pltpu.SemaphoreType.DMA((2, slots))],
        compiler_params=params(),
        cost_estimate=cost(3 * 10**9, 4 * 10**6),
        name="post",
    )(live_counts, slot_prompts, att_t, score_grads, pool_keys, own_keys, raw, recip, query_col)


def tree(terms):
    while len(terms) > 1:
        terms = [left + right for left, right in zip(terms[::2], terms[1::2])]
    return terms[0]


def add_kernel(keep_ref, came_ref, own_ref, *send_refs, size):
    blocks = len(send_refs) + 1
    shard = (keep_ref.shape[0] - TAIL) // blocks
    mine = gain_term(keep_ref[blocks * shard:, :], size)
    other = gain_term(came_ref[blocks * shard:, :], size)
    tail = gain_rows(mine + other, keep_ref.shape[1])
    for at in range(blocks):
        place = slice(at * shard, (at + 1) * shard)
        total = keep_ref[place, :] + came_ref[place, :].astype(F32)
        if at == 0:
            own_ref[:shard, :] = total
            own_ref[shard:, :] = tail.astype(F32)
        else:
            send_refs[at - 1][:shard, :] = total.astype(BF16)
            send_refs[at - 1][shard:, :] = tail


def add(keep, came, blocks, size):
    wide = keep.shape[1]
    shape = ((keep.shape[0] - TAIL) // blocks + TAIL, wide)
    return pl.pallas_call(
        functools.partial(add_kernel, size=size),
        in_specs=[VMEM_SPEC] * 2,
        out_specs=[VMEM_SPEC] * blocks,
        out_shape=[jax.ShapeDtypeStruct(shape, F32)] + [jax.ShapeDtypeStruct(shape, BF16)] * (blocks - 1),
        compiler_params=params(),
        name="add",
    )(keep, came)


def chips_kernel(*refs, size):
    total = tree([gain_term(ref[ref.shape[0] - TAIL:, :], size) for ref in refs[:-1]])
    refs[-1][...] = jnp.broadcast_to(total, refs[-1].shape)


def sum_chips(blocks, size):
    return pl.pallas_call(
        functools.partial(chips_kernel, size=size),
        in_specs=[VMEM_SPEC] * len(blocks),
        out_specs=VMEM_SPEC,
        out_shape=jax.ShapeDtypeStruct((8, size), F32),
        compiler_params=params(),
        name="sum_chips",
    )(*blocks)


def last_kernel(*refs):
    terms, (qg_ref, kg_ref, query_ref, key_ref) = refs[:-4], refs[-4:]
    total = tree([ref[0:1, :] for ref in terms])
    query_ref[...] = total / qg_ref[...]
    key_ref[...] = total / kg_ref[...]


def gain_grads(terms, query_gain, key_gain):
    row = jax.ShapeDtypeStruct((1, query_gain.shape[0]), F32)
    return pl.pallas_call(
        last_kernel,
        in_specs=[VMEM_SPEC] * (len(terms) + 2),
        out_specs=[VMEM_SPEC] * 2,
        out_shape=[row, row],
        compiler_params=params(),
        name="gain_grads",
    )(*terms, query_gain.reshape(1, -1), key_gain.reshape(1, -1))


def finish_kernel(*refs):
    parts, (raw_ref, kg_ref, key_ref, value_ref) = refs[:-4], refs[-4:]
    size = kg_ref.shape[1]
    shard, width = raw_ref.shape
    total = parts[0][:shard, :]
    for ref in parts[1:]:
        total = total + ref[:shard, :].astype(F32)
    for head in range(width // size):
        columns = slice(head * size, (head + 1) * size)
        unit_rows, recip = unit(raw_ref[:, columns].astype(F32))
        key_ref[:, columns] = norm_back(total[:, columns], unit_rows, recip, kg_ref[0:1, :])
    value_ref[...] = total[:, width:]


def finish(blocks, raw, key_row):
    shape = jax.ShapeDtypeStruct(raw.shape, F32)
    return pl.pallas_call(
        finish_kernel,
        in_specs=[VMEM_SPEC] * (len(blocks) + 2),
        out_specs=[VMEM_SPEC] * 2,
        out_shape=[shape, shape],
        compiler_params=params(),
        cost_estimate=cost(10**8, 10**6),
        name="finish",
    )(*blocks, raw, key_row)


def swap(values, axis, step):
    return lax.ppermute(values, axis, [(i, i ^ step) for i in range(lax.axis_size(axis))])


def local(
    comp_queries, comp_keys, comp_values, prompt_keys, prompt_values,
    query_gain, key_gain, out_grad, live_counts, slot_prompts,
):
    grp, tp = lax.axis_size("grp"), lax.axis_size("tp")
    shard = prompt_keys.shape[0]
    size = query_gain.shape[0]
    by_permute = shard % 16 == 0 and grp > 1 and grp & (grp - 1) == 0 and tp & (tp - 1) == 0
    slots, width = slot_prompts.shape[0], comp_keys.shape[1]
    query_col, key_row = spread_gains(query_gain, key_gain, comp_queries.shape[1] // width * CL)
    mine = pack(prompt_keys, prompt_values, key_row)
    raw, recip, queries, grads = prepare(live_counts, comp_queries, out_grad, query_col, slots, width)
    if by_permute:
        me = lax.axis_index("grp").astype(jnp.int32).reshape(1)
        even = [mine] + [swap(mine, "grp", step) for step in range(2, grp, 2)]
        odd = [swap(mine, "grp", 1)]
        even, queries = lax.optimization_barrier((even, queries))
        odd += [swap(piece, "grp", 1) for piece in even[1:]]
        pieces = [piece for pair in zip(even, odd) for piece in pair]
    else:
        me = jnp.zeros((1,), jnp.int32)
        pieces = [lax.all_gather(mine, "grp", axis=0, tiled=True)]
    att_t, score_grads, pool_keys, own_keys, key_grads, value_grads, keep, send = attention(
        live_counts, slot_prompts, me, queries, grads, comp_keys, comp_values, key_row, pieces,
    )
    attended, query_grads = post(
        live_counts, slot_prompts, att_t, score_grads, pool_keys, own_keys, raw, recip, query_col, comp_queries.shape,
    )
    if by_permute:
        own, *blocks = add(keep, swap(send, "grp", 1), grp // 2, size)
        blocks = [own] + [swap(block, "grp", 2 * at + 2) for at, block in enumerate(blocks)]
        blocks, attended = lax.optimization_barrier((blocks, attended))
        total = sum_chips(blocks, size)
        terms = [total] + [swap(total, "tp", step) for step in range(1, tp)]
    else:
        blocks = [lax.psum_scatter(keep, "grp", scatter_dimension=0, tiled=True)]
        terms = [lax.psum(send, ("grp", "tp"))]
    prompt_key_grads, prompt_value_grads = finish(blocks, prompt_keys, key_row)
    query_gain_grad, key_gain_grad = gain_grads(terms, query_gain, key_gain)
    return (
        attended, query_grads, key_grads, value_grads, prompt_key_grads, prompt_value_grads,
        query_gain_grad.reshape(size), key_gain_grad.reshape(size),
    )


def solution(mesh):
    split, whole = P("grp", "tp"), P()
    return jax.shard_map(
        local,
        mesh=mesh,
        in_specs=(split, split, split, split, split, whole, whole, split, P("grp"), P("grp")),
        out_specs=(split, split, split, split, split, split, whole, whole),
        check_vma=False,
    )
```

```python
import functools
import math

import jax
import jax.numpy as jnp
from jax import lax
from jax.experimental import pallas as pl
from jax.experimental.pallas import tpu as pltpu
from jax.sharding import PartitionSpec as P

PL = 384
CL = 64
EPS = 1e-06
TAIL = 16
CHUNK = 256
VMEM_LIMIT = 24 * 1024 * 1024
F32 = jnp.float32
BF16 = jnp.bfloat16
SMEM_SPEC = pl.BlockSpec(memory_space=pltpu.SMEM)
VMEM_SPEC = pl.BlockSpec(memory_space=pltpu.VMEM)
HBM_SPEC = pl.BlockSpec(memory_space=pltpu.HBM)


def dot(left, right):
    return jnp.dot(left, right, preferred_element_type=F32)


def dot_nt(left, right):
    return lax.dot_general(left, right, (((1,), (1,)), ((), ())), preferred_element_type=F32)


def unit(raw):
    recip = lax.rsqrt(jnp.mean(raw * raw, axis=-1, keepdims=True) + EPS)
    return raw * recip, recip


def norm_back(upstream, unit_rows, recip, gain):
    scaled = upstream * gain
    return recip * (scaled - unit_rows * jnp.mean(unit_rows * scaled, axis=-1, keepdims=True))


def halves(row):
    upper = row.astype(BF16)
    return [upper, (row - upper.astype(F32)).astype(BF16)]


def gain_rows(term, wide):
    row = jnp.concatenate([part.astype(F32) for part in halves(term)], axis=1)
    if wide > row.shape[1]:
        row = jnp.concatenate([row, jnp.zeros((1, wide - row.shape[1]), F32)], axis=1)
    rows = jnp.broadcast_to(row, (TAIL, wide))
    return jnp.where(lax.broadcasted_iota(jnp.int32, rows.shape, 0) == 0, rows, 0.0).astype(BF16)


def gain_term(rows, size):
    row = rows.astype(F32)[0:1]
    return row[:, :size] + row[:, size:2 * size]


def params(limit=VMEM_LIMIT):
    return pltpu.CompilerParams(vmem_limit_bytes=limit)


def cost(flops, size):
    return pl.CostEstimate(flops=flops, bytes_accessed=size, transcendentals=0)


def causal_kernel(mask_ref):
    key_no = lax.broadcasted_iota(jnp.int32, mask_ref.shape, 0)
    token_no = lax.broadcasted_iota(jnp.int32, mask_ref.shape, 1) % CL
    mask_ref[...] = jnp.where(key_no <= token_no, 0.0, -jnp.inf)


def causal():
    return pl.pallas_call(
        causal_kernel,
        out_specs=VMEM_SPEC,
        out_shape=jax.ShapeDtypeStruct((CL, CHUNK), F32),
        compiler_params=params(),
        cost_estimate=cost(4 * 10**9, 10**6),
        name="causal",
    )()


def pack_kernel(keys_ref, values_ref, kg_ref, out_ref):
    size, width = kg_ref.shape[1], keys_ref.shape[1]
    for head in range(width // size):
        columns = slice(head * size, (head + 1) * size)
        unit_rows, _ = unit(keys_ref[:, columns].astype(F32))
        out_ref[:, columns] = (unit_rows * kg_ref[...]).astype(BF16)
    out_ref[:, width:] = values_ref[...]


def pack(keys, values, key_gain):
    return pl.pallas_call(
        pack_kernel,
        in_specs=[VMEM_SPEC] * 3,
        out_specs=VMEM_SPEC,
        out_shape=jax.ShapeDtypeStruct((keys.shape[0], 2 * keys.shape[1]), BF16),
        compiler_params=params(),
        cost_estimate=cost(4 * 10**9, 10**6),
        name="pack",
    )(keys, values, key_gain)


def head_columns(head, group, size):
    return [slice((head * group + g) * size, (head * group + g + 1) * size) for g in range(group)]


def slot_rows(slot):
    return pl.ds(pl.multiple_of(slot * CL, CL), CL)


def prepare_kernel(live_ref, q_ref, do_ref, qg_ref, raw_ref, recip_ref, queries_ref, grads_ref, col_ref):
    size = col_ref.shape[0]
    heads = raw_ref.shape[1] // size
    group = q_ref.shape[1] // raw_ref.shape[1]
    column = jnp.broadcast_to(qg_ref[...], (size, size)).T
    for at in range(0, col_ref.shape[1], size):
        col_ref[:, at:at + size] = column

    def live(slot, carry):
        for head in range(heads):
            places = head_columns(head, group, size)
            rows = slice(head * size, (head + 1) * size)
            half = jnp.concatenate([q_ref[slot_rows(slot), place] for place in places], axis=0).T
            raw_ref[slot, rows, :] = half
            raw = half.astype(F32)
            recip = lax.rsqrt(jnp.mean(raw * raw, axis=0, keepdims=True) + EPS)
            recip_ref[slot, head:head + 1, :] = recip
            queries_ref[slot, rows, :] = (raw * recip * col_ref[...]).astype(BF16)
            grads_ref[slot, rows, :] = jnp.concatenate([do_ref[slot_rows(slot), place] for place in places], axis=0).T
        return carry

    lax.fori_loop(0, live_ref[0], live, 0)


def prepare(live_counts, queries, out_grad, query_gain, slots, width):
    size = query_gain.shape[1]
    lanes = queries.shape[1] // width * CL
    turned = jax.ShapeDtypeStruct((slots, width, lanes), BF16)
    return pl.pallas_call(
        prepare_kernel,
        in_specs=[SMEM_SPEC] + [VMEM_SPEC] * 3,
        out_specs=[VMEM_SPEC] * 5,
        out_shape=[
            turned, jax.ShapeDtypeStruct((slots, 8, lanes), F32), turned, turned,
            jax.ShapeDtypeStruct((size, lanes), F32),
        ],
        compiler_params=params(),
        cost_estimate=cost(2 * 10**9, 6 * queries.size),
        name="prepare",
    )(live_counts, queries, out_grad, query_gain)


def attention_kernel(*refs, parts, heads):
    live_ref, prompt_ref, me_ref, queries_ref, grads_ref, ck_ref, cv_ref, kg_ref, mask_ref = refs[:9]
    pieces, refs = refs[9:9 + parts], refs[9 + parts:]
    att_ref, ds_ref, pool_keys, own_keys, dk_ref, dv_ref, term_ref, keep_ref = refs[:8]
    send_ref, refs = (refs[8], refs[9:]) if parts > 1 else (None, refs[8:])
    acc, own_acc, pool_values, pool_values_t, own_values_t = refs[:5]
    size = kg_ref.shape[1]
    width = heads * size
    slots, _, lanes = queries_ref.shape
    per_head = lanes // CHUNK
    count = heads * per_head
    scores, weights, summed, grads, prob_grads, deltas = (refs[5 + at * count:5 + (at + 1) * count] for at in range(6))
    score_scale = 1.0 / math.sqrt(size)
    shard = pieces[0].shape[0]
    pool_rows = parts * shard

    def columns(head):
        return slice(head * size, (head + 1) * size)

    def piece_rows(piece_no):
        return pl.ds(pl.multiple_of((me_ref[0] ^ piece_no) * shard, shard), shard)

    acc[...] = jnp.zeros_like(acc)
    own_acc[...] = jnp.zeros_like(own_acc)
    for piece_no, piece in enumerate(pieces):
        pool_keys[piece_rows(piece_no), :] = piece[:, :width]
        pool_values[piece_rows(piece_no), :] = piece[:, width:]
    for head in range(heads):
        pool_values_t[columns(head), :] = pool_values[:, columns(head)].T
        own_unit, _ = unit(ck_ref[:, columns(head)].astype(F32))
        own_keys[:, columns(head)] = (own_unit * kg_ref[...]).astype(BF16)
        for slot in range(slots):
            own_values_t[slot, head] = cv_ref[slot * CL:(slot + 1) * CL, columns(head)].T
    alive = live_ref[0]

    def step(turn, carry):
        now, before = jnp.minimum(turn, alive - 1), jnp.maximum(turn - 1, 0)
        slot_of = {True: now, False: before}
        rows_of = {True: prompt_ref[now] * PL, False: prompt_ref[before] * PL}
        target_of = {
            True: jnp.where(turn < alive, rows_of[True], pool_rows),
            False: jnp.where(turn > 0, rows_of[False], pool_rows),
        }
        own_of = {True: jnp.where(turn < alive, turn, slots), False: jnp.where(turn > 0, turn - 1, slots)}

        def prompt_rows(at):
            return pl.ds(pl.multiple_of(at, PL), PL)

        def part(no):
            head = no // per_head
            return head, columns(head), slice(no % per_head * CHUNK, (no % per_head + 1) * CHUNK)

        def begin(no, fresh):
            _, place, span = part(no)
            keys = jnp.concatenate(
                [pool_keys[prompt_rows(rows_of[fresh]), place], own_keys[slot_rows(slot_of[fresh]), place]], axis=0
            )
            scores[no][...] = dot(keys, queries_ref[slot_of[fresh], place, span])

        def weigh(no, fresh):
            head, place, _ = part(no)
            prompt, own = scores[no][:PL, :], scores[no][PL:, :] + mask_ref[...]
            factor = score_scale * math.log2(math.e)
            high = jnp.maximum(jnp.max(prompt, axis=0, keepdims=True), jnp.max(own, axis=0, keepdims=True))
            both = jnp.concatenate([prompt, own], axis=0)
            half = jnp.exp2((both - high) * factor).astype(BF16)
            weights[no][...] = half
            values_t = jnp.concatenate(
                [pool_values_t[place, prompt_rows(rows_of[fresh])], own_values_t[slot_of[fresh], head]], axis=1
            )
            values_t = jnp.concatenate([values_t, jnp.ones((TAIL, PL + CL), BF16)], axis=0)
            summed[no][...] = dot(values_t, half)

        def attend(no, fresh):
            _, place, span = part(no)
            inverse = 1.0 / summed[no][size:size + 1, :]
            attended = (summed[no][:size, :] * inverse).astype(BF16)
            att_ref[slot_of[fresh], place, span] = attended
            scaled = (grads_ref[slot_of[fresh], place, span].astype(F32) * inverse).astype(BF16)
            grads[no][...] = scaled
            delta = jnp.sum(scaled.astype(F32) * attended.astype(F32), axis=0, keepdims=True)
            deltas[no][...] = jnp.broadcast_to(delta, deltas[no].shape)
            values = jnp.concatenate(
                [pool_values[prompt_rows(rows_of[fresh]), place], cv_ref[slot_rows(slot_of[fresh]), place]], axis=0
            )
            prob_grads[no][...] = dot(values, scaled)

        def back(no, fresh):
            head, place, span = part(no)
            half = weights[no][...]
            score_grad = (half.astype(F32) * (prob_grads[no][...] - deltas[no][0:1, :])).astype(BF16)
            ds_ref[slot_of[fresh], head, :, span] = score_grad
            value_grad = dot_nt(half, grads[no][...])
            key_grad = dot_nt(score_grad, queries_ref[slot_of[fresh], place, span])
            target = prompt_rows(target_of[fresh])
            acc[target, place] += key_grad[:PL]
            acc[target, width + head * size:width + (head + 1) * size] += value_grad[:PL]
            own_acc[own_of[fresh], head, 0] += key_grad[PL:]
            own_acc[own_of[fresh], head, 1] += value_grad[PL:]

        stages = (begin, weigh, attend, back)
        for tick in range(count):
            for number, stage in enumerate(stages):
                stage((tick - number) % count, tick >= number)
        return carry

    lax.fori_loop(0, alive + 1, step, 0)

    total = jnp.zeros((1, size), F32)
    for head in range(heads):
        own_grad = own_acc[:slots, head, 0].reshape(slots * CL, size) * score_scale
        own_unit, own_recip = unit(ck_ref[:, columns(head)].astype(F32))
        dk_ref[:, columns(head)] = norm_back(own_grad, own_unit, own_recip, kg_ref[...]).astype(BF16)
        dv_ref[:, columns(head)] = own_acc[:slots, head, 1].reshape(slots * CL, size).astype(BF16)
        total = total + jnp.sum(own_grad * own_keys[:, columns(head)].astype(F32), axis=0, keepdims=True)
        pool_term = acc[:pool_rows, columns(head)] * pool_keys[:, columns(head)].astype(F32)
        total = total + jnp.sum(pool_term, axis=0, keepdims=True) * score_scale
    term_ref[...] = jnp.broadcast_to(total, term_ref.shape)
    if parts == 1:
        keep_ref[:, :width] = acc[:pool_rows, :width] * score_scale
        keep_ref[:, width:] = acc[:pool_rows, width:]
    else:
        for piece_no in range(parts):
            place = slice(piece_no // 2 * shard, (piece_no // 2 + 1) * shard)
            ref = keep_ref if piece_no % 2 == 0 else send_ref
            ref[place, :width] = (acc[piece_rows(piece_no), :width] * score_scale).astype(ref.dtype)
            ref[place, width:] = acc[piece_rows(piece_no), width:].astype(ref.dtype)


def attention(live_counts, slot_prompts, me, queries, grads, keys, values, key_gain, mask, pieces):
    size = key_gain.shape[1]
    slots, width, lanes = queries.shape
    heads = width // size
    parts = len(pieces)
    pool_rows = parts * pieces[0].shape[0]
    count = heads * lanes // CHUNK
    span = PL + CL
    own = jax.ShapeDtypeStruct(keys.shape, BF16)
    out_shape = [
        jax.ShapeDtypeStruct(queries.shape, BF16),
        jax.ShapeDtypeStruct((slots, heads, span, lanes), BF16),
        jax.ShapeDtypeStruct((pool_rows, width), BF16),
        own, own, own,
        jax.ShapeDtypeStruct((8, size), F32),
    ]
    if parts > 1:
        half = (pool_rows // 2, 2 * width)
        out_shape += [jax.ShapeDtypeStruct(half, F32), jax.ShapeDtypeStruct(half, BF16)]
    else:
        out_shape += [jax.ShapeDtypeStruct((pool_rows, 2 * width), F32)]
    kinds = [
        ((span, CHUNK), F32), ((span, CHUNK), BF16), ((size + TAIL, CHUNK), F32),
        ((size, CHUNK), BF16), ((span, CHUNK), F32), ((8, CHUNK), F32),
    ]
    return pl.pallas_call(
        functools.partial(attention_kernel, parts=parts, heads=heads),
        in_specs=[SMEM_SPEC] * 3 + [VMEM_SPEC] * (6 + parts),
        out_specs=[VMEM_SPEC] * len(out_shape),
        out_shape=out_shape,
        scratch_shapes=[
            pltpu.VMEM((pool_rows + PL, 2 * width), F32),
            pltpu.VMEM((slots + 1, heads, 2, CL, size), F32),
            pltpu.VMEM((pool_rows, width), BF16),
            pltpu.VMEM((width, pool_rows), BF16),
            pltpu.VMEM((slots, heads, size, CL), BF16),
        ] + [pltpu.VMEM(shape, kind) for shape, kind in kinds for _ in range(count)],
        compiler_params=params(),
        cost_estimate=cost(3 * 10**9, 10**7),
        name="attention",
    )(live_counts, slot_prompts, me, queries, grads, keys, values, key_gain, mask, *pieces)


def post_kernel(
    live_ref, prompt_ref, att_t_ref, ds_ref, pool_keys, own_keys_ref, raw_ref, recip_ref, col_ref,
    att_ref, dq_ref, att_out, dq_out, sems,
):
    slots, width, lanes = raw_ref.shape
    size = col_ref.shape[0]
    heads = width // size
    group = att_ref.shape[1] // width
    score_scale = 1.0 / math.sqrt(size)

    def copy_out(slot, which):
        source, target = ((att_out, att_ref), (dq_out, dq_ref))[which]
        return pltpu.make_async_copy(source.at[slot], target.at[slot_rows(slot), :], sems.at[which, slot])

    def dead(slot, carry):
        att_out[slot] = jnp.zeros(att_out.shape[1:], BF16)
        dq_out[slot] = jnp.zeros(dq_out.shape[1:], BF16)
        for which in range(2):
            copy_out(slot, which).start()
        return carry

    def live(slot, carry):
        rows = pl.ds(pl.multiple_of(prompt_ref[slot] * PL, PL), PL)
        for head in range(heads):
            columns = slice(head * size, (head + 1) * size)
            keys_t = jnp.concatenate([pool_keys[rows, columns], own_keys_ref[slot_rows(slot), columns]], axis=0).T
            query_grad = dot(keys_t, ds_ref[slot, head]) * score_scale
            recip = recip_ref[slot, head:head + 1, :]
            query_unit = raw_ref[slot, columns, :].astype(F32) * recip
            scaled = query_grad * col_ref[...]
            mean = jnp.mean(query_unit * scaled, axis=0, keepdims=True)
            query_out = (recip * (scaled - query_unit * mean)).astype(BF16).T
            attended = att_t_ref[slot, columns, :].T
            for g, place in enumerate(head_columns(head, group, size)):
                att_out[slot, :, place] = attended[g * CL:(g + 1) * CL]
                dq_out[slot, :, place] = query_out[g * CL:(g + 1) * CL]
        for which in range(2):
            copy_out(slot, which).start()
        return carry

    lax.fori_loop(live_ref[0], slots, dead, 0)
    lax.fori_loop(0, live_ref[0], live, 0)
    for slot in range(slots):
        for which in range(2):
            copy_out(slot, which).wait()


def post(live_counts, slot_prompts, att_t, score_grads, pool_keys, own_keys, raw, recip, query_col, shape):
    slots = raw.shape[0]
    out = jax.ShapeDtypeStruct(shape, BF16)
    slab = pltpu.VMEM((slots, CL, shape[1]), BF16)
    return pl.pallas_call(
        post_kernel,
        in_specs=[SMEM_SPEC] * 2 + [VMEM_SPEC] * 7,
        out_specs=[HBM_SPEC] * 2,
        out_shape=[out, out],
        scratch_shapes=[slab, slab, pltpu.SemaphoreType.DMA((2, slots))],
        compiler_params=params(),
        cost_estimate=cost(3 * 10**9, 4 * 10**6),
        name="post",
    )(live_counts, slot_prompts, att_t, score_grads, pool_keys, own_keys, raw, recip, query_col)


def tree(terms):
    while len(terms) > 1:
        terms = [left + right for left, right in zip(terms[::2], terms[1::2])]
    return terms[0]


def add_kernel(keep_ref, came_ref, *refs, terms, size):
    tail = gain_rows(tree([ref[0:1, :] for ref in refs[:terms]]), keep_ref.shape[1])
    own_ref, send_refs = refs[terms], refs[terms + 1:]
    blocks = len(send_refs) + 1
    shard = keep_ref.shape[0] // blocks
    for at in range(blocks):
        place = slice(at * shard, (at + 1) * shard)
        total = keep_ref[place, :] + came_ref[place, :].astype(F32)
        ref = send_refs[at - 1] if at > 0 else own_ref
        ref[:shard, :] = total.astype(ref.dtype)
        ref[shard:, :] = tail.astype(ref.dtype)


def add(keep, came, terms, blocks):
    shape = (keep.shape[0] // blocks + TAIL, keep.shape[1])
    return pl.pallas_call(
        functools.partial(add_kernel, terms=len(terms), size=terms[0].shape[1]),
        in_specs=[VMEM_SPEC] * (2 + len(terms)),
        out_specs=[VMEM_SPEC] * blocks,
        out_shape=[jax.ShapeDtypeStruct(shape, F32)] + [jax.ShapeDtypeStruct(shape, BF16)] * (blocks - 1),
        compiler_params=params(),
        name="add",
    )(keep, came, *terms)


def chips_kernel(*refs, size):
    total = tree([gain_term(ref[ref.shape[0] - TAIL:, :], size) for ref in refs[:-1]])
    refs[-1][...] = jnp.broadcast_to(total, refs[-1].shape)


def sum_chips(blocks, size):
    return pl.pallas_call(
        functools.partial(chips_kernel, size=size),
        in_specs=[VMEM_SPEC] * len(blocks),
        out_specs=VMEM_SPEC,
        out_shape=jax.ShapeDtypeStruct((8, size), F32),
        compiler_params=params(),
        name="sum_chips",
    )(*blocks)


def last_kernel(*refs):
    terms, (qg_ref, kg_ref, query_ref, key_ref) = refs[:-4], refs[-4:]
    total = tree([ref[0:1, :] for ref in terms])
    query_ref[...] = total / qg_ref[...]
    key_ref[...] = total / kg_ref[...]


def gain_grads(terms, query_gain, key_gain):
    row = jax.ShapeDtypeStruct(query_gain.shape, F32)
    return pl.pallas_call(
        last_kernel,
        in_specs=[VMEM_SPEC] * (len(terms) + 2),
        out_specs=[VMEM_SPEC] * 2,
        out_shape=[row, row],
        compiler_params=params(),
        name="gain_grads",
    )(*terms, query_gain, key_gain)


def finish_kernel(*refs):
    parts, (raw_ref, kg_ref, key_ref, value_ref) = refs[:-4], refs[-4:]
    size = kg_ref.shape[1]
    shard, width = raw_ref.shape
    total = parts[0][:shard, :]
    for ref in parts[1:]:
        total = total + ref[:shard, :].astype(F32)
    for head in range(width // size):
        columns = slice(head * size, (head + 1) * size)
        unit_rows, recip = unit(raw_ref[:, columns].astype(F32))
        key_ref[:, columns] = norm_back(total[:, columns], unit_rows, recip, kg_ref[...])
    value_ref[...] = total[:, width:]


def finish(blocks, raw, key_gain):
    shape = jax.ShapeDtypeStruct(raw.shape, F32)
    return pl.pallas_call(
        finish_kernel,
        in_specs=[VMEM_SPEC] * (len(blocks) + 2),
        out_specs=[VMEM_SPEC] * 2,
        out_shape=[shape, shape],
        compiler_params=params(),
        cost_estimate=cost(10**8, 10**6),
        name="finish",
    )(*blocks, raw, key_gain)


def swap(values, axis, step):
    return lax.ppermute(values, axis, [(i, i ^ step) for i in range(lax.axis_size(axis))])


def local(
    comp_queries, comp_keys, comp_values, prompt_keys, prompt_values,
    query_gain, key_gain, out_grad, live_counts, slot_prompts,
):
    grp, tp = lax.axis_size("grp"), lax.axis_size("tp")
    shard = prompt_keys.shape[0]
    size = query_gain.shape[0]
    by_permute = shard % 16 == 0 and grp > 1 and grp & (grp - 1) == 0 and tp & (tp - 1) == 0
    slots, width = slot_prompts.shape[0], comp_keys.shape[1]
    query_gain, key_gain = query_gain.reshape(1, size), key_gain.reshape(1, size)
    mask = causal()
    mask, keys_in, values_in = lax.optimization_barrier((mask, prompt_keys, prompt_values))
    mine = pack(keys_in, values_in, key_gain)
    raw, recip, queries, grads, query_col = prepare(live_counts, comp_queries, out_grad, query_gain, slots, width)
    if by_permute:
        me = lax.axis_index("grp").astype(jnp.int32).reshape(1)
        even = [mine] + [swap(mine, "grp", step) for step in range(2, grp, 2)]
        odd = [swap(mine, "grp", 1)]
        even, queries, grads, raw, recip, query_col = lax.optimization_barrier(
            (even, queries, grads, raw, recip, query_col)
        )
        odd += [swap(piece, "grp", 1) for piece in even[1:]]
        pieces = [piece for pair in zip(even, odd) for piece in pair]
    else:
        me = jnp.zeros((1,), jnp.int32)
        pieces = [lax.all_gather(mine, "grp", axis=0, tiled=True)]
    att_t, score_grads, pool_keys, own_keys, key_grads, value_grads, term, keep, *send = attention(
        live_counts, slot_prompts, me, queries, grads, comp_keys, comp_values, key_gain, mask, pieces,
    )
    attended, query_grads = post(
        live_counts, slot_prompts, att_t, score_grads, pool_keys, own_keys, raw, recip, query_col, comp_queries.shape,
    )
    if by_permute:
        came = swap(send[0], "grp", 1)
        terms = [term] + [swap(term, "tp", step) for step in range(1, tp)]
        own, *blocks = add(keep, came, terms, grp // 2)
        blocks = [own] + [swap(block, "grp", 2 * at + 2) for at, block in enumerate(blocks)]
        blocks, attended = lax.optimization_barrier((blocks, attended))
        total = sum_chips(blocks, size)
        terms = [total, swap(total, "grp", 1)]
    else:
        blocks = [lax.psum_scatter(keep, "grp", scatter_dimension=0, tiled=True)]
        terms = [lax.psum(term, ("grp", "tp"))]
    prompt_key_grads, prompt_value_grads = finish(blocks, prompt_keys, key_gain)
    query_gain_grad, key_gain_grad = gain_grads(terms, query_gain, key_gain)
    return (
        attended, query_grads, key_grads, value_grads, prompt_key_grads, prompt_value_grads,
        query_gain_grad.reshape(size), key_gain_grad.reshape(size),
    )


def solution(mesh):
    split, whole = P("grp", "tp"), P()
    return jax.shard_map(
        local,
        mesh=mesh,
        in_specs=(split, split, split, split, split, whole, whole, split, P("grp"), P("grp")),
        out_specs=(split, split, split, split, split, split, whole, whole),
        check_vma=False,
    )
```

```python
import functools
import math

import jax
import jax.numpy as jnp
from jax import lax
from jax.experimental import pallas as pl
from jax.experimental.pallas import tpu as pltpu
from jax.sharding import PartitionSpec as P

PL = 384
CL = 64
EPS = 1e-06
TAIL = 16
CHUNK = 256
VMEM_LIMIT = 24 * 1024 * 1024
F32 = jnp.float32
BF16 = jnp.bfloat16
SMEM_SPEC = pl.BlockSpec(memory_space=pltpu.SMEM)
VMEM_SPEC = pl.BlockSpec(memory_space=pltpu.VMEM)
HBM_SPEC = pl.BlockSpec(memory_space=pltpu.HBM)


def dot(left, right):
    return jnp.dot(left, right, preferred_element_type=F32)


def dot_nt(left, right):
    return lax.dot_general(left, right, (((1,), (1,)), ((), ())), preferred_element_type=F32)


def unit(raw):
    recip = lax.rsqrt(jnp.mean(raw * raw, axis=-1, keepdims=True) + EPS)
    return raw * recip, recip


def norm_back(upstream, unit_rows, recip, gain):
    scaled = upstream * gain
    return recip * (scaled - unit_rows * jnp.mean(unit_rows * scaled, axis=-1, keepdims=True))


def halves(row):
    upper = row.astype(BF16)
    return [upper, (row - upper.astype(F32)).astype(BF16)]


def gain_rows(term, wide):
    row = jnp.concatenate([part.astype(F32) for part in halves(term)], axis=1)
    if wide > row.shape[1]:
        row = jnp.concatenate([row, jnp.zeros((1, wide - row.shape[1]), F32)], axis=1)
    rows = jnp.broadcast_to(row, (TAIL, wide))
    return jnp.where(lax.broadcasted_iota(jnp.int32, rows.shape, 0) == 0, rows, 0.0).astype(BF16)


def gain_term(rows, size):
    row = rows.astype(F32)[0:1]
    return row[:, :size] + row[:, size:2 * size]


def params(limit=VMEM_LIMIT):
    return pltpu.CompilerParams(vmem_limit_bytes=limit)


def cost(flops, size):
    return pl.CostEstimate(flops=flops, bytes_accessed=size, transcendentals=0)


def causal_kernel(mask_ref):
    key_no = lax.broadcasted_iota(jnp.int32, mask_ref.shape, 0)
    token_no = lax.broadcasted_iota(jnp.int32, mask_ref.shape, 1) % CL
    mask_ref[...] = jnp.where(key_no <= token_no, 0.0, -jnp.inf)


def causal():
    return pl.pallas_call(
        causal_kernel,
        out_specs=VMEM_SPEC,
        out_shape=jax.ShapeDtypeStruct((CL, CHUNK), F32),
        compiler_params=params(),
        cost_estimate=cost(4 * 10**9, 10**6),
        name="causal",
    )()


def pack_kernel(keys_ref, values_ref, kg_ref, out_ref):
    size, width = kg_ref.shape[1], keys_ref.shape[1]
    for head in range(width // size):
        columns = slice(head * size, (head + 1) * size)
        unit_rows, _ = unit(keys_ref[:, columns].astype(F32))
        out_ref[:, columns] = (unit_rows * kg_ref[...]).astype(BF16)
    out_ref[:, width:] = values_ref[...]


def pack(keys, values, key_gain):
    return pl.pallas_call(
        pack_kernel,
        in_specs=[VMEM_SPEC] * 3,
        out_specs=VMEM_SPEC,
        out_shape=jax.ShapeDtypeStruct((keys.shape[0], 2 * keys.shape[1]), BF16),
        compiler_params=params(),
        cost_estimate=cost(4 * 10**9, 10**6),
        name="pack",
    )(keys, values, key_gain)


def head_columns(head, group, size):
    return [slice((head * group + g) * size, (head * group + g + 1) * size) for g in range(group)]


def slot_rows(slot):
    return pl.ds(pl.multiple_of(slot * CL, CL), CL)


def prepare_kernel(live_ref, q_ref, do_ref, qg_ref, raw_ref, recip_ref, queries_ref, grads_ref, col_ref):
    size = col_ref.shape[0]
    heads = raw_ref.shape[1] // size
    group = q_ref.shape[1] // raw_ref.shape[1]
    column = jnp.broadcast_to(qg_ref[...], (size, size)).T
    for at in range(0, col_ref.shape[1], size):
        col_ref[:, at:at + size] = column

    def live(slot, carry):
        for head in range(heads):
            places = head_columns(head, group, size)
            rows = slice(head * size, (head + 1) * size)
            half = jnp.concatenate([q_ref[slot_rows(slot), place] for place in places], axis=0).T
            raw_ref[slot, rows, :] = half
            raw = half.astype(F32)
            recip = lax.rsqrt(jnp.mean(raw * raw, axis=0, keepdims=True) + EPS)
            recip_ref[slot, head:head + 1, :] = recip
            queries_ref[slot, rows, :] = (raw * recip * col_ref[...]).astype(BF16)
            grads_ref[slot, rows, :] = jnp.concatenate([do_ref[slot_rows(slot), place] for place in places], axis=0).T
        return carry

    lax.fori_loop(0, live_ref[0], live, 0)


def prepare(live_counts, queries, out_grad, query_gain, slots, width):
    size = query_gain.shape[1]
    lanes = queries.shape[1] // width * CL
    turned = jax.ShapeDtypeStruct((slots, width, lanes), BF16)
    return pl.pallas_call(
        prepare_kernel,
        in_specs=[SMEM_SPEC] + [VMEM_SPEC] * 3,
        out_specs=[VMEM_SPEC] * 5,
        out_shape=[
            turned, jax.ShapeDtypeStruct((slots, 8, lanes), F32), turned, turned,
            jax.ShapeDtypeStruct((size, lanes), F32),
        ],
        compiler_params=params(),
        cost_estimate=cost(2 * 10**9, 6 * queries.size),
        name="prepare",
    )(live_counts, queries, out_grad, query_gain)


def attention_kernel(*refs, parts, heads):
    live_ref, prompt_ref, me_ref, queries_ref, grads_ref, ck_ref, cv_ref, kg_ref, mask_ref = refs[:9]
    pieces, refs = refs[9:9 + parts], refs[9 + parts:]
    att_ref, ds_ref, pool_keys, own_keys, own_acc, term_ref, keep_ref = refs[:7]
    send_ref, refs = (refs[7], refs[8:]) if parts > 1 else (None, refs[7:])
    acc, pool_values, pool_values_t, own_values_t = refs[:4]
    size = kg_ref.shape[1]
    width = heads * size
    slots, _, lanes = queries_ref.shape
    per_head = lanes // CHUNK
    count = heads * per_head
    weights, grads = refs[4:4 + heads], refs[4 + heads:4 + 2 * heads]
    scores, summed = refs[4 + 2 * heads:4 + 2 * heads + count], refs[4 + 2 * heads + count:]
    score_scale = 1.0 / math.sqrt(size)
    shard = pieces[0].shape[0]

    def columns(head):
        return slice(head * size, (head + 1) * size)

    def piece_rows(piece_no):
        return pl.ds(pl.multiple_of((me_ref[0] ^ piece_no) * shard, shard), shard)

    acc[...] = jnp.zeros_like(acc)
    own_acc[...] = jnp.zeros_like(own_acc)
    for piece_no, piece in enumerate(pieces):
        pool_keys[piece_rows(piece_no), :] = piece[:, :width]
        pool_values[piece_rows(piece_no), :] = piece[:, width:]
    for head in range(heads):
        pool_values_t[columns(head), :] = pool_values[:, columns(head)].T
        own_unit, _ = unit(ck_ref[:, columns(head)].astype(F32))
        own_keys[:, columns(head)] = (own_unit * kg_ref[...]).astype(BF16)
        for slot in range(slots):
            own_values_t[slot, head] = cv_ref[slot * CL:(slot + 1) * CL, columns(head)].T

    def prompt_rows(slot):
        return pl.ds(pl.multiple_of(prompt_ref[slot] * PL, PL), PL)

    def part(no):
        head = no // per_head
        return head, columns(head), slice(no % per_head * CHUNK, (no % per_head + 1) * CHUNK)

    def begin(slot, no):
        _, place, span = part(no)
        keys = jnp.concatenate([pool_keys[prompt_rows(slot), place], own_keys[slot_rows(slot), place]], axis=0)
        scores[no][...] = dot(keys, queries_ref[slot, place, span])

    def weigh(slot, no):
        head, place, span = part(no)
        prompt, own = scores[no][:PL, :], scores[no][PL:, :] + mask_ref[...]
        factor = score_scale * math.log2(math.e)
        high = jnp.maximum(jnp.max(prompt, axis=0, keepdims=True), jnp.max(own, axis=0, keepdims=True))
        both = jnp.concatenate([prompt, own], axis=0)
        half = jnp.exp2((both - high) * factor).astype(BF16)
        weights[head][:, span] = half
        values_t = jnp.concatenate([pool_values_t[place, prompt_rows(slot)], own_values_t[slot, head]], axis=1)
        values_t = jnp.concatenate([values_t, jnp.ones((TAIL, PL + CL), BF16)], axis=0)
        summed[no][...] = dot(values_t, half)

    def back(slot, no):
        head, place, span = part(no)
        inverse = 1.0 / summed[no][size:size + 1, :]
        attended = (summed[no][:size, :] * inverse).astype(BF16)
        att_ref[slot, place, span] = attended
        scaled = (grads_ref[slot, place, span].astype(F32) * inverse).astype(BF16)
        grads[head][:, span] = scaled
        delta = jnp.sum(scaled.astype(F32) * attended.astype(F32), axis=0, keepdims=True)
        values = jnp.concatenate([pool_values[prompt_rows(slot), place], cv_ref[slot_rows(slot), place]], axis=0)
        score_grad = weights[head][:, span].astype(F32) * (dot(values, scaled) - delta)
        ds_ref[slot, head, :, span] = score_grad.astype(BF16)

    def close(slot, head):
        value_grad = dot_nt(weights[head][...], grads[head][...])
        key_grad = dot_nt(ds_ref[slot, head], queries_ref[slot, columns(head), :])
        acc[prompt_rows(slot), columns(head)] += key_grad[:PL]
        acc[prompt_rows(slot), width + head * size:width + (head + 1) * size] += value_grad[:PL]
        own_acc[slot, head, 0] = key_grad[PL:]
        own_acc[slot, head, 1] = value_grad[PL:]

    def ticks(now, before):
        for tick in range(count):
            if now is not None:
                begin(now, tick)
            for number, stage in ((1, weigh), (2, back)):
                slot = now if tick >= number else before
                if slot is not None:
                    stage(slot, (tick - number) % count)
            done = (tick - 3) % count
            slot = now if tick >= 3 else before
            if slot is not None and done % per_head == per_head - 1:
                close(slot, done // per_head)

    def step(slot, carry):
        ticks(slot, slot - 1)
        return carry

    ticks(0, None)
    lax.fori_loop(1, live_ref[0], step, 0)
    ticks(None, live_ref[0] - 1)

    total = jnp.zeros((1, size), F32)
    for head in range(heads):
        own_grad = own_acc[:, head, 0].reshape(slots * CL, size)
        total = total + jnp.sum(own_grad * own_keys[:, columns(head)].astype(F32), axis=0, keepdims=True)
        pool_term = acc[:, columns(head)] * pool_keys[:, columns(head)].astype(F32)
        total = total + jnp.sum(pool_term, axis=0, keepdims=True)
    term_ref[...] = jnp.broadcast_to(total * score_scale, term_ref.shape)
    if parts == 1:
        keep_ref[:, :width] = acc[:, :width] * score_scale
        keep_ref[:, width:] = acc[:, width:]
    else:
        for piece_no in range(parts):
            place = slice(piece_no // 2 * shard, (piece_no // 2 + 1) * shard)
            ref = keep_ref if piece_no % 2 == 0 else send_ref
            ref[place, :width] = (acc[piece_rows(piece_no), :width] * score_scale).astype(ref.dtype)
            ref[place, width:] = acc[piece_rows(piece_no), width:].astype(ref.dtype)


def attention(live_counts, slot_prompts, me, queries, grads, keys, values, key_gain, mask, pieces):
    size = key_gain.shape[1]
    slots, width, lanes = queries.shape
    heads = width // size
    parts = len(pieces)
    pool_rows = parts * pieces[0].shape[0]
    count = heads * lanes // CHUNK
    span = PL + CL
    out_shape = [
        jax.ShapeDtypeStruct(queries.shape, BF16),
        jax.ShapeDtypeStruct((slots, heads, span, lanes), BF16),
        jax.ShapeDtypeStruct((pool_rows, width), BF16),
        jax.ShapeDtypeStruct(keys.shape, BF16),
        jax.ShapeDtypeStruct((slots, heads, 2, CL, size), F32),
        jax.ShapeDtypeStruct((8, size), F32),
    ]
    if parts > 1:
        half = (pool_rows // 2, 2 * width)
        out_shape += [jax.ShapeDtypeStruct(half, F32), jax.ShapeDtypeStruct(half, BF16)]
    else:
        out_shape += [jax.ShapeDtypeStruct((pool_rows, 2 * width), F32)]
    return pl.pallas_call(
        functools.partial(attention_kernel, parts=parts, heads=heads),
        in_specs=[SMEM_SPEC] * 3 + [VMEM_SPEC] * (6 + parts),
        out_specs=[VMEM_SPEC] * len(out_shape),
        out_shape=out_shape,
        scratch_shapes=[
            pltpu.VMEM((pool_rows, 2 * width), F32),
            pltpu.VMEM((pool_rows, width), BF16),
            pltpu.VMEM((width, pool_rows), BF16),
            pltpu.VMEM((slots, heads, size, CL), BF16),
        ]
        + [pltpu.VMEM((span, lanes), BF16)] * heads
        + [pltpu.VMEM((size, lanes), BF16)] * heads
        + [pltpu.VMEM((span, CHUNK), F32)] * count
        + [pltpu.VMEM((size + TAIL, CHUNK), F32)] * count,
        compiler_params=params(),
        cost_estimate=cost(3 * 10**9, 10**7),
        name="attention",
    )(live_counts, slot_prompts, me, queries, grads, keys, values, key_gain, mask, *pieces)


def post_kernel(
    live_ref, prompt_ref, att_t_ref, ds_ref, pool_keys, own_keys_ref, own_acc, raw_ref, recip_ref, col_ref,
    ck_ref, kg_ref, att_ref, dq_ref, dk_ref, dv_ref, att_out, dq_out, sems,
):
    slots, width, lanes = raw_ref.shape
    size = col_ref.shape[0]
    heads = width // size
    group = att_ref.shape[1] // width
    score_scale = 1.0 / math.sqrt(size)

    def copy_out(slot, which):
        source, target = ((att_out, att_ref), (dq_out, dq_ref))[which]
        return pltpu.make_async_copy(source.at[slot], target.at[slot_rows(slot), :], sems.at[which, slot])

    def dead(slot, carry):
        att_out[slot] = jnp.zeros(att_out.shape[1:], BF16)
        dq_out[slot] = jnp.zeros(dq_out.shape[1:], BF16)
        for which in range(2):
            copy_out(slot, which).start()
        return carry

    def live(slot, carry):
        rows = pl.ds(pl.multiple_of(prompt_ref[slot] * PL, PL), PL)
        for head in range(heads):
            columns = slice(head * size, (head + 1) * size)
            keys_t = jnp.concatenate([pool_keys[rows, columns], own_keys_ref[slot_rows(slot), columns]], axis=0).T
            query_grad = dot(keys_t, ds_ref[slot, head]) * score_scale
            recip = recip_ref[slot, head:head + 1, :]
            query_unit = raw_ref[slot, columns, :].astype(F32) * recip
            scaled = query_grad * col_ref[...]
            mean = jnp.mean(query_unit * scaled, axis=0, keepdims=True)
            query_out = (recip * (scaled - query_unit * mean)).astype(BF16).T
            attended = att_t_ref[slot, columns, :].T
            for g, place in enumerate(head_columns(head, group, size)):
                att_out[slot, :, place] = attended[g * CL:(g + 1) * CL]
                dq_out[slot, :, place] = query_out[g * CL:(g + 1) * CL]
        for which in range(2):
            copy_out(slot, which).start()
        return carry

    lax.fori_loop(live_ref[0], slots, dead, 0)
    lax.fori_loop(0, live_ref[0], live, 0)
    for head in range(heads):
        columns = slice(head * size, (head + 1) * size)
        own_grad = own_acc[:, head, 0].reshape(slots * CL, size) * score_scale
        own_unit, own_recip = unit(ck_ref[:, columns].astype(F32))
        dk_ref[:, columns] = norm_back(own_grad, own_unit, own_recip, kg_ref[...]).astype(BF16)
        dv_ref[:, columns] = own_acc[:, head, 1].reshape(slots * CL, size).astype(BF16)
    for slot in range(slots):
        for which in range(2):
            copy_out(slot, which).wait()


def post(
    live_counts, slot_prompts, att_t, score_grads, pool_keys, own_keys, own_acc, raw, recip, query_col,
    keys, key_gain, shape,
):
    slots = raw.shape[0]
    out = jax.ShapeDtypeStruct(shape, BF16)
    own = jax.ShapeDtypeStruct(keys.shape, BF16)
    slab = pltpu.VMEM((slots, CL, shape[1]), BF16)
    return pl.pallas_call(
        post_kernel,
        in_specs=[SMEM_SPEC] * 2 + [VMEM_SPEC] * 10,
        out_specs=[HBM_SPEC] * 2 + [VMEM_SPEC] * 2,
        out_shape=[out, out, own, own],
        scratch_shapes=[slab, slab, pltpu.SemaphoreType.DMA((2, slots))],
        compiler_params=params(),
        cost_estimate=cost(3 * 10**9, 4 * 10**6),
        name="post",
    )(
        live_counts, slot_prompts, att_t, score_grads, pool_keys, own_keys, own_acc, raw, recip, query_col,
        keys, key_gain,
    )


def tree(terms):
    while len(terms) > 1:
        terms = [left + right for left, right in zip(terms[::2], terms[1::2])]
    return terms[0]


def add_kernel(keep_ref, came_ref, *refs, terms, size):
    tail = gain_rows(tree([ref[0:1, :] for ref in refs[:terms]]), keep_ref.shape[1])
    own_ref, send_refs = refs[terms], refs[terms + 1:]
    blocks = len(send_refs) + 1
    shard = keep_ref.shape[0] // blocks
    for at in range(blocks):
        place = slice(at * shard, (at + 1) * shard)
        total = keep_ref[place, :] + came_ref[place, :].astype(F32)
        ref = send_refs[at - 1] if at > 0 else own_ref
        ref[:shard, :] = total.astype(ref.dtype)
        ref[shard:, :] = tail.astype(ref.dtype)


def add(keep, came, terms, blocks):
    shape = (keep.shape[0] // blocks + TAIL, keep.shape[1])
    return pl.pallas_call(
        functools.partial(add_kernel, terms=len(terms), size=terms[0].shape[1]),
        in_specs=[VMEM_SPEC] * (2 + len(terms)),
        out_specs=[VMEM_SPEC] * blocks,
        out_shape=[jax.ShapeDtypeStruct(shape, F32)] + [jax.ShapeDtypeStruct(shape, BF16)] * (blocks - 1),
        compiler_params=params(),
        name="add",
    )(keep, came, *terms)


def chips_kernel(*refs, size):
    total = tree([gain_term(ref[ref.shape[0] - TAIL:, :], size) for ref in refs[:-1]])
    refs[-1][...] = jnp.broadcast_to(total, refs[-1].shape)


def sum_chips(blocks, size):
    return pl.pallas_call(
        functools.partial(chips_kernel, size=size),
        in_specs=[VMEM_SPEC] * len(blocks),
        out_specs=VMEM_SPEC,
        out_shape=jax.ShapeDtypeStruct((8, size), F32),
        compiler_params=params(),
        name="sum_chips",
    )(*blocks)


def last_kernel(*refs):
    terms, (qg_ref, kg_ref, query_ref, key_ref) = refs[:-4], refs[-4:]
    total = tree([ref[0:1, :] for ref in terms])
    query_ref[...] = total / qg_ref[...]
    key_ref[...] = total / kg_ref[...]


def gain_grads(terms, query_gain, key_gain):
    row = jax.ShapeDtypeStruct(query_gain.shape, F32)
    return pl.pallas_call(
        last_kernel,
        in_specs=[VMEM_SPEC] * (len(terms) + 2),
        out_specs=[VMEM_SPEC] * 2,
        out_shape=[row, row],
        compiler_params=params(),
        name="gain_grads",
    )(*terms, query_gain, key_gain)


def finish_kernel(*refs):
    parts, (raw_ref, kg_ref, key_ref, value_ref) = refs[:-4], refs[-4:]
    size = kg_ref.shape[1]
    shard, width = raw_ref.shape
    total = parts[0][:shard, :]
    for ref in parts[1:]:
        total = total + ref[:shard, :].astype(F32)
    for head in range(width // size):
        columns = slice(head * size, (head + 1) * size)
        unit_rows, recip = unit(raw_ref[:, columns].astype(F32))
        key_ref[:, columns] = norm_back(total[:, columns], unit_rows, recip, kg_ref[...])
    value_ref[...] = total[:, width:]


def finish(blocks, raw, key_gain):
    shape = jax.ShapeDtypeStruct(raw.shape, F32)
    return pl.pallas_call(
        finish_kernel,
        in_specs=[VMEM_SPEC] * (len(blocks) + 2),
        out_specs=[VMEM_SPEC] * 2,
        out_shape=[shape, shape],
        compiler_params=params(),
        cost_estimate=cost(10**8, 10**6),
        name="finish",
    )(*blocks, raw, key_gain)


def swap(values, axis, step):
    return lax.ppermute(values, axis, [(i, i ^ step) for i in range(lax.axis_size(axis))])


def local(
    comp_queries, comp_keys, comp_values, prompt_keys, prompt_values,
    query_gain, key_gain, out_grad, live_counts, slot_prompts,
):
    grp, tp = lax.axis_size("grp"), lax.axis_size("tp")
    shard = prompt_keys.shape[0]
    size = query_gain.shape[0]
    by_permute = shard % 16 == 0 and grp > 1 and grp & (grp - 1) == 0 and tp & (tp - 1) == 0
    slots, width = slot_prompts.shape[0], comp_keys.shape[1]
    query_gain, key_gain = query_gain.reshape(1, size), key_gain.reshape(1, size)
    me = lax.axis_index("grp").astype(jnp.int32).reshape(1) if by_permute else jnp.zeros((1,), jnp.int32)
    mask, me, keys_in, values_in = lax.optimization_barrier((causal(), me, prompt_keys, prompt_values))
    mine = pack(keys_in, values_in, key_gain)
    raw, recip, queries, grads, query_col = prepare(live_counts, comp_queries, out_grad, query_gain, slots, width)
    if by_permute:
        even = [mine] + [swap(mine, "grp", step) for step in range(2, grp, 2)]
        odd = [swap(mine, "grp", 1)]
        even, queries, grads, raw, recip, query_col = lax.optimization_barrier(
            (even, queries, grads, raw, recip, query_col)
        )
        odd += [swap(piece, "grp", 1) for piece in even[1:]]
        pieces = [piece for pair in zip(even, odd) for piece in pair]
    else:
        pieces = [lax.all_gather(mine, "grp", axis=0, tiled=True)]
    att_t, score_grads, pool_keys, own_keys, own_acc, term, keep, *send = attention(
        live_counts, slot_prompts, me, queries, grads, comp_keys, comp_values, key_gain, mask, pieces,
    )
    attended, query_grads, key_grads, value_grads = post(
        live_counts, slot_prompts, att_t, score_grads, pool_keys, own_keys, own_acc, raw, recip, query_col,
        comp_keys, key_gain, comp_queries.shape,
    )
    if by_permute:
        came = swap(send[0], "grp", 1)
        terms = [term] + [swap(term, "tp", step) for step in range(1, tp)]
        own, *blocks = add(keep, came, terms, grp // 2)
        blocks = [own] + [swap(block, "grp", 2 * at + 2) for at, block in enumerate(blocks)]
        blocks, attended = lax.optimization_barrier((blocks, attended))
        total = sum_chips(blocks, size)
        terms = [total, swap(total, "grp", 1)]
    else:
        blocks = [lax.psum_scatter(keep, "grp", scatter_dimension=0, tiled=True)]
        terms = [lax.psum(term, ("grp", "tp"))]
    prompt_key_grads, prompt_value_grads = finish(blocks, prompt_keys, key_gain)
    query_gain_grad, key_gain_grad = gain_grads(terms, query_gain, key_gain)
    return (
        attended, query_grads, key_grads, value_grads, prompt_key_grads, prompt_value_grads,
        query_gain_grad.reshape(size), key_gain_grad.reshape(size),
    )


def solution(mesh):
    split, whole = P("grp", "tp"), P()
    return jax.shard_map(
        local,
        mesh=mesh,
        in_specs=(split, split, split, split, split, whole, whole, split, P("grp"), P("grp")),
        out_specs=(split, split, split, split, split, split, whole, whole),
        check_vma=False,
    )
```

```python
import functools
import math

import jax
import jax.numpy as jnp
from jax import lax
from jax.experimental import pallas as pl
from jax.experimental.pallas import tpu as pltpu
from jax.sharding import PartitionSpec as P

PL = 384
CL = 64
EPS = 1e-06
TAIL = 16
CHUNK = 256
VMEM_LIMIT = 24 * 1024 * 1024
F32 = jnp.float32
BF16 = jnp.bfloat16
SMEM_SPEC = pl.BlockSpec(memory_space=pltpu.SMEM)
VMEM_SPEC = pl.BlockSpec(memory_space=pltpu.VMEM)
HBM_SPEC = pl.BlockSpec(memory_space=pltpu.HBM)


def dot(left, right):
    return jnp.dot(left, right, preferred_element_type=F32)


def dot_nt(left, right):
    return lax.dot_general(left, right, (((1,), (1,)), ((), ())), preferred_element_type=F32)


def unit(raw):
    recip = lax.rsqrt(jnp.mean(raw * raw, axis=-1, keepdims=True) + EPS)
    return raw * recip, recip


def norm_back(upstream, unit_rows, recip, gain):
    scaled = upstream * gain
    return recip * (scaled - unit_rows * jnp.mean(unit_rows * scaled, axis=-1, keepdims=True))


def gain_rows(term):
    upper = term.astype(BF16).astype(F32)
    rows = jnp.concatenate([upper, term - upper, jnp.zeros((TAIL - 2, term.shape[1]), F32)], axis=0)
    return rows.astype(BF16)


def gain_term(rows):
    return rows[0:1].astype(F32) + rows[1:2].astype(F32)


def params(limit=VMEM_LIMIT):
    return pltpu.CompilerParams(vmem_limit_bytes=limit)


def cost(flops, size):
    return pl.CostEstimate(flops=flops, bytes_accessed=size, transcendentals=0)


def causal_kernel(mask_ref):
    key_no = lax.broadcasted_iota(jnp.int32, mask_ref.shape, 0)
    token_no = lax.broadcasted_iota(jnp.int32, mask_ref.shape, 1) % CL
    mask_ref[...] = jnp.where(key_no <= token_no, 0.0, -jnp.inf)


def causal():
    return pl.pallas_call(
        causal_kernel,
        out_specs=VMEM_SPEC,
        out_shape=jax.ShapeDtypeStruct((CL, CHUNK), F32),
        compiler_params=params(),
        cost_estimate=cost(4 * 10**9, 10**6),
        name="causal",
    )()


def pack_kernel(keys_ref, values_ref, kg_ref, out_ref):
    size, width = kg_ref.shape[1], keys_ref.shape[1]
    for head in range(width // size):
        columns = slice(head * size, (head + 1) * size)
        unit_rows, _ = unit(keys_ref[:, columns].astype(F32))
        out_ref[:, columns] = (unit_rows * kg_ref[...]).astype(BF16)
    out_ref[:, width:] = values_ref[...]


def pack(keys, values, key_gain):
    return pl.pallas_call(
        pack_kernel,
        in_specs=[VMEM_SPEC] * 3,
        out_specs=VMEM_SPEC,
        out_shape=jax.ShapeDtypeStruct((keys.shape[0], 2 * keys.shape[1]), BF16),
        compiler_params=params(),
        cost_estimate=cost(4 * 10**9, 10**6),
        name="pack",
    )(keys, values, key_gain)


def head_columns(head, group, size):
    return [slice((head * group + g) * size, (head * group + g + 1) * size) for g in range(group)]


def slot_rows(slot):
    return pl.ds(pl.multiple_of(slot * CL, CL), CL)


def prepare_kernel(live_ref, q_ref, do_ref, qg_ref, raw_ref, recip_ref, queries_ref, grads_ref, col_ref):
    size = col_ref.shape[0]
    heads = raw_ref.shape[1] // size
    group = q_ref.shape[1] // raw_ref.shape[1]
    column = jnp.broadcast_to(qg_ref[...], (size, size)).T
    for at in range(0, col_ref.shape[1], size):
        col_ref[:, at:at + size] = column

    def live(slot, carry):
        for head in range(heads):
            places = head_columns(head, group, size)
            rows = slice(head * size, (head + 1) * size)
            half = jnp.concatenate([q_ref[slot_rows(slot), place] for place in places], axis=0).T
            raw_ref[slot, rows, :] = half
            raw = half.astype(F32)
            recip = lax.rsqrt(jnp.mean(raw * raw, axis=0, keepdims=True) + EPS)
            recip_ref[slot, head:head + 1, :] = recip
            queries_ref[slot, rows, :] = (raw * recip * col_ref[...]).astype(BF16)
            grads_ref[slot, rows, :] = jnp.concatenate([do_ref[slot_rows(slot), place] for place in places], axis=0).T
        return carry

    lax.fori_loop(0, live_ref[0], live, 0)


def prepare(live_counts, queries, out_grad, query_gain, slots, width):
    size = query_gain.shape[1]
    lanes = queries.shape[1] // width * CL
    turned = jax.ShapeDtypeStruct((slots, width, lanes), BF16)
    return pl.pallas_call(
        prepare_kernel,
        in_specs=[SMEM_SPEC] + [VMEM_SPEC] * 3,
        out_specs=[VMEM_SPEC] * 5,
        out_shape=[
            turned, jax.ShapeDtypeStruct((slots, 8, lanes), F32), turned, turned,
            jax.ShapeDtypeStruct((size, lanes), F32),
        ],
        compiler_params=params(),
        cost_estimate=cost(2 * 10**9, 6 * queries.size),
        name="prepare",
    )(live_counts, queries, out_grad, query_gain)


def attention_kernel(*refs, parts, heads):
    live_ref, prompt_ref, me_ref, queries_ref, grads_ref, ck_ref, cv_ref, kg_ref, mask_ref = refs[:9]
    pieces, refs = refs[9:9 + parts], refs[9 + parts:]
    att_ref, ds_ref, pool_keys, own_keys, own_acc, term_ref, keep_ref = refs[:7]
    send_ref, refs = (refs[7], refs[8:]) if parts > 1 else (None, refs[7:])
    acc, pool_values, pool_values_t, own_values_t = refs[:4]
    size = kg_ref.shape[1]
    width = heads * size
    slots, _, lanes = queries_ref.shape
    per_head = lanes // CHUNK
    count = heads * per_head
    weights, grads = refs[4:4 + heads], refs[4 + heads:4 + 2 * heads]
    scores, summed = refs[4 + 2 * heads:4 + 2 * heads + count], refs[4 + 2 * heads + count:]
    score_scale = 1.0 / math.sqrt(size)
    shard = pieces[0].shape[0]

    def columns(head):
        return slice(head * size, (head + 1) * size)

    def piece_rows(piece_no):
        return pl.ds(pl.multiple_of((me_ref[0] ^ piece_no) * shard, shard), shard)

    acc[...] = jnp.zeros_like(acc)
    own_acc[...] = jnp.zeros_like(own_acc)
    for piece_no, piece in enumerate(pieces):
        pool_keys[piece_rows(piece_no), :] = piece[:, :width]
        pool_values[piece_rows(piece_no), :] = piece[:, width:]
    for head in range(heads):
        pool_values_t[columns(head), :] = pool_values[:, columns(head)].T
        own_unit, _ = unit(ck_ref[:, columns(head)].astype(F32))
        own_keys[:, columns(head)] = (own_unit * kg_ref[...]).astype(BF16)
        for slot in range(slots):
            own_values_t[slot, head] = cv_ref[slot * CL:(slot + 1) * CL, columns(head)].T

    def prompt_rows(slot):
        return pl.ds(pl.multiple_of(prompt_ref[slot] * PL, PL), PL)

    def part(no):
        head = no // per_head
        return head, columns(head), slice(no % per_head * CHUNK, (no % per_head + 1) * CHUNK)

    def begin(slot, no):
        _, place, span = part(no)
        keys = jnp.concatenate([pool_keys[prompt_rows(slot), place], own_keys[slot_rows(slot), place]], axis=0)
        scores[no][...] = dot(keys, queries_ref[slot, place, span])

    def weigh(slot, no):
        head, place, span = part(no)
        prompt, own = scores[no][:PL, :], scores[no][PL:, :] + mask_ref[...]
        factor = score_scale * math.log2(math.e)
        high = jnp.maximum(jnp.max(prompt, axis=0, keepdims=True), jnp.max(own, axis=0, keepdims=True))
        both = jnp.concatenate([prompt, own], axis=0)
        half = jnp.exp2((both - high) * factor).astype(BF16)
        weights[head][:, span] = half
        values_t = jnp.concatenate([pool_values_t[place, prompt_rows(slot)], own_values_t[slot, head]], axis=1)
        values_t = jnp.concatenate([values_t, jnp.ones((TAIL, PL + CL), BF16)], axis=0)
        summed[no][...] = dot(values_t, half)

    def back(slot, no):
        head, place, span = part(no)
        inverse = 1.0 / summed[no][size:size + 1, :]
        attended = (summed[no][:size, :] * inverse).astype(BF16)
        att_ref[slot, place, span] = attended
        scaled = (grads_ref[slot, place, span].astype(F32) * inverse).astype(BF16)
        grads[head][:, span] = scaled
        delta = jnp.sum(scaled.astype(F32) * attended.astype(F32), axis=0, keepdims=True)
        values = jnp.concatenate([pool_values[prompt_rows(slot), place], cv_ref[slot_rows(slot), place]], axis=0)
        score_grad = weights[head][:, span].astype(F32) * (dot(values, scaled) - delta)
        ds_ref[slot, head, :, span] = score_grad.astype(BF16)

    def close(slot, head):
        value_grad = dot_nt(weights[head][...], grads[head][...])
        key_grad = dot_nt(ds_ref[slot, head], queries_ref[slot, columns(head), :])
        acc[prompt_rows(slot), columns(head)] += key_grad[:PL]
        acc[prompt_rows(slot), width + head * size:width + (head + 1) * size] += value_grad[:PL]
        own_acc[slot, head, 0] = key_grad[PL:]
        own_acc[slot, head, 1] = value_grad[PL:]

    def ticks(now, before):
        for tick in range(count):
            if now is not None:
                begin(now, tick)
            for number, stage in ((1, weigh), (2, back)):
                slot = now if tick >= number else before
                if slot is not None:
                    stage(slot, (tick - number) % count)
            done = (tick - 3) % count
            slot = now if tick >= 3 else before
            if slot is not None and done % per_head == per_head - 1:
                close(slot, done // per_head)

    def step(slot, carry):
        ticks(slot, slot - 1)
        return carry

    ticks(0, None)
    lax.fori_loop(1, live_ref[0], step, 0)
    ticks(None, live_ref[0] - 1)

    total = jnp.zeros((1, size), F32)
    for head in range(heads):
        own_grad = own_acc[:, head, 0].reshape(slots * CL, size)
        total = total + jnp.sum(own_grad * own_keys[:, columns(head)].astype(F32), axis=0, keepdims=True)
        pool_term = acc[:, columns(head)] * pool_keys[:, columns(head)].astype(F32)
        total = total + jnp.sum(pool_term, axis=0, keepdims=True)
    term_ref[...] = jnp.broadcast_to(total * score_scale, term_ref.shape)
    if parts == 1:
        keep_ref[:, :width] = acc[:, :width] * score_scale
        keep_ref[:, width:] = acc[:, width:]
    else:
        for piece_no in range(parts):
            place = slice(piece_no // 2 * shard, (piece_no // 2 + 1) * shard)
            ref = keep_ref if piece_no % 2 == 0 else send_ref
            ref[place, :width] = (acc[piece_rows(piece_no), :width] * score_scale).astype(ref.dtype)
            ref[place, width:] = acc[piece_rows(piece_no), width:].astype(ref.dtype)


def attention(live_counts, slot_prompts, me, queries, grads, keys, values, key_gain, mask, pieces):
    size = key_gain.shape[1]
    slots, width, lanes = queries.shape
    heads = width // size
    parts = len(pieces)
    pool_rows = parts * pieces[0].shape[0]
    count = heads * lanes // CHUNK
    span = PL + CL
    out_shape = [
        jax.ShapeDtypeStruct(queries.shape, BF16),
        jax.ShapeDtypeStruct((slots, heads, span, lanes), BF16),
        jax.ShapeDtypeStruct((pool_rows, width), BF16),
        jax.ShapeDtypeStruct(keys.shape, BF16),
        jax.ShapeDtypeStruct((slots, heads, 2, CL, size), F32),
        jax.ShapeDtypeStruct((8, size), F32),
    ]
    if parts > 1:
        half = (pool_rows // 2, 2 * width)
        out_shape += [jax.ShapeDtypeStruct(half, F32), jax.ShapeDtypeStruct(half, BF16)]
    else:
        out_shape += [jax.ShapeDtypeStruct((pool_rows, 2 * width), F32)]
    return pl.pallas_call(
        functools.partial(attention_kernel, parts=parts, heads=heads),
        in_specs=[SMEM_SPEC] * 3 + [VMEM_SPEC] * (6 + parts),
        out_specs=[VMEM_SPEC] * len(out_shape),
        out_shape=out_shape,
        scratch_shapes=[
            pltpu.VMEM((pool_rows, 2 * width), F32),
            pltpu.VMEM((pool_rows, width), BF16),
            pltpu.VMEM((width, pool_rows), BF16),
            pltpu.VMEM((slots, heads, size, CL), BF16),
        ]
        + [pltpu.VMEM((span, lanes), BF16)] * heads
        + [pltpu.VMEM((size, lanes), BF16)] * heads
        + [pltpu.VMEM((span, CHUNK), F32)] * count
        + [pltpu.VMEM((size + TAIL, CHUNK), F32)] * count,
        compiler_params=params(),
        cost_estimate=cost(3 * 10**9, 10**7),
        name="attention",
    )(live_counts, slot_prompts, me, queries, grads, keys, values, key_gain, mask, *pieces)


def post_kernel(
    live_ref, prompt_ref, att_t_ref, ds_ref, pool_keys, own_keys_ref, own_acc, raw_ref, recip_ref, col_ref,
    ck_ref, kg_ref, att_ref, dq_ref, dk_ref, dv_ref, att_out, dq_out, zeros, dk_out, dv_out, sems, own_sems,
):
    slots, width, lanes = raw_ref.shape
    size = col_ref.shape[0]
    heads = width // size
    group = att_ref.shape[1] // width
    score_scale = 1.0 / math.sqrt(size)

    def copy_out(source, slot, which):
        target = (att_ref, dq_ref)[which]
        return pltpu.make_async_copy(source, target.at[slot_rows(slot), :], sems.at[which, slot])

    def dead(slot, carry):
        for which in range(2):
            copy_out(zeros, slot, which).start()
        return carry

    def live(slot, carry):
        rows = pl.ds(pl.multiple_of(prompt_ref[slot] * PL, PL), PL)
        for head in range(heads):
            columns = slice(head * size, (head + 1) * size)
            keys_t = jnp.concatenate([pool_keys[rows, columns], own_keys_ref[slot_rows(slot), columns]], axis=0).T
            query_grad = dot(keys_t, ds_ref[slot, head]) * score_scale
            recip = recip_ref[slot, head:head + 1, :]
            query_unit = raw_ref[slot, columns, :].astype(F32) * recip
            scaled = query_grad * col_ref[...]
            mean = jnp.mean(query_unit * scaled, axis=0, keepdims=True)
            query_out = (recip * (scaled - query_unit * mean)).astype(BF16).T
            attended = att_t_ref[slot, columns, :].T
            for g, place in enumerate(head_columns(head, group, size)):
                att_out[slot, :, place] = attended[g * CL:(g + 1) * CL]
                dq_out[slot, :, place] = query_out[g * CL:(g + 1) * CL]
        for which in range(2):
            copy_out((att_out, dq_out)[which].at[slot], slot, which).start()
        return carry

    zeros[...] = jnp.zeros_like(zeros)
    lax.fori_loop(live_ref[0], slots, dead, 0)
    for head in range(heads):
        columns = slice(head * size, (head + 1) * size)
        own_grad = own_acc[:, head, 0].reshape(slots * CL, size) * score_scale
        own_unit, own_recip = unit(ck_ref[:, columns].astype(F32))
        dk_out[:, columns] = norm_back(own_grad, own_unit, own_recip, kg_ref[...]).astype(BF16)
        dv_out[:, columns] = own_acc[:, head, 1].reshape(slots * CL, size).astype(BF16)
    own_copies = [
        pltpu.make_async_copy(dk_out, dk_ref, own_sems.at[0]),
        pltpu.make_async_copy(dv_out, dv_ref, own_sems.at[1]),
    ]
    for copy in own_copies:
        copy.start()
    lax.fori_loop(0, live_ref[0], live, 0)
    for copy in own_copies:
        copy.wait()
    for slot in range(slots):
        for which in range(2):
            copy_out(zeros, slot, which).wait()


def post(
    live_counts, slot_prompts, att_t, score_grads, pool_keys, own_keys, own_acc, raw, recip, query_col,
    keys, key_gain, shape,
):
    slots = raw.shape[0]
    out = jax.ShapeDtypeStruct(shape, BF16)
    own = jax.ShapeDtypeStruct(keys.shape, BF16)
    slab = pltpu.VMEM((slots, CL, shape[1]), BF16)
    return pl.pallas_call(
        post_kernel,
        in_specs=[SMEM_SPEC] * 2 + [VMEM_SPEC] * 10,
        out_specs=[HBM_SPEC] * 4,
        out_shape=[out, out, own, own],
        scratch_shapes=[
            slab, slab, pltpu.VMEM((CL, shape[1]), BF16), pltpu.VMEM(keys.shape, BF16), pltpu.VMEM(keys.shape, BF16),
            pltpu.SemaphoreType.DMA((2, slots)), pltpu.SemaphoreType.DMA((2,)),
        ],
        compiler_params=params(),
        cost_estimate=cost(3 * 10**9, 4 * 10**6),
        name="post",
    )(
        live_counts, slot_prompts, att_t, score_grads, pool_keys, own_keys, own_acc, raw, recip, query_col,
        keys, key_gain,
    )


def tree(terms):
    while len(terms) > 1:
        terms = [left + right for left, right in zip(terms[::2], terms[1::2])]
    return terms[0]


def add_kernel(keep_ref, came_ref, *refs, terms):
    tail = gain_rows(tree([ref[0:1, :] for ref in refs[:terms]]))
    size = tail.shape[1]
    own_ref, send_refs = refs[terms], refs[terms + 1:]
    blocks = len(send_refs) + 1
    shard = keep_ref.shape[0] // blocks
    for at in range(blocks):
        place = slice(at * shard, (at + 1) * shard)
        ref = send_refs[at - 1] if at > 0 else own_ref
        total = keep_ref[place, :] + came_ref[place, :].astype(F32)
        for slab in range(keep_ref.shape[1] // size):
            ref[slab * shard:(slab + 1) * shard, :] = total[:, slab * size:(slab + 1) * size].astype(ref.dtype)
        ref[ref.shape[0] - TAIL:, :] = tail.astype(ref.dtype)


def add(keep, came, terms, blocks):
    size = terms[0].shape[1]
    shape = (keep.size // blocks // size + TAIL, size)
    return pl.pallas_call(
        functools.partial(add_kernel, terms=len(terms)),
        in_specs=[VMEM_SPEC] * (2 + len(terms)),
        out_specs=[VMEM_SPEC] * blocks,
        out_shape=[jax.ShapeDtypeStruct(shape, F32)] + [jax.ShapeDtypeStruct(shape, BF16)] * (blocks - 1),
        compiler_params=params(),
        name="add",
    )(keep, came, *terms)


def chips_kernel(*refs):
    total = tree([gain_term(ref[ref.shape[0] - TAIL:, :]) for ref in refs[:-1]])
    refs[-1][...] = jnp.broadcast_to(total, refs[-1].shape)


def sum_chips(blocks):
    return pl.pallas_call(
        chips_kernel,
        in_specs=[VMEM_SPEC] * len(blocks),
        out_specs=VMEM_SPEC,
        out_shape=jax.ShapeDtypeStruct((8, blocks[0].shape[1]), F32),
        compiler_params=params(),
        name="sum_chips",
    )(*blocks)


def last_kernel(*refs):
    terms, (qg_ref, kg_ref, query_ref, key_ref) = refs[:-4], refs[-4:]
    total = tree([ref[0:1, :] for ref in terms])
    query_ref[...] = total / qg_ref[...]
    key_ref[...] = total / kg_ref[...]


def gain_grads(terms, query_gain, key_gain):
    row = jax.ShapeDtypeStruct(query_gain.shape, F32)
    return pl.pallas_call(
        last_kernel,
        in_specs=[VMEM_SPEC] * (len(terms) + 2),
        out_specs=[VMEM_SPEC] * 2,
        out_shape=[row, row],
        compiler_params=params(),
        name="gain_grads",
    )(*terms, query_gain, key_gain)


def finish_kernel(*refs):
    parts, (raw_ref, kg_ref, key_ref, value_ref) = refs[:-4], refs[-4:]
    size = kg_ref.shape[1]
    shard, width = raw_ref.shape
    heads = width // size
    for slab in range(2 * heads):
        rows = slice(slab * shard, (slab + 1) * shard)
        total = parts[0][rows, :]
        for ref in parts[1:]:
            total = total + ref[rows, :].astype(F32)
        columns = slice(slab % heads * size, (slab % heads + 1) * size)
        if slab < heads:
            unit_rows, recip = unit(raw_ref[:, columns].astype(F32))
            key_ref[:, columns] = norm_back(total, unit_rows, recip, kg_ref[...])
        else:
            value_ref[:, columns] = total


def finish(blocks, raw, key_gain):
    shape = jax.ShapeDtypeStruct(raw.shape, F32)
    return pl.pallas_call(
        finish_kernel,
        in_specs=[VMEM_SPEC] * (len(blocks) + 2),
        out_specs=[VMEM_SPEC] * 2,
        out_shape=[shape, shape],
        compiler_params=params(),
        cost_estimate=cost(10**8, 10**6),
        name="finish",
    )(*blocks, raw, key_gain)


def swap(values, axis, step):
    return lax.ppermute(values, axis, [(i, i ^ step) for i in range(lax.axis_size(axis))])


def local(
    comp_queries, comp_keys, comp_values, prompt_keys, prompt_values,
    query_gain, key_gain, out_grad, live_counts, slot_prompts,
):
    grp, tp = lax.axis_size("grp"), lax.axis_size("tp")
    shard = prompt_keys.shape[0]
    size = query_gain.shape[0]
    by_permute = shard % 16 == 0 and grp > 1 and grp & (grp - 1) == 0 and tp & (tp - 1) == 0
    slots, width = slot_prompts.shape[0], comp_keys.shape[1]
    query_gain, key_gain = query_gain.reshape(1, size), key_gain.reshape(1, size)
    me = lax.axis_index("grp").astype(jnp.int32).reshape(1) if by_permute else jnp.zeros((1,), jnp.int32)
    mask, me, keys_in, values_in = lax.optimization_barrier((causal(), me, prompt_keys, prompt_values))
    mine = pack(keys_in, values_in, key_gain)
    raw, recip, queries, grads, query_col = prepare(live_counts, comp_queries, out_grad, query_gain, slots, width)
    if by_permute:
        even = [mine] + [swap(mine, "grp", step) for step in range(2, grp, 2)]
        odd = [swap(mine, "grp", 1)]
        for at in range(1, len(even)):
            even[at], query_col = lax.optimization_barrier((even[at], query_col))
            odd.append(swap(even[at], "grp", 1))
        pieces = [piece for pair in zip(even, odd) for piece in pair]
    else:
        pieces = [lax.all_gather(mine, "grp", axis=0, tiled=True)]
    att_t, score_grads, pool_keys, own_keys, own_acc, term, keep, *send = attention(
        live_counts, slot_prompts, me, queries, grads, comp_keys, comp_values, key_gain, mask, pieces,
    )
    attended, query_grads, key_grads, value_grads = post(
        live_counts, slot_prompts, att_t, score_grads, pool_keys, own_keys, own_acc, raw, recip, query_col,
        comp_keys, key_gain, comp_queries.shape,
    )
    if by_permute:
        came = swap(send[0], "grp", 1)
        others = {step: swap(term, "tp", step) for step in range(tp - 1, 0, -1)}
        terms = [term] + [others[step] for step in range(1, tp)]
        own, *blocks = add(keep, came, terms, grp // 2)
        others = {at: swap(blocks[at], "grp", 2 * at + 2) for at in range(len(blocks) - 1, -1, -1)}
        blocks = [own] + [others[at] for at in range(len(blocks))]
        blocks, attended = lax.optimization_barrier((blocks, attended))
        total = sum_chips(blocks)
        terms = [total, swap(total, "grp", 1)]
    else:
        block = lax.psum_scatter(keep, "grp", scatter_dimension=0, tiled=True)
        blocks = [jnp.concatenate([block[:, at:at + size] for at in range(0, 2 * width, size)], axis=0)]
        terms = [lax.psum(term, ("grp", "tp"))]
    prompt_key_grads, prompt_value_grads = finish(blocks, prompt_keys, key_gain)
    query_gain_grad, key_gain_grad = gain_grads(terms, query_gain, key_gain)
    return (
        attended, query_grads, key_grads, value_grads, prompt_key_grads, prompt_value_grads,
        query_gain_grad.reshape(size), key_gain_grad.reshape(size),
    )


def solution(mesh):
    split, whole = P("grp", "tp"), P()
    return jax.shard_map(
        local,
        mesh=mesh,
        in_specs=(split, split, split, split, split, whole, whole, split, P("grp"), P("grp")),
        out_specs=(split, split, split, split, split, split, whole, whole),
        check_vma=False,
    )
```

```python
import functools
import math

import jax
import jax.numpy as jnp
from jax import lax
from jax.experimental import pallas as pl
from jax.experimental.pallas import tpu as pltpu
from jax.sharding import PartitionSpec as P

PL = 384
CL = 64
EPS = 1e-06
TAIL = 16
CHUNK = 256
VMEM_LIMIT = 24 * 1024 * 1024
F32 = jnp.float32
BF16 = jnp.bfloat16
SMEM_SPEC = pl.BlockSpec(memory_space=pltpu.SMEM)
VMEM_SPEC = pl.BlockSpec(memory_space=pltpu.VMEM)
HBM_SPEC = pl.BlockSpec(memory_space=pltpu.HBM)


def dot(left, right):
    return jnp.dot(left, right, preferred_element_type=F32)


def dot_nt(left, right):
    return lax.dot_general(left, right, (((1,), (1,)), ((), ())), preferred_element_type=F32)


def unit(raw):
    recip = lax.rsqrt(jnp.mean(raw * raw, axis=-1, keepdims=True) + EPS)
    return raw * recip, recip


def norm_back(upstream, unit_rows, recip, gain):
    scaled = upstream * gain
    return recip * (scaled - unit_rows * jnp.mean(unit_rows * scaled, axis=-1, keepdims=True))


def gain_rows(term):
    upper = term.astype(BF16).astype(F32)
    rows = jnp.concatenate([upper, term - upper, jnp.zeros((TAIL - 2, term.shape[1]), F32)], axis=0)
    return rows.astype(BF16)


def gain_term(rows):
    return rows[0:1].astype(F32) + rows[1:2].astype(F32)


def params(limit=VMEM_LIMIT):
    return pltpu.CompilerParams(vmem_limit_bytes=limit)


def cost(flops, size):
    return pl.CostEstimate(flops=flops, bytes_accessed=size, transcendentals=0)


def causal_kernel(mask_ref):
    key_no = lax.broadcasted_iota(jnp.int32, mask_ref.shape, 0)
    token_no = lax.broadcasted_iota(jnp.int32, mask_ref.shape, 1) % CL
    mask_ref[...] = jnp.where(key_no <= token_no, 0.0, -jnp.inf)


def causal():
    return pl.pallas_call(
        causal_kernel,
        out_specs=VMEM_SPEC,
        out_shape=jax.ShapeDtypeStruct((CL, CHUNK), F32),
        compiler_params=params(),
        cost_estimate=cost(4 * 10**9, 10**6),
        name="causal",
    )()


def pack_kernel(keys_ref, values_ref, kg_ref, out_ref):
    size, width = kg_ref.shape[1], keys_ref.shape[1]
    for head in range(width // size):
        columns = slice(head * size, (head + 1) * size)
        unit_rows, _ = unit(keys_ref[:, columns].astype(F32))
        out_ref[:, columns] = (unit_rows * kg_ref[...]).astype(BF16)
    out_ref[:, width:] = values_ref[...]


def pack(keys, values, key_gain):
    return pl.pallas_call(
        pack_kernel,
        in_specs=[VMEM_SPEC] * 3,
        out_specs=VMEM_SPEC,
        out_shape=jax.ShapeDtypeStruct((keys.shape[0], 2 * keys.shape[1]), BF16),
        compiler_params=params(),
        cost_estimate=cost(4 * 10**9, 10**6),
        name="pack",
    )(keys, values, key_gain)


def head_columns(head, group, size):
    return [slice((head * group + g) * size, (head * group + g + 1) * size) for g in range(group)]


def slot_rows(slot):
    return pl.ds(pl.multiple_of(slot * CL, CL), CL)


def prepare_kernel(live_ref, q_ref, do_ref, qg_ref, raw_ref, recip_ref, queries_ref, grads_ref, col_ref):
    size = col_ref.shape[0]
    heads = raw_ref.shape[1] // size
    group = q_ref.shape[1] // raw_ref.shape[1]
    column = jnp.broadcast_to(qg_ref[...], (size, size)).T
    for at in range(0, col_ref.shape[1], size):
        col_ref[:, at:at + size] = column

    def live(slot, carry):
        for head in range(heads):
            places = head_columns(head, group, size)
            rows = slice(head * size, (head + 1) * size)
            half = jnp.concatenate([q_ref[slot_rows(slot), place] for place in places], axis=0).T
            raw_ref[slot, rows, :] = half
            raw = half.astype(F32)
            recip = lax.rsqrt(jnp.mean(raw * raw, axis=0, keepdims=True) + EPS)
            recip_ref[slot, head:head + 1, :] = recip
            queries_ref[slot, rows, :] = (raw * recip * col_ref[...]).astype(BF16)
            grads_ref[slot, rows, :] = jnp.concatenate([do_ref[slot_rows(slot), place] for place in places], axis=0).T
        return carry

    lax.fori_loop(0, live_ref[0], live, 0)


def prepare(live_counts, queries, out_grad, query_gain, slots, width):
    size = query_gain.shape[1]
    lanes = queries.shape[1] // width * CL
    turned = jax.ShapeDtypeStruct((slots, width, lanes), BF16)
    return pl.pallas_call(
        prepare_kernel,
        in_specs=[SMEM_SPEC] + [VMEM_SPEC] * 3,
        out_specs=[VMEM_SPEC] * 5,
        out_shape=[
            turned, jax.ShapeDtypeStruct((slots, 8, lanes), F32), turned, turned,
            jax.ShapeDtypeStruct((size, lanes), F32),
        ],
        compiler_params=params(),
        cost_estimate=cost(2 * 10**9, 6 * queries.size),
        name="prepare",
    )(live_counts, queries, out_grad, query_gain)


def attention_kernel(*refs, parts, heads):
    live_ref, prompt_ref, me_ref, queries_ref, grads_ref, ck_ref, cv_ref, kg_ref, mask_ref = refs[:9]
    pieces, refs = refs[9:9 + parts], refs[9 + parts:]
    att_ref, ds_ref, pool_keys, own_keys, own_acc, term_ref, keep_ref = refs[:7]
    send_ref, refs = (refs[7], refs[8:]) if parts > 1 else (None, refs[7:])
    acc, pool_values, pool_values_t, own_values_t = refs[:4]
    size = kg_ref.shape[1]
    width = heads * size
    slots, _, lanes = queries_ref.shape
    per_head = lanes // CHUNK
    count = heads * per_head
    weights, grads = refs[4:4 + heads], refs[4 + heads:4 + 2 * heads]
    scores, summed = refs[4 + 2 * heads:4 + 2 * heads + count], refs[4 + 2 * heads + count:]
    score_scale = 1.0 / math.sqrt(size)
    shard = pieces[0].shape[0]

    def columns(head):
        return slice(head * size, (head + 1) * size)

    def piece_rows(piece_no):
        return pl.ds(pl.multiple_of((me_ref[0] ^ piece_no) * shard, shard), shard)

    acc[...] = jnp.zeros_like(acc)
    own_acc[...] = jnp.zeros_like(own_acc)
    for piece_no, piece in enumerate(pieces):
        pool_keys[piece_rows(piece_no), :] = piece[:, :width]
        pool_values[piece_rows(piece_no), :] = piece[:, width:]
    for head in range(heads):
        pool_values_t[columns(head), :] = pool_values[:, columns(head)].T
        own_unit, _ = unit(ck_ref[:, columns(head)].astype(F32))
        own_keys[:, columns(head)] = (own_unit * kg_ref[...]).astype(BF16)
        for slot in range(slots):
            own_values_t[slot, head] = cv_ref[slot * CL:(slot + 1) * CL, columns(head)].T

    def prompt_rows(slot):
        return pl.ds(pl.multiple_of(prompt_ref[slot] * PL, PL), PL)

    def part(no):
        head = no // per_head
        return head, columns(head), slice(no % per_head * CHUNK, (no % per_head + 1) * CHUNK)

    def begin(slot, no):
        _, place, span = part(no)
        keys = jnp.concatenate([pool_keys[prompt_rows(slot), place], own_keys[slot_rows(slot), place]], axis=0)
        scores[no][...] = dot(keys, queries_ref[slot, place, span])

    def weigh(slot, no):
        head, place, span = part(no)
        prompt, own = scores[no][:PL, :], scores[no][PL:, :] + mask_ref[...]
        factor = score_scale * math.log2(math.e)
        high = jnp.maximum(jnp.max(prompt, axis=0, keepdims=True), jnp.max(own, axis=0, keepdims=True))
        both = jnp.concatenate([prompt, own], axis=0)
        half = jnp.exp2((both - high) * factor).astype(BF16)
        weights[head][:, span] = half
        values_t = jnp.concatenate([pool_values_t[place, prompt_rows(slot)], own_values_t[slot, head]], axis=1)
        values_t = jnp.concatenate([values_t, jnp.ones((TAIL, PL + CL), BF16)], axis=0)
        summed[no][...] = dot(values_t, half)

    def back(slot, no):
        head, place, span = part(no)
        inverse = 1.0 / summed[no][size:size + 1, :]
        attended = (summed[no][:size, :] * inverse).astype(BF16)
        att_ref[slot, place, span] = attended
        scaled = (grads_ref[slot, place, span].astype(F32) * inverse).astype(BF16)
        grads[head][:, span] = scaled
        delta = jnp.sum(scaled.astype(F32) * attended.astype(F32), axis=0, keepdims=True)
        values = jnp.concatenate([pool_values[prompt_rows(slot), place], cv_ref[slot_rows(slot), place]], axis=0)
        score_grad = weights[head][:, span].astype(F32) * (dot(values, scaled) - delta)
        ds_ref[slot, head, :, span] = score_grad.astype(BF16)

    def close(slot, head):
        value_grad = dot_nt(weights[head][...], grads[head][...])
        key_grad = dot_nt(ds_ref[slot, head], queries_ref[slot, columns(head), :])
        acc[prompt_rows(slot), columns(head)] += key_grad[:PL]
        acc[prompt_rows(slot), width + head * size:width + (head + 1) * size] += value_grad[:PL]
        own_acc[slot, head, 0] = key_grad[PL:]
        own_acc[slot, head, 1] = value_grad[PL:]

    def ticks(now, before):
        for tick in range(count):
            if now is not None:
                begin(now, tick)
            for number, stage in ((1, weigh), (2, back)):
                slot = now if tick >= number else before
                if slot is not None:
                    stage(slot, (tick - number) % count)
            done = (tick - 3) % count
            slot = now if tick >= 3 else before
            if slot is not None and done % per_head == per_head - 1:
                close(slot, done // per_head)

    def step(slot, carry):
        ticks(slot, slot - 1)
        return carry

    ticks(0, None)
    lax.fori_loop(1, live_ref[0], step, 0)
    ticks(None, live_ref[0] - 1)

    total = jnp.zeros((1, size), F32)
    for head in range(heads):
        own_grad = own_acc[:, head, 0].reshape(slots * CL, size)
        total = total + jnp.sum(own_grad * own_keys[:, columns(head)].astype(F32), axis=0, keepdims=True)
        pool_term = acc[:, columns(head)] * pool_keys[:, columns(head)].astype(F32)
        total = total + jnp.sum(pool_term, axis=0, keepdims=True)
    term_ref[...] = jnp.broadcast_to(total * score_scale, term_ref.shape)
    if parts == 1:
        keep_ref[:, :width] = acc[:, :width] * score_scale
        keep_ref[:, width:] = acc[:, width:]
    else:
        for piece_no in range(parts):
            place = slice(piece_no // 2 * shard, (piece_no // 2 + 1) * shard)
            ref = keep_ref if piece_no % 2 == 0 else send_ref
            ref[place, :width] = (acc[piece_rows(piece_no), :width] * score_scale).astype(ref.dtype)
            ref[place, width:] = acc[piece_rows(piece_no), width:].astype(ref.dtype)


def attention(live_counts, slot_prompts, me, queries, grads, keys, values, key_gain, mask, pieces):
    size = key_gain.shape[1]
    slots, width, lanes = queries.shape
    heads = width // size
    parts = len(pieces)
    pool_rows = parts * pieces[0].shape[0]
    count = heads * lanes // CHUNK
    span = PL + CL
    out_shape = [
        jax.ShapeDtypeStruct(queries.shape, BF16),
        jax.ShapeDtypeStruct((slots, heads, span, lanes), BF16),
        jax.ShapeDtypeStruct((pool_rows, width), BF16),
        jax.ShapeDtypeStruct(keys.shape, BF16),
        jax.ShapeDtypeStruct((slots, heads, 2, CL, size), F32),
        jax.ShapeDtypeStruct((8, size), F32),
    ]
    if parts > 1:
        half = (pool_rows // 2, 2 * width)
        out_shape += [jax.ShapeDtypeStruct(half, F32), jax.ShapeDtypeStruct(half, BF16)]
    else:
        out_shape += [jax.ShapeDtypeStruct((pool_rows, 2 * width), F32)]
    return pl.pallas_call(
        functools.partial(attention_kernel, parts=parts, heads=heads),
        in_specs=[SMEM_SPEC] * 3 + [VMEM_SPEC] * (6 + parts),
        out_specs=[VMEM_SPEC] * len(out_shape),
        out_shape=out_shape,
        scratch_shapes=[
            pltpu.VMEM((pool_rows, 2 * width), F32),
            pltpu.VMEM((pool_rows, width), BF16),
            pltpu.VMEM((width, pool_rows), BF16),
            pltpu.VMEM((slots, heads, size, CL), BF16),
        ]
        + [pltpu.VMEM((span, lanes), BF16)] * heads
        + [pltpu.VMEM((size, lanes), BF16)] * heads
        + [pltpu.VMEM((span, CHUNK), F32)] * count
        + [pltpu.VMEM((size + TAIL, CHUNK), F32)] * count,
        compiler_params=params(),
        cost_estimate=cost(3 * 10**9, 10**7),
        name="attention",
    )(live_counts, slot_prompts, me, queries, grads, keys, values, key_gain, mask, *pieces)


def post_kernel(
    live_ref, prompt_ref, att_t_ref, ds_ref, pool_keys, own_keys_ref, own_acc, raw_ref, recip_ref, col_ref,
    ck_ref, kg_ref, att_ref, dq_ref, dk_ref, dv_ref, att_out, dq_out, zeros, dk_out, dv_out, sems, own_sems,
):
    slots, width, lanes = raw_ref.shape
    size = col_ref.shape[0]
    heads = width // size
    group = att_ref.shape[1] // width
    score_scale = 1.0 / math.sqrt(size)

    def copy_out(source, slot, which):
        target = (att_ref, dq_ref)[which]
        return pltpu.make_async_copy(source, target.at[slot_rows(slot), :], sems.at[which, slot])

    def dead(slot, carry):
        for which in range(2):
            copy_out(zeros, slot, which).start()
        return carry

    def live(slot, carry):
        rows = pl.ds(pl.multiple_of(prompt_ref[slot] * PL, PL), PL)
        for head in range(heads):
            columns = slice(head * size, (head + 1) * size)
            keys_t = jnp.concatenate([pool_keys[rows, columns], own_keys_ref[slot_rows(slot), columns]], axis=0).T
            query_grad = dot(keys_t, ds_ref[slot, head]) * score_scale
            recip = recip_ref[slot, head:head + 1, :]
            query_unit = raw_ref[slot, columns, :].astype(F32) * recip
            scaled = query_grad * col_ref[...]
            mean = jnp.mean(query_unit * scaled, axis=0, keepdims=True)
            query_out = (recip * (scaled - query_unit * mean)).astype(BF16).T
            attended = att_t_ref[slot, columns, :].T
            for g, place in enumerate(head_columns(head, group, size)):
                att_out[slot, :, place] = attended[g * CL:(g + 1) * CL]
                dq_out[slot, :, place] = query_out[g * CL:(g + 1) * CL]
        for which in range(2):
            copy_out((att_out, dq_out)[which].at[slot], slot, which).start()
        return carry

    zeros[...] = jnp.zeros_like(zeros)
    lax.fori_loop(live_ref[0], slots, dead, 0)
    for head in range(heads):
        columns = slice(head * size, (head + 1) * size)
        own_grad = own_acc[:, head, 0].reshape(slots * CL, size) * score_scale
        own_unit, own_recip = unit(ck_ref[:, columns].astype(F32))
        dk_out[:, columns] = norm_back(own_grad, own_unit, own_recip, kg_ref[...]).astype(BF16)
        dv_out[:, columns] = own_acc[:, head, 1].reshape(slots * CL, size).astype(BF16)
    own_copies = [
        pltpu.make_async_copy(dk_out, dk_ref, own_sems.at[0]),
        pltpu.make_async_copy(dv_out, dv_ref, own_sems.at[1]),
    ]
    for copy in own_copies:
        copy.start()
    lax.fori_loop(0, live_ref[0], live, 0)
    for copy in own_copies:
        copy.wait()
    for slot in range(slots):
        for which in range(2):
            copy_out(zeros, slot, which).wait()


def post(
    live_counts, slot_prompts, att_t, score_grads, pool_keys, own_keys, own_acc, raw, recip, query_col,
    keys, key_gain, shape,
):
    slots = raw.shape[0]
    out = jax.ShapeDtypeStruct(shape, BF16)
    own = jax.ShapeDtypeStruct(keys.shape, BF16)
    slab = pltpu.VMEM((slots, CL, shape[1]), BF16)
    return pl.pallas_call(
        post_kernel,
        in_specs=[SMEM_SPEC] * 2 + [VMEM_SPEC] * 10,
        out_specs=[HBM_SPEC] * 4,
        out_shape=[out, out, own, own],
        scratch_shapes=[
            slab, slab, pltpu.VMEM((CL, shape[1]), BF16), pltpu.VMEM(keys.shape, BF16), pltpu.VMEM(keys.shape, BF16),
            pltpu.SemaphoreType.DMA((2, slots)), pltpu.SemaphoreType.DMA((2,)),
        ],
        compiler_params=params(),
        cost_estimate=cost(3 * 10**9, 4 * 10**6),
        name="post",
    )(
        live_counts, slot_prompts, att_t, score_grads, pool_keys, own_keys, own_acc, raw, recip, query_col,
        keys, key_gain,
    )


def tree(terms):
    while len(terms) > 1:
        terms = [left + right for left, right in zip(terms[::2], terms[1::2])]
    return terms[0]


def first_partner(me):
    return 1 + me % 2, 2 - me % 2


def stack_slabs(total, size):
    return jnp.concatenate([total[:, at:at + size] for at in range(0, total.shape[1], size)], axis=0)


def add_kernel(me_ref, keep_ref, came_ref, *refs):
    terms, (own_ref, later_ref, send_ref) = refs[:-3], refs[-3:]
    tail = gain_rows(tree([ref[0:1, :] for ref in terms[:1] + terms[:0:-1]]))
    size = tail.shape[1]
    shard = keep_ref.shape[0] // 4
    block = own_ref.shape[0] - TAIL
    near, far = first_partner(me_ref[0])

    def total(number):
        rows = pl.ds(pl.multiple_of(number * shard, shard), shard)
        return stack_slabs(keep_ref[rows, :] + came_ref[rows, :].astype(F32), size)

    own_ref[:block, :] = total(0)
    own_ref[block:, :] = tail.astype(F32)
    later_ref[...] = total(far)
    send_ref[:block, :] = total(near).astype(BF16)
    send_ref[block:2 * block, :] = total(3).astype(BF16)
    send_ref[2 * block:, :] = tail


def add(me, keep, came, terms):
    size = terms[0].shape[1]
    block = keep.size // 4 // size
    return pl.pallas_call(
        add_kernel,
        in_specs=[SMEM_SPEC] + [VMEM_SPEC] * (2 + len(terms)),
        out_specs=[VMEM_SPEC] * 3,
        out_shape=[
            jax.ShapeDtypeStruct((block + TAIL, size), F32),
            jax.ShapeDtypeStruct((block, size), F32),
            jax.ShapeDtypeStruct((2 * block + TAIL, size), BF16),
        ],
        compiler_params=params(),
        name="add",
    )(me, keep, came, *terms)


def relay_kernel(own_ref, later_ref, came_ref, out_ref, send_ref):
    block = later_ref.shape[0]
    out_ref[:block, :] = own_ref[:block, :] + came_ref[:block, :].astype(F32)
    tail = gain_rows(gain_term(own_ref[block:, :]) + gain_term(came_ref[2 * block:, :]))
    out_ref[block:, :] = tail.astype(F32)
    send_ref[:block, :] = (later_ref[...] + came_ref[block:2 * block, :].astype(F32)).astype(BF16)
    send_ref[block:, :] = tail


def relay(own, later, came):
    return pl.pallas_call(
        relay_kernel,
        in_specs=[VMEM_SPEC] * 3,
        out_specs=[VMEM_SPEC] * 2,
        out_shape=[jax.ShapeDtypeStruct(own.shape, F32), jax.ShapeDtypeStruct(own.shape, BF16)],
        compiler_params=params(),
        name="relay",
    )(own, later, came)


def chips_kernel(own_ref, came_ref, out_ref):
    total = gain_term(own_ref[own_ref.shape[0] - TAIL:, :]) + gain_term(came_ref[came_ref.shape[0] - TAIL:, :])
    out_ref[...] = jnp.broadcast_to(total, out_ref.shape)


def sum_chips(own, came):
    return pl.pallas_call(
        chips_kernel,
        in_specs=[VMEM_SPEC] * 2,
        out_specs=VMEM_SPEC,
        out_shape=jax.ShapeDtypeStruct((8, own.shape[1]), F32),
        compiler_params=params(),
        name="sum_chips",
    )(own, came)


def last_kernel(*refs):
    terms, (qg_ref, kg_ref, query_ref, key_ref) = refs[:-4], refs[-4:]
    total = tree([ref[0:1, :] for ref in terms])
    query_ref[...] = total / qg_ref[...]
    key_ref[...] = total / kg_ref[...]


def gain_grads(terms, query_gain, key_gain):
    row = jax.ShapeDtypeStruct(query_gain.shape, F32)
    return pl.pallas_call(
        last_kernel,
        in_specs=[VMEM_SPEC] * (len(terms) + 2),
        out_specs=[VMEM_SPEC] * 2,
        out_shape=[row, row],
        compiler_params=params(),
        name="gain_grads",
    )(*terms, query_gain, key_gain)


def finish_kernel(*refs):
    parts, (raw_ref, kg_ref, key_ref, value_ref) = refs[:-4], refs[-4:]
    size = kg_ref.shape[1]
    shard, width = raw_ref.shape
    heads = width // size
    for slab in range(2 * heads):
        rows = slice(slab * shard, (slab + 1) * shard)
        total = parts[0][rows, :]
        for ref in parts[1:]:
            total = total + ref[rows, :].astype(F32)
        columns = slice(slab % heads * size, (slab % heads + 1) * size)
        if slab < heads:
            unit_rows, recip = unit(raw_ref[:, columns].astype(F32))
            key_ref[:, columns] = norm_back(total, unit_rows, recip, kg_ref[...])
        else:
            value_ref[:, columns] = total


def finish(blocks, raw, key_gain):
    shape = jax.ShapeDtypeStruct(raw.shape, F32)
    return pl.pallas_call(
        finish_kernel,
        in_specs=[VMEM_SPEC] * (len(blocks) + 2),
        out_specs=[VMEM_SPEC] * 2,
        out_shape=[shape, shape],
        compiler_params=params(),
        cost_estimate=cost(10**8, 10**6),
        name="finish",
    )(*blocks, raw, key_gain)


def swap(values, axis, step, odd_step=None):
    steps = (step, step if odd_step is None else odd_step)
    return lax.ppermute(values, axis, [(i, i ^ steps[i % 2]) for i in range(lax.axis_size(axis))])


def local(
    comp_queries, comp_keys, comp_values, prompt_keys, prompt_values,
    query_gain, key_gain, out_grad, live_counts, slot_prompts,
):
    grp, tp = lax.axis_size("grp"), lax.axis_size("tp")
    shard = prompt_keys.shape[0]
    size = query_gain.shape[0]
    by_permute = shard % 16 == 0 and grp == 8 and tp & (tp - 1) == 0
    slots, width = slot_prompts.shape[0], comp_keys.shape[1]
    query_gain, key_gain = query_gain.reshape(1, size), key_gain.reshape(1, size)
    me = lax.axis_index("grp").astype(jnp.int32).reshape(1) if by_permute else jnp.zeros((1,), jnp.int32)
    mask, me, keys_in, values_in = lax.optimization_barrier((causal(), me, prompt_keys, prompt_values))
    mine = pack(keys_in, values_in, key_gain)
    raw, recip, queries, grads, query_col = prepare(live_counts, comp_queries, out_grad, query_gain, slots, width)
    if by_permute:
        even = [mine] + [swap(mine, "grp", step) for step in range(2, grp, 2)]
        odd = [swap(mine, "grp", 1)]
        for at in range(1, len(even)):
            even[at], query_col = lax.optimization_barrier((even[at], query_col))
            odd.append(swap(even[at], "grp", 1))
        pieces = [piece for pair in zip(even, odd) for piece in pair]
    else:
        pieces = [lax.all_gather(mine, "grp", axis=0, tiled=True)]
    att_t, score_grads, pool_keys, own_keys, own_acc, term, keep, *send = attention(
        live_counts, slot_prompts, me, queries, grads, comp_keys, comp_values, key_gain, mask, pieces,
    )
    attended, query_grads, key_grads, value_grads = post(
        live_counts, slot_prompts, att_t, score_grads, pool_keys, own_keys, own_acc, raw, recip, query_col,
        comp_keys, key_gain, comp_queries.shape,
    )
    if by_permute:
        came = swap(send[0], "grp", 1)
        terms = [term] + [swap(term, "tp", step) for step in range(tp - 1, 0, -1)]
        own, later, sent = add(me, keep, came, terms)
        came = swap(sent, "grp", 2, 4)
        came, attended = lax.optimization_barrier((came, attended))
        own, sent = relay(own, later, came)
        blocks = [own, swap(sent, "grp", 4, 2)]
        total = sum_chips(*blocks)
        terms = [total, swap(total, "grp", 1)]
    else:
        block = lax.psum_scatter(keep, "grp", scatter_dimension=0, tiled=True)
        blocks = [jnp.concatenate([block[:, at:at + size] for at in range(0, 2 * width, size)], axis=0)]
        terms = [lax.psum(term, ("grp", "tp"))]
    prompt_key_grads, prompt_value_grads = finish(blocks, prompt_keys, key_gain)
    query_gain_grad, key_gain_grad = gain_grads(terms, query_gain, key_gain)
    return (
        attended, query_grads, key_grads, value_grads, prompt_key_grads, prompt_value_grads,
        query_gain_grad.reshape(size), key_gain_grad.reshape(size),
    )


def solution(mesh):
    split, whole = P("grp", "tp"), P()
    return jax.shard_map(
        local,
        mesh=mesh,
        in_specs=(split, split, split, split, split, whole, whole, split, P("grp"), P("grp")),
        out_specs=(split, split, split, split, split, split, whole, whole),
        check_vma=False,
    )
```

```python
import functools
import math

import jax
import jax.numpy as jnp
from jax import lax
from jax.experimental import pallas as pl
from jax.experimental.pallas import tpu as pltpu
from jax.sharding import PartitionSpec as P

PL = 384
CL = 64
EPS = 1e-06
TAIL = 16
CHUNK = 256
VMEM_LIMIT = 24 * 1024 * 1024
F32 = jnp.float32
BF16 = jnp.bfloat16
SMEM_SPEC = pl.BlockSpec(memory_space=pltpu.SMEM)
VMEM_SPEC = pl.BlockSpec(memory_space=pltpu.VMEM)
HBM_SPEC = pl.BlockSpec(memory_space=pltpu.HBM)


def dot(left, right):
    return jnp.dot(left, right, preferred_element_type=F32)


def dot_nt(left, right):
    return lax.dot_general(left, right, (((1,), (1,)), ((), ())), preferred_element_type=F32)


def unit(raw):
    recip = lax.rsqrt(jnp.mean(raw * raw, axis=-1, keepdims=True) + EPS)
    return raw * recip, recip


def norm_back(upstream, unit_rows, recip, gain):
    scaled = upstream * gain
    return recip * (scaled - unit_rows * jnp.mean(unit_rows * scaled, axis=-1, keepdims=True))


def gain_rows(term):
    upper = term.astype(BF16).astype(F32)
    rows = jnp.concatenate([upper, term - upper, jnp.zeros((TAIL - 2, term.shape[1]), F32)], axis=0)
    return rows.astype(BF16)


def gain_term(rows):
    return rows[0:1].astype(F32) + rows[1:2].astype(F32)


def params(limit=VMEM_LIMIT):
    return pltpu.CompilerParams(vmem_limit_bytes=limit)


def cost(flops, size):
    return pl.CostEstimate(flops=flops, bytes_accessed=size, transcendentals=0)


def causal_kernel(mask_ref):
    key_no = lax.broadcasted_iota(jnp.int32, mask_ref.shape, 0)
    token_no = lax.broadcasted_iota(jnp.int32, mask_ref.shape, 1) % CL
    mask_ref[...] = jnp.where(key_no <= token_no, 0.0, -jnp.inf)


def causal():
    return pl.pallas_call(
        causal_kernel,
        out_specs=VMEM_SPEC,
        out_shape=jax.ShapeDtypeStruct((CL, CHUNK), F32),
        compiler_params=params(),
        cost_estimate=cost(4 * 10**9, 10**6),
        name="causal",
    )()


def pack_kernel(keys_ref, values_ref, kg_ref, out_ref):
    size, width = kg_ref.shape[1], keys_ref.shape[1]
    for head in range(width // size):
        columns = slice(head * size, (head + 1) * size)
        unit_rows, _ = unit(keys_ref[:, columns].astype(F32))
        out_ref[:, columns] = (unit_rows * kg_ref[...]).astype(BF16)
    out_ref[:, width:] = values_ref[...]


def pack(keys, values, key_gain):
    return pl.pallas_call(
        pack_kernel,
        in_specs=[VMEM_SPEC] * 3,
        out_specs=VMEM_SPEC,
        out_shape=jax.ShapeDtypeStruct((keys.shape[0], 2 * keys.shape[1]), BF16),
        compiler_params=params(),
        cost_estimate=cost(4 * 10**9, 10**6),
        name="pack",
    )(keys, values, key_gain)


def head_columns(head, group, size):
    return [slice((head * group + g) * size, (head * group + g + 1) * size) for g in range(group)]


def slot_rows(slot):
    return pl.ds(pl.multiple_of(slot * CL, CL), CL)


def prepare_kernel(live_ref, q_ref, do_ref, qg_ref, raw_ref, recip_ref, queries_ref, grads_ref, col_ref):
    size = col_ref.shape[0]
    heads = raw_ref.shape[1] // size
    group = q_ref.shape[1] // raw_ref.shape[1]
    column = jnp.broadcast_to(qg_ref[...], (size, size)).T
    for at in range(0, col_ref.shape[1], size):
        col_ref[:, at:at + size] = column

    def live(slot, carry):
        for head in range(heads):
            places = head_columns(head, group, size)
            rows = slice(head * size, (head + 1) * size)
            half = jnp.concatenate([q_ref[slot_rows(slot), place] for place in places], axis=0).T
            raw_ref[slot, rows, :] = half
            raw = half.astype(F32)
            recip = lax.rsqrt(jnp.mean(raw * raw, axis=0, keepdims=True) + EPS)
            recip_ref[slot, head:head + 1, :] = recip
            queries_ref[slot, rows, :] = (raw * recip * col_ref[...]).astype(BF16)
            grads_ref[slot, rows, :] = jnp.concatenate([do_ref[slot_rows(slot), place] for place in places], axis=0).T
        return carry

    lax.fori_loop(0, live_ref[0], live, 0)


def prepare(live_counts, queries, out_grad, query_gain, slots, width):
    size = query_gain.shape[1]
    lanes = queries.shape[1] // width * CL
    turned = jax.ShapeDtypeStruct((slots, width, lanes), BF16)
    return pl.pallas_call(
        prepare_kernel,
        in_specs=[SMEM_SPEC] + [VMEM_SPEC] * 3,
        out_specs=[VMEM_SPEC] * 5,
        out_shape=[
            turned, jax.ShapeDtypeStruct((slots, 8, lanes), F32), turned, turned,
            jax.ShapeDtypeStruct((size, lanes), F32),
        ],
        compiler_params=params(),
        cost_estimate=cost(2 * 10**9, 6 * queries.size),
        name="prepare",
    )(live_counts, queries, out_grad, query_gain)


def attention_kernel(*refs, parts, heads):
    live_ref, prompt_ref, me_ref, queries_ref, grads_ref, ck_ref, cv_ref, kg_ref, mask_ref = refs[:9]
    pieces, refs = refs[9:9 + parts], refs[9 + parts:]
    att_ref, ds_ref, pool_keys, own_keys, own_acc, term_ref, keep_ref = refs[:7]
    send_ref, refs = (refs[7], refs[8:]) if parts > 1 else (None, refs[7:])
    acc, pool_values, pool_values_t, own_values_t = refs[:4]
    size = kg_ref.shape[1]
    width = heads * size
    slots, _, lanes = queries_ref.shape
    per_head = lanes // CHUNK
    count = heads * per_head
    weights, grads = refs[4:4 + heads], refs[4 + heads:4 + 2 * heads]
    scores, summed = refs[4 + 2 * heads:4 + 2 * heads + count], refs[4 + 2 * heads + count:]
    score_scale = 1.0 / math.sqrt(size)
    shard = pieces[0].shape[0]

    def columns(head):
        return slice(head * size, (head + 1) * size)

    def piece_rows(piece_no):
        return pl.ds(pl.multiple_of((me_ref[0] ^ piece_no) * shard, shard), shard)

    acc[...] = jnp.zeros_like(acc)
    own_acc[...] = jnp.zeros_like(own_acc)
    for piece_no, piece in enumerate(pieces):
        pool_keys[piece_rows(piece_no), :] = piece[:, :width]
        pool_values[piece_rows(piece_no), :] = piece[:, width:]
    for head in range(heads):
        pool_values_t[columns(head), :] = pool_values[:, columns(head)].T
        own_unit, _ = unit(ck_ref[:, columns(head)].astype(F32))
        own_keys[:, columns(head)] = (own_unit * kg_ref[...]).astype(BF16)
        for slot in range(slots):
            own_values_t[slot, head] = cv_ref[slot * CL:(slot + 1) * CL, columns(head)].T

    def prompt_rows(slot):
        return pl.ds(pl.multiple_of(prompt_ref[slot] * PL, PL), PL)

    def part(no):
        head = no // per_head
        return head, columns(head), slice(no % per_head * CHUNK, (no % per_head + 1) * CHUNK)

    def begin(slot, no):
        _, place, span = part(no)
        keys = jnp.concatenate([pool_keys[prompt_rows(slot), place], own_keys[slot_rows(slot), place]], axis=0)
        scores[no][...] = dot(keys, queries_ref[slot, place, span])

    def weigh(slot, no):
        head, place, span = part(no)
        prompt, own = scores[no][:PL, :], scores[no][PL:, :] + mask_ref[...]
        factor = score_scale * math.log2(math.e)
        high = jnp.maximum(jnp.max(prompt, axis=0, keepdims=True), jnp.max(own, axis=0, keepdims=True))
        both = jnp.concatenate([prompt, own], axis=0)
        half = jnp.exp2((both - high) * factor).astype(BF16)
        weights[head][:, span] = half
        values_t = jnp.concatenate([pool_values_t[place, prompt_rows(slot)], own_values_t[slot, head]], axis=1)
        values_t = jnp.concatenate([values_t, jnp.ones((TAIL, PL + CL), BF16)], axis=0)
        summed[no][...] = dot(values_t, half)

    def back(slot, no):
        head, place, span = part(no)
        inverse = 1.0 / summed[no][size:size + 1, :]
        attended = (summed[no][:size, :] * inverse).astype(BF16)
        att_ref[slot, place, span] = attended
        scaled = (grads_ref[slot, place, span].astype(F32) * inverse).astype(BF16)
        grads[head][:, span] = scaled
        delta = jnp.sum(scaled.astype(F32) * attended.astype(F32), axis=0, keepdims=True)
        values = jnp.concatenate([pool_values[prompt_rows(slot), place], cv_ref[slot_rows(slot), place]], axis=0)
        score_grad = weights[head][:, span].astype(F32) * (dot(values, scaled) - delta)
        ds_ref[slot, head, :, span] = score_grad.astype(BF16)

    def close(slot, head):
        value_grad = dot_nt(weights[head][...], grads[head][...])
        key_grad = dot_nt(ds_ref[slot, head], queries_ref[slot, columns(head), :])
        acc[prompt_rows(slot), columns(head)] += key_grad[:PL]
        acc[prompt_rows(slot), width + head * size:width + (head + 1) * size] += value_grad[:PL]
        own_acc[slot, head, 0] = key_grad[PL:]
        own_acc[slot, head, 1] = value_grad[PL:]

    def ticks(now, before):
        for tick in range(count):
            if now is not None:
                begin(now, tick)
            for number, stage in ((1, weigh), (2, back)):
                slot = now if tick >= number else before
                if slot is not None:
                    stage(slot, (tick - number) % count)
            done = (tick - 3) % count
            slot = now if tick >= 3 else before
            if slot is not None and done % per_head == per_head - 1:
                close(slot, done // per_head)

    def step(slot, carry):
        ticks(slot, slot - 1)
        return carry

    ticks(0, None)
    lax.fori_loop(1, live_ref[0], step, 0)
    ticks(None, live_ref[0] - 1)

    total = jnp.zeros((1, size), F32)
    for head in range(heads):
        own_grad = own_acc[:, head, 0].reshape(slots * CL, size)
        total = total + jnp.sum(own_grad * own_keys[:, columns(head)].astype(F32), axis=0, keepdims=True)
        pool_term = acc[:, columns(head)] * pool_keys[:, columns(head)].astype(F32)
        total = total + jnp.sum(pool_term, axis=0, keepdims=True)
    term_ref[...] = jnp.broadcast_to(total * score_scale, term_ref.shape)
    if parts == 1:
        keep_ref[:, :width] = acc[:, :width] * score_scale
        keep_ref[:, width:] = acc[:, width:]
    else:
        for piece_no in range(parts):
            place = slice(piece_no // 2 * shard, (piece_no // 2 + 1) * shard)
            ref = keep_ref if piece_no % 2 == 0 else send_ref
            ref[place, :width] = (acc[piece_rows(piece_no), :width] * score_scale).astype(ref.dtype)
            ref[place, width:] = acc[piece_rows(piece_no), width:].astype(ref.dtype)


def attention(live_counts, slot_prompts, me, queries, grads, keys, values, key_gain, mask, pieces):
    size = key_gain.shape[1]
    slots, width, lanes = queries.shape
    heads = width // size
    parts = len(pieces)
    pool_rows = parts * pieces[0].shape[0]
    count = heads * lanes // CHUNK
    span = PL + CL
    out_shape = [
        jax.ShapeDtypeStruct(queries.shape, BF16),
        jax.ShapeDtypeStruct((slots, heads, span, lanes), BF16),
        jax.ShapeDtypeStruct((pool_rows, width), BF16),
        jax.ShapeDtypeStruct(keys.shape, BF16),
        jax.ShapeDtypeStruct((slots, heads, 2, CL, size), F32),
        jax.ShapeDtypeStruct((8, size), F32),
    ]
    if parts > 1:
        half = (pool_rows // 2, 2 * width)
        out_shape += [jax.ShapeDtypeStruct(half, F32), jax.ShapeDtypeStruct(half, BF16)]
    else:
        out_shape += [jax.ShapeDtypeStruct((pool_rows, 2 * width), F32)]
    return pl.pallas_call(
        functools.partial(attention_kernel, parts=parts, heads=heads),
        in_specs=[SMEM_SPEC] * 3 + [VMEM_SPEC] * (6 + parts),
        out_specs=[VMEM_SPEC] * len(out_shape),
        out_shape=out_shape,
        scratch_shapes=[
            pltpu.VMEM((pool_rows, 2 * width), F32),
            pltpu.VMEM((pool_rows, width), BF16),
            pltpu.VMEM((width, pool_rows), BF16),
            pltpu.VMEM((slots, heads, size, CL), BF16),
        ]
        + [pltpu.VMEM((span, lanes), BF16)] * heads
        + [pltpu.VMEM((size, lanes), BF16)] * heads
        + [pltpu.VMEM((span, CHUNK), F32)] * count
        + [pltpu.VMEM((size + TAIL, CHUNK), F32)] * count,
        compiler_params=params(),
        cost_estimate=cost(3 * 10**9, 10**7),
        name="attention",
    )(live_counts, slot_prompts, me, queries, grads, keys, values, key_gain, mask, *pieces)


def copy_slots(live_ref, zeros, out, target, sems):
    slots = out.shape[0]

    def copy(source, slot):
        return pltpu.make_async_copy(source, target.at[slot_rows(slot), :], sems.at[slot])

    def dead(slot, carry):
        copy(zeros, slot).start()
        return carry

    def wait():
        for slot in range(slots):
            copy(zeros, slot).wait()

    zeros[...] = jnp.zeros_like(zeros)
    lax.fori_loop(live_ref[0], slots, dead, 0)
    return lambda slot: copy(out.at[slot], slot).start(), wait


def turn_kernel(
    live_ref, att_t_ref, own_acc, ck_ref, kg_ref, att_ref, dk_ref, dv_ref, att_out, zeros, dk_out, dv_out, sems, own_sems,
):
    slots, width, _ = att_t_ref.shape
    size = kg_ref.shape[1]
    heads = width // size
    group = att_ref.shape[1] // width
    start, wait = copy_slots(live_ref, zeros, att_out, att_ref, sems)

    def live(slot, carry):
        for head in range(heads):
            attended = att_t_ref[slot, head * size:(head + 1) * size, :].T
            for g, place in enumerate(head_columns(head, group, size)):
                att_out[slot, :, place] = attended[g * CL:(g + 1) * CL]
        start(slot)
        return carry

    lax.fori_loop(0, live_ref[0], live, 0)
    for head in range(heads):
        columns = slice(head * size, (head + 1) * size)
        own_grad = own_acc[:, head, 0].reshape(slots * CL, size) * (1.0 / math.sqrt(size))
        own_unit, own_recip = unit(ck_ref[:, columns].astype(F32))
        dk_out[:, columns] = norm_back(own_grad, own_unit, own_recip, kg_ref[...]).astype(BF16)
        dv_out[:, columns] = own_acc[:, head, 1].reshape(slots * CL, size).astype(BF16)
    own_copies = [
        pltpu.make_async_copy(dk_out, dk_ref, own_sems.at[0]),
        pltpu.make_async_copy(dv_out, dv_ref, own_sems.at[1]),
    ]
    for copy in own_copies:
        copy.start()
    for copy in own_copies:
        copy.wait()
    wait()


def turn(live_counts, att_t, own_acc, keys, key_gain, shape):
    slots = att_t.shape[0]
    own = jax.ShapeDtypeStruct(keys.shape, BF16)
    own_slab = pltpu.VMEM(keys.shape, BF16)
    return pl.pallas_call(
        turn_kernel,
        in_specs=[SMEM_SPEC] + [VMEM_SPEC] * 4,
        out_specs=[HBM_SPEC] * 3,
        out_shape=[jax.ShapeDtypeStruct(shape, BF16), own, own],
        scratch_shapes=[
            pltpu.VMEM((slots, CL, shape[1]), BF16), pltpu.VMEM((CL, shape[1]), BF16), own_slab, own_slab,
            pltpu.SemaphoreType.DMA((slots,)), pltpu.SemaphoreType.DMA((2,)),
        ],
        compiler_params=params(),
        cost_estimate=cost(2 * 10**9, 2 * 10**6),
        name="turn",
    )(live_counts, att_t, own_acc, keys, key_gain)


def post_kernel(
    live_ref, prompt_ref, ds_ref, pool_keys, own_keys_ref, raw_ref, recip_ref, col_ref, dq_ref, dq_out, zeros, sems,
):
    slots, width, lanes = raw_ref.shape
    size = col_ref.shape[0]
    heads = width // size
    group = dq_ref.shape[1] // width
    score_scale = 1.0 / math.sqrt(size)
    start, wait = copy_slots(live_ref, zeros, dq_out, dq_ref, sems)

    def live(slot, carry):
        rows = pl.ds(pl.multiple_of(prompt_ref[slot] * PL, PL), PL)
        for head in range(heads):
            columns = slice(head * size, (head + 1) * size)
            keys_t = jnp.concatenate([pool_keys[rows, columns], own_keys_ref[slot_rows(slot), columns]], axis=0).T
            query_grad = dot(keys_t, ds_ref[slot, head]) * score_scale
            recip = recip_ref[slot, head:head + 1, :]
            query_unit = raw_ref[slot, columns, :].astype(F32) * recip
            scaled = query_grad * col_ref[...]
            mean = jnp.mean(query_unit * scaled, axis=0, keepdims=True)
            query_out = (recip * (scaled - query_unit * mean)).astype(BF16).T
            for g, place in enumerate(head_columns(head, group, size)):
                dq_out[slot, :, place] = query_out[g * CL:(g + 1) * CL]
        start(slot)
        return carry

    lax.fori_loop(0, live_ref[0], live, 0)
    wait()


def post(live_counts, slot_prompts, score_grads, pool_keys, own_keys, raw, recip, query_col, shape):
    slots = raw.shape[0]
    return pl.pallas_call(
        post_kernel,
        in_specs=[SMEM_SPEC] * 2 + [VMEM_SPEC] * 6,
        out_specs=HBM_SPEC,
        out_shape=jax.ShapeDtypeStruct(shape, BF16),
        scratch_shapes=[
            pltpu.VMEM((slots, CL, shape[1]), BF16), pltpu.VMEM((CL, shape[1]), BF16),
            pltpu.SemaphoreType.DMA((slots,)),
        ],
        compiler_params=params(),
        cost_estimate=cost(3 * 10**9, 4 * 10**6),
        name="post",
    )(live_counts, slot_prompts, score_grads, pool_keys, own_keys, raw, recip, query_col)


def tree(terms):
    while len(terms) > 1:
        terms = [left + right for left, right in zip(terms[::2], terms[1::2])]
    return terms[0]


def add_kernel(keep_ref, came_ref, *refs, terms):
    tail = gain_rows(tree([ref[0:1, :] for ref in refs[:terms]]))
    size = tail.shape[1]
    own_ref, send_refs = refs[terms], refs[terms + 1:]
    blocks = len(send_refs) + 1
    shard = keep_ref.shape[0] // blocks
    for at in range(blocks):
        place = slice(at * shard, (at + 1) * shard)
        ref = send_refs[at - 1] if at > 0 else own_ref
        total = keep_ref[place, :] + came_ref[place, :].astype(F32)
        for slab in range(keep_ref.shape[1] // size):
            ref[slab * shard:(slab + 1) * shard, :] = total[:, slab * size:(slab + 1) * size].astype(ref.dtype)
        ref[ref.shape[0] - TAIL:, :] = tail.astype(ref.dtype)


def add(keep, came, terms, blocks):
    size = terms[0].shape[1]
    shape = (keep.size // blocks // size + TAIL, size)
    return pl.pallas_call(
        functools.partial(add_kernel, terms=len(terms)),
        in_specs=[VMEM_SPEC] * (2 + len(terms)),
        out_specs=[VMEM_SPEC] * blocks,
        out_shape=[jax.ShapeDtypeStruct(shape, F32)] + [jax.ShapeDtypeStruct(shape, BF16)] * (blocks - 1),
        compiler_params=params(),
        name="add",
    )(keep, came, *terms)


def chips_kernel(*refs):
    parts = [gain_term(ref[ref.shape[0] - TAIL:, :]) for ref in refs[:-1]]
    total = tree(parts[:1] + parts[:0:-1])
    refs[-1][...] = jnp.broadcast_to(total, refs[-1].shape)


def sum_chips(blocks):
    return pl.pallas_call(
        chips_kernel,
        in_specs=[VMEM_SPEC] * len(blocks),
        out_specs=VMEM_SPEC,
        out_shape=jax.ShapeDtypeStruct((8, blocks[0].shape[1]), F32),
        compiler_params=params(),
        name="sum_chips",
    )(*blocks)


def last_kernel(*refs):
    terms, (qg_ref, kg_ref, query_ref, key_ref) = refs[:-4], refs[-4:]
    total = tree([ref[0:1, :] for ref in terms])
    query_ref[...] = total / qg_ref[...]
    key_ref[...] = total / kg_ref[...]


def gain_grads(terms, query_gain, key_gain):
    row = jax.ShapeDtypeStruct(query_gain.shape, F32)
    return pl.pallas_call(
        last_kernel,
        in_specs=[VMEM_SPEC] * (len(terms) + 2),
        out_specs=[VMEM_SPEC] * 2,
        out_shape=[row, row],
        compiler_params=params(),
        name="gain_grads",
    )(*terms, query_gain, key_gain)


def finish_kernel(*refs):
    parts, (raw_ref, kg_ref, key_ref, value_ref) = refs[:-4], refs[-4:]
    size = kg_ref.shape[1]
    shard, width = raw_ref.shape
    heads = width // size
    for slab in range(2 * heads):
        rows = slice(slab * shard, (slab + 1) * shard)
        total = parts[0][rows, :]
        for ref in parts[1:]:
            total = total + ref[rows, :].astype(F32)
        columns = slice(slab % heads * size, (slab % heads + 1) * size)
        if slab < heads:
            unit_rows, recip = unit(raw_ref[:, columns].astype(F32))
            key_ref[:, columns] = norm_back(total, unit_rows, recip, kg_ref[...])
        else:
            value_ref[:, columns] = total


def finish(blocks, raw, key_gain):
    shape = jax.ShapeDtypeStruct(raw.shape, F32)
    return pl.pallas_call(
        finish_kernel,
        in_specs=[VMEM_SPEC] * (len(blocks) + 2),
        out_specs=[VMEM_SPEC] * 2,
        out_shape=[shape, shape],
        compiler_params=params(),
        cost_estimate=cost(10**8, 10**6),
        name="finish",
    )(*blocks, raw, key_gain)


def swap(values, axis, step):
    return lax.ppermute(values, axis, [(i, i ^ step) for i in range(lax.axis_size(axis))])


def local(
    comp_queries, comp_keys, comp_values, prompt_keys, prompt_values,
    query_gain, key_gain, out_grad, live_counts, slot_prompts,
):
    grp, tp = lax.axis_size("grp"), lax.axis_size("tp")
    shard = prompt_keys.shape[0]
    size = query_gain.shape[0]
    by_permute = shard % 16 == 0 and grp > 1 and grp & (grp - 1) == 0 and tp & (tp - 1) == 0
    slots, width = slot_prompts.shape[0], comp_keys.shape[1]
    query_gain, key_gain = query_gain.reshape(1, size), key_gain.reshape(1, size)
    me = lax.axis_index("grp").astype(jnp.int32).reshape(1) if by_permute else jnp.zeros((1,), jnp.int32)
    mask, me, keys_in, values_in = lax.optimization_barrier((causal(), me, prompt_keys, prompt_values))
    mine = pack(keys_in, values_in, key_gain)
    raw, recip, queries, grads, query_col = prepare(live_counts, comp_queries, out_grad, query_gain, slots, width)
    if by_permute:
        even = [mine] + [swap(mine, "grp", step) for step in range(2, grp, 2)]
        odd = [swap(mine, "grp", 1)]
        for at in range(1, len(even)):
            even[at], query_col = lax.optimization_barrier((even[at], query_col))
            odd.append(swap(even[at], "grp", 1))
        pieces = [piece for pair in zip(even, odd) for piece in pair]
    else:
        pieces = [lax.all_gather(mine, "grp", axis=0, tiled=True)]
    att_t, score_grads, pool_keys, own_keys, own_acc, term, keep, *send = attention(
        live_counts, slot_prompts, me, queries, grads, comp_keys, comp_values, key_gain, mask, pieces,
    )
    attended, key_grads, value_grads = turn(live_counts, att_t, own_acc, comp_keys, key_gain, comp_queries.shape)
    query_grads = post(
        live_counts, slot_prompts, score_grads, pool_keys, own_keys, raw, recip, query_col, comp_queries.shape,
    )
    if by_permute:
        came = swap(send[0], "grp", 1)
        terms = [term] + [swap(term, "tp", step) for step in range(1, tp)]
        terms, attended = lax.optimization_barrier((terms, attended))
        own, *blocks = add(keep, came, terms, grp // 2)
        blocks = [swap(block, "grp", 2 * at + 2) for at, block in enumerate(blocks)]
        blocks, query_grads = lax.optimization_barrier((blocks, query_grads))
        blocks = [own] + blocks[::-1]
        total = sum_chips(blocks)
        terms = [total, swap(total, "grp", 1)]
    else:
        block = lax.psum_scatter(keep, "grp", scatter_dimension=0, tiled=True)
        blocks = [jnp.concatenate([block[:, at:at + size] for at in range(0, 2 * width, size)], axis=0)]
        terms = [lax.psum(term, ("grp", "tp"))]
    prompt_key_grads, prompt_value_grads = finish(blocks, prompt_keys, key_gain)
    query_gain_grad, key_gain_grad = gain_grads(terms, query_gain, key_gain)
    return (
        attended, query_grads, key_grads, value_grads, prompt_key_grads, prompt_value_grads,
        query_gain_grad.reshape(size), key_gain_grad.reshape(size),
    )


def solution(mesh):
    split, whole = P("grp", "tp"), P()
    return jax.shard_map(
        local,
        mesh=mesh,
        in_specs=(split, split, split, split, split, whole, whole, split, P("grp"), P("grp")),
        out_specs=(split, split, split, split, split, split, whole, whole),
        check_vma=False,
    )
```

```python
import functools
import math

import jax
import jax.numpy as jnp
from jax import lax
from jax.experimental import pallas as pl
from jax.experimental.pallas import tpu as pltpu
from jax.sharding import PartitionSpec as P

PL = 384
CL = 64
EPS = 1e-06
TAIL = 16
CHUNK = 512
VMEM_LIMIT = 24 * 1024 * 1024
F32 = jnp.float32
BF16 = jnp.bfloat16
SMEM_SPEC = pl.BlockSpec(memory_space=pltpu.SMEM)
VMEM_SPEC = pl.BlockSpec(memory_space=pltpu.VMEM)
HBM_SPEC = pl.BlockSpec(memory_space=pltpu.HBM)


def dot(left, right):
    return jnp.dot(left, right, preferred_element_type=F32)


def dot_nt(left, right):
    return lax.dot_general(left, right, (((1,), (1,)), ((), ())), preferred_element_type=F32)


def unit(raw):
    recip = lax.rsqrt(jnp.mean(raw * raw, axis=-1, keepdims=True) + EPS)
    return raw * recip, recip


def norm_back(upstream, unit_rows, recip, gain):
    scaled = upstream * gain
    return recip * (scaled - unit_rows * jnp.mean(unit_rows * scaled, axis=-1, keepdims=True))


def gain_rows(term):
    upper = term.astype(BF16).astype(F32)
    rows = jnp.concatenate([upper, term - upper, jnp.zeros((TAIL - 2, term.shape[1]), F32)], axis=0)
    return rows.astype(BF16)


def gain_term(rows):
    return rows[0:1].astype(F32) + rows[1:2].astype(F32)


def params(limit=VMEM_LIMIT):
    return pltpu.CompilerParams(vmem_limit_bytes=limit)


def cost(flops, size):
    return pl.CostEstimate(flops=flops, bytes_accessed=size, transcendentals=0)


def causal_kernel(mask_ref):
    key_no = lax.broadcasted_iota(jnp.int32, mask_ref.shape, 0)
    token_no = lax.broadcasted_iota(jnp.int32, mask_ref.shape, 1) % CL
    mask_ref[...] = jnp.where(key_no <= token_no, 0.0, -jnp.inf)


def causal():
    return pl.pallas_call(
        causal_kernel,
        out_specs=VMEM_SPEC,
        out_shape=jax.ShapeDtypeStruct((CL, CHUNK), F32),
        compiler_params=params(),
        cost_estimate=cost(4 * 10**9, 10**6),
        name="causal",
    )()


def pack_kernel(keys_ref, values_ref, kg_ref, out_ref):
    size, width = kg_ref.shape[1], keys_ref.shape[1]
    for head in range(width // size):
        columns = slice(head * size, (head + 1) * size)
        unit_rows, _ = unit(keys_ref[:, columns].astype(F32))
        out_ref[:, columns] = (unit_rows * kg_ref[...]).astype(BF16)
    out_ref[:, width:] = values_ref[...]


def pack(keys, values, key_gain):
    return pl.pallas_call(
        pack_kernel,
        in_specs=[VMEM_SPEC] * 3,
        out_specs=VMEM_SPEC,
        out_shape=jax.ShapeDtypeStruct((keys.shape[0], 2 * keys.shape[1]), BF16),
        compiler_params=params(),
        cost_estimate=cost(4 * 10**9, 10**6),
        name="pack",
    )(keys, values, key_gain)


def head_columns(head, group, size):
    return [slice((head * group + g) * size, (head * group + g + 1) * size) for g in range(group)]


def slot_rows(slot):
    return pl.ds(pl.multiple_of(slot * CL, CL), CL)


def prepare_kernel(live_ref, q_ref, do_ref, qg_ref, raw_ref, recip_ref, queries_ref, grads_ref, col_ref):
    size = col_ref.shape[0]
    heads = raw_ref.shape[1] // size
    group = q_ref.shape[1] // raw_ref.shape[1]
    column = jnp.broadcast_to(qg_ref[...], (size, size)).T
    for at in range(0, col_ref.shape[1], size):
        col_ref[:, at:at + size] = column

    def live(slot, carry):
        for head in range(heads):
            places = head_columns(head, group, size)
            rows = slice(head * size, (head + 1) * size)
            half = jnp.concatenate([q_ref[slot_rows(slot), place] for place in places], axis=0).T
            raw_ref[slot, rows, :] = half
            raw = half.astype(F32)
            recip = lax.rsqrt(jnp.mean(raw * raw, axis=0, keepdims=True) + EPS)
            recip_ref[slot, head:head + 1, :] = recip
            queries_ref[slot, rows, :] = (raw * recip * col_ref[...]).astype(BF16)
            grads_ref[slot, rows, :] = jnp.concatenate([do_ref[slot_rows(slot), place] for place in places], axis=0).T
        return carry

    lax.fori_loop(0, live_ref[0], live, 0)


def prepare(live_counts, queries, out_grad, query_gain, slots, width):
    size = query_gain.shape[1]
    lanes = queries.shape[1] // width * CL
    turned = jax.ShapeDtypeStruct((slots, width, lanes), BF16)
    return pl.pallas_call(
        prepare_kernel,
        in_specs=[SMEM_SPEC] + [VMEM_SPEC] * 3,
        out_specs=[VMEM_SPEC] * 5,
        out_shape=[
            turned, jax.ShapeDtypeStruct((slots, 8, lanes), F32), turned, turned,
            jax.ShapeDtypeStruct((size, lanes), F32),
        ],
        compiler_params=params(),
        cost_estimate=cost(2 * 10**9, 6 * queries.size),
        name="prepare",
    )(live_counts, queries, out_grad, query_gain)


def attention_kernel(*refs, parts, heads):
    live_ref, prompt_ref, me_ref, queries_ref, grads_ref, ck_ref, cv_ref, kg_ref, mask_ref = refs[:9]
    pieces, refs = refs[9:9 + parts], refs[9 + parts:]
    att_ref, ds_ref, pool_keys, own_keys, own_acc, term_ref, keep_ref = refs[:7]
    send_ref, refs = (refs[7], refs[8:]) if parts > 1 else (None, refs[7:])
    acc, pool_values, pool_values_t, own_values_t = refs[:4]
    size = kg_ref.shape[1]
    width = heads * size
    slots, _, lanes = queries_ref.shape
    per_head = lanes // CHUNK
    count = heads * per_head
    weights, grads = refs[4:4 + heads], refs[4 + heads:4 + 2 * heads]
    scores, summed = refs[4 + 2 * heads:4 + 2 * heads + count], refs[4 + 2 * heads + count:]
    score_scale = 1.0 / math.sqrt(size)
    shard = pieces[0].shape[0]

    def columns(head):
        return slice(head * size, (head + 1) * size)

    def piece_rows(piece_no):
        return pl.ds(pl.multiple_of((me_ref[0] ^ piece_no) * shard, shard), shard)

    acc[...] = jnp.zeros_like(acc)
    own_acc[...] = jnp.zeros_like(own_acc)
    for piece_no, piece in enumerate(pieces):
        pool_keys[piece_rows(piece_no), :] = piece[:, :width]
        pool_values[piece_rows(piece_no), :] = piece[:, width:]
    for head in range(heads):
        pool_values_t[columns(head), :] = pool_values[:, columns(head)].T
        own_unit, _ = unit(ck_ref[:, columns(head)].astype(F32))
        own_keys[:, columns(head)] = (own_unit * kg_ref[...]).astype(BF16)
        for slot in range(slots):
            own_values_t[slot, head] = cv_ref[slot * CL:(slot + 1) * CL, columns(head)].T

    def prompt_rows(slot):
        return pl.ds(pl.multiple_of(prompt_ref[slot] * PL, PL), PL)

    def part(no):
        head = no // per_head
        return head, columns(head), slice(no % per_head * CHUNK, (no % per_head + 1) * CHUNK)

    def begin(slot, no):
        _, place, span = part(no)
        keys = jnp.concatenate([pool_keys[prompt_rows(slot), place], own_keys[slot_rows(slot), place]], axis=0)
        scores[no][...] = dot(keys, queries_ref[slot, place, span])

    def weigh(slot, no):
        head, place, span = part(no)
        prompt, own = scores[no][:PL, :], scores[no][PL:, :] + mask_ref[...]
        factor = score_scale * math.log2(math.e)
        high = jnp.maximum(jnp.max(prompt, axis=0, keepdims=True), jnp.max(own, axis=0, keepdims=True))
        both = jnp.concatenate([prompt, own], axis=0)
        half = jnp.exp2((both - high) * factor).astype(BF16)
        weights[head][:, span] = half
        values_t = jnp.concatenate([pool_values_t[place, prompt_rows(slot)], own_values_t[slot, head]], axis=1)
        values_t = jnp.concatenate([values_t, jnp.ones((TAIL, PL + CL), BF16)], axis=0)
        summed[no][...] = dot(values_t, half)

    def back(slot, no):
        head, place, span = part(no)
        inverse = 1.0 / summed[no][size:size + 1, :]
        attended = (summed[no][:size, :] * inverse).astype(BF16)
        att_ref[slot, place, span] = attended
        scaled = (grads_ref[slot, place, span].astype(F32) * inverse).astype(BF16)
        grads[head][:, span] = scaled
        delta = jnp.sum(scaled.astype(F32) * attended.astype(F32), axis=0, keepdims=True)
        values = jnp.concatenate([pool_values[prompt_rows(slot), place], cv_ref[slot_rows(slot), place]], axis=0)
        score_grad = weights[head][:, span].astype(F32) * (dot(values, scaled) - delta)
        ds_ref[slot, head, :, span] = score_grad.astype(BF16)

    def close(slot, head):
        value_grad = dot_nt(weights[head][...], grads[head][...])
        key_grad = dot_nt(ds_ref[slot, head], queries_ref[slot, columns(head), :])
        acc[prompt_rows(slot), columns(head)] += key_grad[:PL]
        acc[prompt_rows(slot), width + head * size:width + (head + 1) * size] += value_grad[:PL]
        own_acc[slot, head, 0] = key_grad[PL:]
        own_acc[slot, head, 1] = value_grad[PL:]

    def ticks(now, before):
        for tick in range(count):
            if now is not None:
                begin(now, tick)
            for number, stage in ((1, weigh), (2, back)):
                slot = now if tick >= number else before
                if slot is not None:
                    stage(slot, (tick - number) % count)
            wait = 3 if per_head > 1 else 2
            done = (tick - wait) % count
            slot = now if tick >= wait else before
            if slot is not None and done % per_head == per_head - 1:
                close(slot, done // per_head)

    def step(slot, carry):
        ticks(slot, slot - 1)
        return carry

    ticks(0, None)
    lax.fori_loop(1, live_ref[0], step, 0)
    ticks(None, live_ref[0] - 1)

    total = jnp.zeros((1, size), F32)
    for head in range(heads):
        own_grad = own_acc[:, head, 0].reshape(slots * CL, size)
        total = total + jnp.sum(own_grad * own_keys[:, columns(head)].astype(F32), axis=0, keepdims=True)
        pool_term = acc[:, columns(head)] * pool_keys[:, columns(head)].astype(F32)
        total = total + jnp.sum(pool_term, axis=0, keepdims=True)
    term_ref[...] = jnp.broadcast_to(total * score_scale, term_ref.shape)
    if parts == 1:
        keep_ref[:, :width] = acc[:, :width] * score_scale
        keep_ref[:, width:] = acc[:, width:]
    else:
        for piece_no in range(parts):
            place = slice(piece_no // 2 * shard, (piece_no // 2 + 1) * shard)
            ref = keep_ref if piece_no % 2 == 0 else send_ref
            ref[place, :width] = (acc[piece_rows(piece_no), :width] * score_scale).astype(ref.dtype)
            ref[place, width:] = acc[piece_rows(piece_no), width:].astype(ref.dtype)


def attention(live_counts, slot_prompts, me, queries, grads, keys, values, key_gain, mask, pieces):
    size = key_gain.shape[1]
    slots, width, lanes = queries.shape
    heads = width // size
    parts = len(pieces)
    pool_rows = parts * pieces[0].shape[0]
    count = heads * lanes // CHUNK
    span = PL + CL
    out_shape = [
        jax.ShapeDtypeStruct(queries.shape, BF16),
        jax.ShapeDtypeStruct((slots, heads, span, lanes), BF16),
        jax.ShapeDtypeStruct((pool_rows, width), BF16),
        jax.ShapeDtypeStruct(keys.shape, BF16),
        jax.ShapeDtypeStruct((slots, heads, 2, CL, size), F32),
        jax.ShapeDtypeStruct((8, size), F32),
    ]
    if parts > 1:
        half = (pool_rows // 2, 2 * width)
        out_shape += [jax.ShapeDtypeStruct(half, F32), jax.ShapeDtypeStruct(half, BF16)]
    else:
        out_shape += [jax.ShapeDtypeStruct((pool_rows, 2 * width), F32)]
    return pl.pallas_call(
        functools.partial(attention_kernel, parts=parts, heads=heads),
        in_specs=[SMEM_SPEC] * 3 + [VMEM_SPEC] * (6 + parts),
        out_specs=[VMEM_SPEC] * len(out_shape),
        out_shape=out_shape,
        scratch_shapes=[
            pltpu.VMEM((pool_rows, 2 * width), F32),
            pltpu.VMEM((pool_rows, width), BF16),
            pltpu.VMEM((width, pool_rows), BF16),
            pltpu.VMEM((slots, heads, size, CL), BF16),
        ]
        + [pltpu.VMEM((span, lanes), BF16)] * heads
        + [pltpu.VMEM((size, lanes), BF16)] * heads
        + [pltpu.VMEM((span, CHUNK), F32)] * count
        + [pltpu.VMEM((size + TAIL, CHUNK), F32)] * count,
        compiler_params=params(),
        cost_estimate=cost(3 * 10**9, 10**7),
        name="attention",
    )(live_counts, slot_prompts, me, queries, grads, keys, values, key_gain, mask, *pieces)


def copy_slots(live_ref, zeros, out, target, sems):
    slots = out.shape[0]

    def copy(source, slot):
        return pltpu.make_async_copy(source, target.at[slot_rows(slot), :], sems.at[slot])

    def dead(slot, carry):
        copy(zeros, slot).start()
        return carry

    def wait():
        for slot in range(slots):
            copy(zeros, slot).wait()

    zeros[...] = jnp.zeros_like(zeros)
    lax.fori_loop(live_ref[0], slots, dead, 0)
    return lambda slot: copy(out.at[slot], slot).start(), wait


def turn_kernel(
    live_ref, att_t_ref, own_acc, ck_ref, kg_ref, att_ref, dk_ref, dv_ref, att_out, zeros, dk_out, dv_out, sems, own_sems,
):
    slots, width, _ = att_t_ref.shape
    size = kg_ref.shape[1]
    heads = width // size
    group = att_ref.shape[1] // width
    start, wait = copy_slots(live_ref, zeros, att_out, att_ref, sems)

    def live(slot, carry):
        for head in range(heads):
            attended = att_t_ref[slot, head * size:(head + 1) * size, :].T
            for g, place in enumerate(head_columns(head, group, size)):
                att_out[slot, :, place] = attended[g * CL:(g + 1) * CL]
        start(slot)
        return carry

    lax.fori_loop(0, live_ref[0], live, 0)
    for head in range(heads):
        columns = slice(head * size, (head + 1) * size)
        own_grad = own_acc[:, head, 0].reshape(slots * CL, size) * (1.0 / math.sqrt(size))
        own_unit, own_recip = unit(ck_ref[:, columns].astype(F32))
        dk_out[:, columns] = norm_back(own_grad, own_unit, own_recip, kg_ref[...]).astype(BF16)
        dv_out[:, columns] = own_acc[:, head, 1].reshape(slots * CL, size).astype(BF16)
    own_copies = [
        pltpu.make_async_copy(dk_out, dk_ref, own_sems.at[0]),
        pltpu.make_async_copy(dv_out, dv_ref, own_sems.at[1]),
    ]
    for copy in own_copies:
        copy.start()
    for copy in own_copies:
        copy.wait()
    wait()


def turn(live_counts, att_t, own_acc, keys, key_gain, shape):
    slots = att_t.shape[0]
    own = jax.ShapeDtypeStruct(keys.shape, BF16)
    own_slab = pltpu.VMEM(keys.shape, BF16)
    return pl.pallas_call(
        turn_kernel,
        in_specs=[SMEM_SPEC] + [VMEM_SPEC] * 4,
        out_specs=[HBM_SPEC] * 3,
        out_shape=[jax.ShapeDtypeStruct(shape, BF16), own, own],
        scratch_shapes=[
            pltpu.VMEM((slots, CL, shape[1]), BF16), pltpu.VMEM((CL, shape[1]), BF16), own_slab, own_slab,
            pltpu.SemaphoreType.DMA((slots,)), pltpu.SemaphoreType.DMA((2,)),
        ],
        compiler_params=params(),
        cost_estimate=cost(2 * 10**9, 2 * 10**6),
        name="turn",
    )(live_counts, att_t, own_acc, keys, key_gain)


def post_kernel(
    live_ref, prompt_ref, ds_ref, pool_keys, own_keys_ref, raw_ref, recip_ref, col_ref, dq_ref, dq_out, zeros, sems,
):
    slots, width, lanes = raw_ref.shape
    size = col_ref.shape[0]
    heads = width // size
    group = dq_ref.shape[1] // width
    score_scale = 1.0 / math.sqrt(size)
    start, wait = copy_slots(live_ref, zeros, dq_out, dq_ref, sems)

    def live(slot, carry):
        rows = pl.ds(pl.multiple_of(prompt_ref[slot] * PL, PL), PL)
        for head in range(heads):
            columns = slice(head * size, (head + 1) * size)
            keys_t = jnp.concatenate([pool_keys[rows, columns], own_keys_ref[slot_rows(slot), columns]], axis=0).T
            query_grad = dot(keys_t, ds_ref[slot, head]) * score_scale
            recip = recip_ref[slot, head:head + 1, :]
            query_unit = raw_ref[slot, columns, :].astype(F32) * recip
            scaled = query_grad * col_ref[...]
            mean = jnp.mean(query_unit * scaled, axis=0, keepdims=True)
            query_out = (recip * (scaled - query_unit * mean)).astype(BF16).T
            for g, place in enumerate(head_columns(head, group, size)):
                dq_out[slot, :, place] = query_out[g * CL:(g + 1) * CL]
        start(slot)
        return carry

    lax.fori_loop(0, live_ref[0], live, 0)
    wait()


def post(live_counts, slot_prompts, score_grads, pool_keys, own_keys, raw, recip, query_col, shape):
    slots = raw.shape[0]
    return pl.pallas_call(
        post_kernel,
        in_specs=[SMEM_SPEC] * 2 + [VMEM_SPEC] * 6,
        out_specs=HBM_SPEC,
        out_shape=jax.ShapeDtypeStruct(shape, BF16),
        scratch_shapes=[
            pltpu.VMEM((slots, CL, shape[1]), BF16), pltpu.VMEM((CL, shape[1]), BF16),
            pltpu.SemaphoreType.DMA((slots,)),
        ],
        compiler_params=params(),
        cost_estimate=cost(3 * 10**9, 4 * 10**6),
        name="post",
    )(live_counts, slot_prompts, score_grads, pool_keys, own_keys, raw, recip, query_col)


def tree(terms):
    while len(terms) > 1:
        terms = [left + right for left, right in zip(terms[::2], terms[1::2])]
    return terms[0]


def add_kernel(keep_ref, came_ref, *refs, terms):
    tail = gain_rows(tree([ref[0:1, :] for ref in refs[:terms]]))
    size = tail.shape[1]
    own_ref, send_refs = refs[terms], refs[terms + 1:]
    blocks = len(send_refs) + 1
    shard = keep_ref.shape[0] // blocks
    for at in range(blocks):
        place = slice(at * shard, (at + 1) * shard)
        ref = send_refs[blocks - 1 - at] if at > 0 else own_ref
        total = keep_ref[place, :] + came_ref[place, :].astype(F32)
        for slab in range(keep_ref.shape[1] // size):
            ref[slab * shard:(slab + 1) * shard, :] = total[:, slab * size:(slab + 1) * size].astype(ref.dtype)
        ref[ref.shape[0] - TAIL:, :] = tail.astype(ref.dtype)


def add(keep, came, terms, blocks):
    size = terms[0].shape[1]
    shape = (keep.size // blocks // size + TAIL, size)
    return pl.pallas_call(
        functools.partial(add_kernel, terms=len(terms)),
        in_specs=[VMEM_SPEC] * (2 + len(terms)),
        out_specs=[VMEM_SPEC] * blocks,
        out_shape=[jax.ShapeDtypeStruct(shape, F32)] + [jax.ShapeDtypeStruct(shape, BF16)] * (blocks - 1),
        compiler_params=params(),
        name="add",
    )(keep, came, *terms)


def chips_kernel(*refs):
    parts = [gain_term(ref[ref.shape[0] - TAIL:, :]) for ref in refs[:-1]]
    total = tree(parts[:1] + parts[:0:-1])
    refs[-1][...] = jnp.broadcast_to(total, refs[-1].shape)


def sum_chips(blocks):
    return pl.pallas_call(
        chips_kernel,
        in_specs=[VMEM_SPEC] * len(blocks),
        out_specs=VMEM_SPEC,
        out_shape=jax.ShapeDtypeStruct((8, blocks[0].shape[1]), F32),
        compiler_params=params(),
        name="sum_chips",
    )(*blocks)


def last_kernel(*refs):
    terms, (qg_ref, kg_ref, query_ref, key_ref) = refs[:-4], refs[-4:]
    total = tree([ref[0:1, :] for ref in terms])
    query_ref[...] = total / qg_ref[...]
    key_ref[...] = total / kg_ref[...]


def gain_grads(terms, query_gain, key_gain):
    row = jax.ShapeDtypeStruct(query_gain.shape, F32)
    return pl.pallas_call(
        last_kernel,
        in_specs=[VMEM_SPEC] * (len(terms) + 2),
        out_specs=[VMEM_SPEC] * 2,
        out_shape=[row, row],
        compiler_params=params(),
        name="gain_grads",
    )(*terms, query_gain, key_gain)


def finish_kernel(*refs):
    parts, (raw_ref, kg_ref, key_ref, value_ref) = refs[:-4], refs[-4:]
    size = kg_ref.shape[1]
    shard, width = raw_ref.shape
    heads = width // size
    for slab in range(2 * heads):
        rows = slice(slab * shard, (slab + 1) * shard)
        total = parts[0][rows, :]
        for ref in parts[1:]:
            total = total + ref[rows, :].astype(F32)
        columns = slice(slab % heads * size, (slab % heads + 1) * size)
        if slab < heads:
            unit_rows, recip = unit(raw_ref[:, columns].astype(F32))
            key_ref[:, columns] = norm_back(total, unit_rows, recip, kg_ref[...])
        else:
            value_ref[:, columns] = total


def finish(blocks, raw, key_gain):
    shape = jax.ShapeDtypeStruct(raw.shape, F32)
    return pl.pallas_call(
        finish_kernel,
        in_specs=[VMEM_SPEC] * (len(blocks) + 2),
        out_specs=[VMEM_SPEC] * 2,
        out_shape=[shape, shape],
        compiler_params=params(),
        cost_estimate=cost(10**8, 10**6),
        name="finish",
    )(*blocks, raw, key_gain)


def swap(values, axis, step):
    return lax.ppermute(values, axis, [(i, i ^ step) for i in range(lax.axis_size(axis))])


def local(
    comp_queries, comp_keys, comp_values, prompt_keys, prompt_values,
    query_gain, key_gain, out_grad, live_counts, slot_prompts,
):
    grp, tp = lax.axis_size("grp"), lax.axis_size("tp")
    shard = prompt_keys.shape[0]
    size = query_gain.shape[0]
    by_permute = shard % 16 == 0 and grp > 1 and grp & (grp - 1) == 0 and tp & (tp - 1) == 0
    slots, width = slot_prompts.shape[0], comp_keys.shape[1]
    query_gain, key_gain = query_gain.reshape(1, size), key_gain.reshape(1, size)
    me = lax.axis_index("grp").astype(jnp.int32).reshape(1) if by_permute else jnp.zeros((1,), jnp.int32)
    mask, me, keys_in, values_in = lax.optimization_barrier((causal(), me, prompt_keys, prompt_values))
    mine = pack(keys_in, values_in, key_gain)
    raw, recip, queries, grads, query_col = prepare(live_counts, comp_queries, out_grad, query_gain, slots, width)
    if by_permute:
        even = [mine] + [swap(mine, "grp", step) for step in range(2, grp, 2)]
        odd = [swap(mine, "grp", 1)]
        for at in range(1, len(even)):
            even[at], query_col = lax.optimization_barrier((even[at], query_col))
            odd.append(swap(even[at], "grp", 1))
        pieces = [piece for pair in zip(even, odd) for piece in pair]
    else:
        pieces = [lax.all_gather(mine, "grp", axis=0, tiled=True)]
    att_t, score_grads, pool_keys, own_keys, own_acc, term, keep, *send = attention(
        live_counts, slot_prompts, me, queries, grads, comp_keys, comp_values, key_gain, mask, pieces,
    )
    attended, key_grads, value_grads = turn(live_counts, att_t, own_acc, comp_keys, key_gain, comp_queries.shape)
    query_grads = post(
        live_counts, slot_prompts, score_grads, pool_keys, own_keys, raw, recip, query_col, comp_queries.shape,
    )
    if by_permute:
        came = swap(send[0], "grp", 1)
        terms = [term] + [swap(term, "tp", step) for step in range(1, tp)]
        terms, attended = lax.optimization_barrier((terms, attended))
        own, *blocks = add(keep, came, terms, grp // 2)
        blocks = [swap(block, "grp", grp - 2 - 2 * at) for at, block in enumerate(blocks)]
        blocks, query_grads = lax.optimization_barrier((blocks, query_grads))
        blocks = [own] + blocks
        total = sum_chips(blocks)
        terms = [total, swap(total, "grp", 1)]
    else:
        block = lax.psum_scatter(keep, "grp", scatter_dimension=0, tiled=True)
        blocks = [jnp.concatenate([block[:, at:at + size] for at in range(0, 2 * width, size)], axis=0)]
        terms = [lax.psum(term, ("grp", "tp"))]
    prompt_key_grads, prompt_value_grads = finish(blocks, prompt_keys, key_gain)
    query_gain_grad, key_gain_grad = gain_grads(terms, query_gain, key_gain)
    return (
        attended, query_grads, key_grads, value_grads, prompt_key_grads, prompt_value_grads,
        query_gain_grad.reshape(size), key_gain_grad.reshape(size),
    )


def solution(mesh):
    split, whole = P("grp", "tp"), P()
    return jax.shard_map(
        local,
        mesh=mesh,
        in_specs=(split, split, split, split, split, whole, whole, split, P("grp"), P("grp")),
        out_specs=(split, split, split, split, split, split, whole, whole),
        check_vma=False,
    )
```

```python
import functools
import math

import jax
import jax.numpy as jnp
from jax import lax
from jax.experimental import pallas as pl
from jax.experimental.pallas import tpu as pltpu
from jax.sharding import PartitionSpec as P

PL = 384
CL = 64
EPS = 1e-06
TAIL = 16
CHUNK = 512
VMEM_LIMIT = 24 * 1024 * 1024
F32 = jnp.float32
BF16 = jnp.bfloat16
SMEM_SPEC = pl.BlockSpec(memory_space=pltpu.SMEM)
VMEM_SPEC = pl.BlockSpec(memory_space=pltpu.VMEM)
HBM_SPEC = pl.BlockSpec(memory_space=pltpu.HBM)


def dot(left, right):
    return jnp.dot(left, right, preferred_element_type=F32)


def dot_nt(left, right):
    return lax.dot_general(left, right, (((1,), (1,)), ((), ())), preferred_element_type=F32)


def unit(raw):
    recip = lax.rsqrt(jnp.mean(raw * raw, axis=-1, keepdims=True) + EPS)
    return raw * recip, recip


def norm_back(upstream, unit_rows, recip, gain):
    scaled = upstream * gain
    return recip * (scaled - unit_rows * jnp.mean(unit_rows * scaled, axis=-1, keepdims=True))


def gain_rows(term):
    upper = term.astype(BF16).astype(F32)
    rows = jnp.concatenate([upper, term - upper, jnp.zeros((TAIL - 2, term.shape[1]), F32)], axis=0)
    return rows.astype(BF16)


def gain_term(rows):
    return rows[0:1].astype(F32) + rows[1:2].astype(F32)


def params(limit=VMEM_LIMIT):
    return pltpu.CompilerParams(vmem_limit_bytes=limit)


def cost(flops, size):
    return pl.CostEstimate(flops=flops, bytes_accessed=size, transcendentals=0)


def causal_kernel(mask_ref):
    key_no = lax.broadcasted_iota(jnp.int32, mask_ref.shape, 0)
    token_no = lax.broadcasted_iota(jnp.int32, mask_ref.shape, 1) % CL
    mask_ref[...] = jnp.where(key_no <= token_no, 0.0, -jnp.inf)


def causal():
    return pl.pallas_call(
        causal_kernel,
        out_specs=VMEM_SPEC,
        out_shape=jax.ShapeDtypeStruct((CL, CHUNK), F32),
        compiler_params=params(),
        cost_estimate=cost(4 * 10**9, 10**6),
        name="causal",
    )()


def pack_kernel(keys_ref, values_ref, kg_ref, out_ref):
    size, width = kg_ref.shape[1], keys_ref.shape[1]
    for head in range(width // size):
        columns = slice(head * size, (head + 1) * size)
        unit_rows, _ = unit(keys_ref[:, columns].astype(F32))
        out_ref[:, columns] = (unit_rows * kg_ref[...]).astype(BF16)
    out_ref[:, width:] = values_ref[...]


def pack(keys, values, key_gain):
    return pl.pallas_call(
        pack_kernel,
        in_specs=[VMEM_SPEC] * 3,
        out_specs=VMEM_SPEC,
        out_shape=jax.ShapeDtypeStruct((keys.shape[0], 2 * keys.shape[1]), BF16),
        compiler_params=params(),
        cost_estimate=cost(4 * 10**9, 10**6),
        name="pack",
    )(keys, values, key_gain)


def head_columns(head, group, size):
    return [slice((head * group + g) * size, (head * group + g + 1) * size) for g in range(group)]


def slot_rows(slot):
    return pl.ds(pl.multiple_of(slot * CL, CL), CL)


def prepare_kernel(live_ref, q_ref, do_ref, qg_ref, raw_ref, recip_ref, queries_ref, grads_ref, col_ref, rows_ref):
    size = col_ref.shape[0]
    heads = raw_ref.shape[1] // size
    group = q_ref.shape[1] // raw_ref.shape[1]
    column = jnp.broadcast_to(qg_ref[...], (size, size)).T
    for at in range(0, col_ref.shape[1], size):
        col_ref[:, at:at + size] = column

    def live(slot, carry):
        for head in range(heads):
            places = head_columns(head, group, size)
            rows = slice(head * size, (head + 1) * size)
            half = jnp.concatenate([q_ref[slot_rows(slot), place] for place in places], axis=0).T
            raw_ref[slot, rows, :] = half
            raw = half.astype(F32)
            recip = lax.rsqrt(jnp.mean(raw * raw, axis=0, keepdims=True) + EPS)
            recip_ref[slot, head:head + 1, :] = recip
            queries = (raw * recip * col_ref[...]).astype(BF16)
            queries_ref[slot, rows, :] = queries
            rows_ref[slot, head] = queries.T
            grads_ref[slot, rows, :] = jnp.concatenate([do_ref[slot_rows(slot), place] for place in places], axis=0).T
        return carry

    lax.fori_loop(0, live_ref[0], live, 0)


def prepare(live_counts, queries, out_grad, query_gain, slots, width):
    size = query_gain.shape[1]
    lanes = queries.shape[1] // width * CL
    turned = jax.ShapeDtypeStruct((slots, width, lanes), BF16)
    return pl.pallas_call(
        prepare_kernel,
        in_specs=[SMEM_SPEC] + [VMEM_SPEC] * 3,
        out_specs=[VMEM_SPEC] * 6,
        out_shape=[
            turned, jax.ShapeDtypeStruct((slots, 8, lanes), F32), turned, turned,
            jax.ShapeDtypeStruct((size, lanes), F32),
            jax.ShapeDtypeStruct((slots, width // size, lanes, size), BF16),
        ],
        compiler_params=params(),
        cost_estimate=cost(2 * 10**9, 6 * queries.size),
        name="prepare",
    )(live_counts, queries, out_grad, query_gain)


def attention_kernel(*refs, parts, heads):
    live_ref, prompt_ref, me_ref, queries_ref, query_rows, grads_ref, ck_ref, cv_ref, kg_ref, mask_ref = refs[:10]
    pieces, refs = refs[10:10 + parts], refs[10 + parts:]
    att_ref, ds_ref, pool_keys, own_keys, own_acc, term_ref, keep_ref = refs[:7]
    send_ref, refs = (refs[7], refs[8:]) if parts > 1 else (None, refs[7:])
    acc, pool_values, pool_values_t, own_values_t = refs[:4]
    size = kg_ref.shape[1]
    width = heads * size
    slots, _, lanes = queries_ref.shape
    per_head = lanes // CHUNK
    count = heads * per_head
    weights, grads = refs[4:4 + heads], refs[4 + heads:4 + 2 * heads]
    scores, summed = refs[4 + 2 * heads:4 + 2 * heads + count], refs[4 + 2 * heads + count:]
    score_scale = 1.0 / math.sqrt(size)
    shard = pieces[0].shape[0]

    def columns(head):
        return slice(head * size, (head + 1) * size)

    def piece_rows(piece_no):
        return pl.ds(pl.multiple_of((me_ref[0] ^ piece_no) * shard, shard), shard)

    acc[...] = jnp.zeros_like(acc)
    own_acc[...] = jnp.zeros_like(own_acc)
    for piece_no, piece in enumerate(pieces):
        pool_keys[piece_rows(piece_no), :] = piece[:, :width]
        pool_values[piece_rows(piece_no), :] = piece[:, width:]
    for head in range(heads):
        pool_values_t[columns(head), :] = pool_values[:, columns(head)].T
        own_unit, _ = unit(ck_ref[:, columns(head)].astype(F32))
        own_keys[:, columns(head)] = (own_unit * kg_ref[...]).astype(BF16)
        for slot in range(slots):
            own_values_t[slot, head] = cv_ref[slot * CL:(slot + 1) * CL, columns(head)].T

    def prompt_rows(slot):
        return pl.ds(pl.multiple_of(prompt_ref[slot] * PL, PL), PL)

    def part(no):
        head = no // per_head
        return head, columns(head), slice(no % per_head * CHUNK, (no % per_head + 1) * CHUNK)

    def begin(slot, no):
        _, place, span = part(no)
        keys = jnp.concatenate([pool_keys[prompt_rows(slot), place], own_keys[slot_rows(slot), place]], axis=0)
        scores[no][...] = dot(keys, queries_ref[slot, place, span])

    def weigh(slot, no):
        head, place, span = part(no)
        prompt, own = scores[no][:PL, :], scores[no][PL:, :] + mask_ref[...]
        factor = score_scale * math.log2(math.e)
        high = jnp.maximum(jnp.max(prompt, axis=0, keepdims=True), jnp.max(own, axis=0, keepdims=True))
        both = jnp.concatenate([prompt, own], axis=0)
        half = jnp.exp2((both - high) * factor).astype(BF16)
        weights[head][:, span] = half
        values_t = jnp.concatenate([pool_values_t[place, prompt_rows(slot)], own_values_t[slot, head]], axis=1)
        values_t = jnp.concatenate([values_t, jnp.ones((TAIL, PL + CL), BF16)], axis=0)
        summed[no][...] = dot(values_t, half)

    def back(slot, no):
        head, place, span = part(no)
        inverse = 1.0 / summed[no][size:size + 1, :]
        attended = (summed[no][:size, :] * inverse).astype(BF16)
        att_ref[slot, place, span] = attended
        scaled = (grads_ref[slot, place, span].astype(F32) * inverse).astype(BF16)
        grads[head][:, span] = scaled
        delta = jnp.sum(scaled.astype(F32) * attended.astype(F32), axis=0, keepdims=True)
        values = jnp.concatenate([pool_values[prompt_rows(slot), place], cv_ref[slot_rows(slot), place]], axis=0)
        score_grad = weights[head][:, span].astype(F32) * (dot(values, scaled) - delta)
        ds_ref[slot, head, :, span] = score_grad.astype(BF16)

    def close(slot, head):
        value_grad = dot_nt(weights[head][...], grads[head][...])
        key_grad = dot(ds_ref[slot, head], query_rows[slot, head])
        acc[prompt_rows(slot), columns(head)] += key_grad[:PL]
        acc[prompt_rows(slot), width + head * size:width + (head + 1) * size] += value_grad[:PL]
        own_acc[slot, head, 0] = key_grad[PL:]
        own_acc[slot, head, 1] = value_grad[PL:]

    def ticks(now, before):
        for tick in range(count):
            if now is not None:
                begin(now, tick)
            for number, stage in ((1, weigh), (2, back)):
                slot = now if tick >= number else before
                if slot is not None:
                    stage(slot, (tick - number) % count)
            wait = 3 if per_head > 1 else 2
            done = (tick - wait) % count
            slot = now if tick >= wait else before
            if slot is not None and done % per_head == per_head - 1:
                close(slot, done // per_head)

    def step(slot, carry):
        ticks(slot, slot - 1)
        return carry

    ticks(0, None)
    lax.fori_loop(1, live_ref[0], step, 0)
    ticks(None, live_ref[0] - 1)

    total = jnp.zeros((1, size), F32)
    for head in range(heads):
        own_grad = own_acc[:, head, 0].reshape(slots * CL, size)
        total = total + jnp.sum(own_grad * own_keys[:, columns(head)].astype(F32), axis=0, keepdims=True)
        pool_term = acc[:, columns(head)] * pool_keys[:, columns(head)].astype(F32)
        total = total + jnp.sum(pool_term, axis=0, keepdims=True)
    term_ref[...] = jnp.broadcast_to(total * score_scale, term_ref.shape)
    if parts == 1:
        keep_ref[:, :width] = acc[:, :width] * score_scale
        keep_ref[:, width:] = acc[:, width:]
    else:
        for piece_no in range(parts):
            place = slice(piece_no // 2 * shard, (piece_no // 2 + 1) * shard)
            ref = keep_ref if piece_no % 2 == 0 else send_ref
            ref[place, :width] = (acc[piece_rows(piece_no), :width] * score_scale).astype(ref.dtype)
            ref[place, width:] = acc[piece_rows(piece_no), width:].astype(ref.dtype)


def attention(live_counts, slot_prompts, me, queries, query_rows, grads, keys, values, key_gain, mask, pieces):
    size = key_gain.shape[1]
    slots, width, lanes = queries.shape
    heads = width // size
    parts = len(pieces)
    pool_rows = parts * pieces[0].shape[0]
    count = heads * lanes // CHUNK
    span = PL + CL
    out_shape = [
        jax.ShapeDtypeStruct(queries.shape, BF16),
        jax.ShapeDtypeStruct((slots, heads, span, lanes), BF16),
        jax.ShapeDtypeStruct((pool_rows, width), BF16),
        jax.ShapeDtypeStruct(keys.shape, BF16),
        jax.ShapeDtypeStruct((slots, heads, 2, CL, size), F32),
        jax.ShapeDtypeStruct((8, size), F32),
    ]
    if parts > 1:
        half = (pool_rows // 2, 2 * width)
        out_shape += [jax.ShapeDtypeStruct(half, F32), jax.ShapeDtypeStruct(half, BF16)]
    else:
        out_shape += [jax.ShapeDtypeStruct((pool_rows, 2 * width), F32)]
    return pl.pallas_call(
        functools.partial(attention_kernel, parts=parts, heads=heads),
        in_specs=[SMEM_SPEC] * 3 + [VMEM_SPEC] * (7 + parts),
        out_specs=[VMEM_SPEC] * len(out_shape),
        out_shape=out_shape,
        scratch_shapes=[
            pltpu.VMEM((pool_rows, 2 * width), F32),
            pltpu.VMEM((pool_rows, width), BF16),
            pltpu.VMEM((width, pool_rows), BF16),
            pltpu.VMEM((slots, heads, size, CL), BF16),
        ]
        + [pltpu.VMEM((span, lanes), BF16)] * heads
        + [pltpu.VMEM((size, lanes), BF16)] * heads
        + [pltpu.VMEM((span, CHUNK), F32)] * count
        + [pltpu.VMEM((size + TAIL, CHUNK), F32)] * count,
        compiler_params=params(),
        cost_estimate=cost(3 * 10**9, 10**7),
        name="attention",
    )(live_counts, slot_prompts, me, queries, query_rows, grads, keys, values, key_gain, mask, *pieces)


def copy_slots(live_ref, zeros, out, target, sems):
    slots = out.shape[0]

    def copy(source, slot):
        return pltpu.make_async_copy(source, target.at[slot_rows(slot), :], sems.at[slot])

    def dead(slot, carry):
        copy(zeros, slot).start()
        return carry

    def wait():
        for slot in range(slots):
            copy(zeros, slot).wait()

    zeros[...] = jnp.zeros_like(zeros)
    lax.fori_loop(live_ref[0], slots, dead, 0)
    return lambda slot: copy(out.at[slot], slot).start(), wait


def turn_kernel(
    live_ref, att_t_ref, own_acc, ck_ref, kg_ref, att_ref, dk_ref, dv_ref, att_out, zeros, dk_out, dv_out, sems, own_sems,
):
    slots, width, _ = att_t_ref.shape
    size = kg_ref.shape[1]
    heads = width // size
    group = att_ref.shape[1] // width
    start, wait = copy_slots(live_ref, zeros, att_out, att_ref, sems)

    def live(slot, carry):
        for head in range(heads):
            attended = att_t_ref[slot, head * size:(head + 1) * size, :].T
            for g, place in enumerate(head_columns(head, group, size)):
                att_out[slot, :, place] = attended[g * CL:(g + 1) * CL]
        start(slot)
        return carry

    lax.fori_loop(0, live_ref[0], live, 0)
    for head in range(heads):
        columns = slice(head * size, (head + 1) * size)
        own_grad = own_acc[:, head, 0].reshape(slots * CL, size) * (1.0 / math.sqrt(size))
        own_unit, own_recip = unit(ck_ref[:, columns].astype(F32))
        dk_out[:, columns] = norm_back(own_grad, own_unit, own_recip, kg_ref[...]).astype(BF16)
        dv_out[:, columns] = own_acc[:, head, 1].reshape(slots * CL, size).astype(BF16)
    own_copies = [
        pltpu.make_async_copy(dk_out, dk_ref, own_sems.at[0]),
        pltpu.make_async_copy(dv_out, dv_ref, own_sems.at[1]),
    ]
    for copy in own_copies:
        copy.start()
    for copy in own_copies:
        copy.wait()
    wait()


def turn(live_counts, att_t, own_acc, keys, key_gain, shape):
    slots = att_t.shape[0]
    own = jax.ShapeDtypeStruct(keys.shape, BF16)
    own_slab = pltpu.VMEM(keys.shape, BF16)
    return pl.pallas_call(
        turn_kernel,
        in_specs=[SMEM_SPEC] + [VMEM_SPEC] * 4,
        out_specs=[HBM_SPEC] * 3,
        out_shape=[jax.ShapeDtypeStruct(shape, BF16), own, own],
        scratch_shapes=[
            pltpu.VMEM((slots, CL, shape[1]), BF16), pltpu.VMEM((CL, shape[1]), BF16), own_slab, own_slab,
            pltpu.SemaphoreType.DMA((slots,)), pltpu.SemaphoreType.DMA((2,)),
        ],
        compiler_params=params(),
        cost_estimate=cost(2 * 10**9, 2 * 10**6),
        name="turn",
    )(live_counts, att_t, own_acc, keys, key_gain)


def post_kernel(
    live_ref, prompt_ref, ds_ref, pool_keys, own_keys_ref, raw_ref, recip_ref, col_ref, dq_ref, dq_out, zeros, sems,
):
    slots, width, lanes = raw_ref.shape
    size = col_ref.shape[0]
    heads = width // size
    group = dq_ref.shape[1] // width
    score_scale = 1.0 / math.sqrt(size)
    start, wait = copy_slots(live_ref, zeros, dq_out, dq_ref, sems)

    def live(slot, carry):
        rows = pl.ds(pl.multiple_of(prompt_ref[slot] * PL, PL), PL)
        for head in range(heads):
            columns = slice(head * size, (head + 1) * size)
            keys_t = jnp.concatenate([pool_keys[rows, columns], own_keys_ref[slot_rows(slot), columns]], axis=0).T
            query_grad = dot(keys_t, ds_ref[slot, head]) * score_scale
            recip = recip_ref[slot, head:head + 1, :]
            query_unit = raw_ref[slot, columns, :].astype(F32) * recip
            scaled = query_grad * col_ref[...]
            mean = jnp.mean(query_unit * scaled, axis=0, keepdims=True)
            query_out = (recip * (scaled - query_unit * mean)).astype(BF16).T
            for g, place in enumerate(head_columns(head, group, size)):
                dq_out[slot, :, place] = query_out[g * CL:(g + 1) * CL]
        start(slot)
        return carry

    lax.fori_loop(0, live_ref[0], live, 0)
    wait()


def post(live_counts, slot_prompts, score_grads, pool_keys, own_keys, raw, recip, query_col, shape):
    slots = raw.shape[0]
    return pl.pallas_call(
        post_kernel,
        in_specs=[SMEM_SPEC] * 2 + [VMEM_SPEC] * 6,
        out_specs=HBM_SPEC,
        out_shape=jax.ShapeDtypeStruct(shape, BF16),
        scratch_shapes=[
            pltpu.VMEM((slots, CL, shape[1]), BF16), pltpu.VMEM((CL, shape[1]), BF16),
            pltpu.SemaphoreType.DMA((slots,)),
        ],
        compiler_params=params(),
        cost_estimate=cost(3 * 10**9, 4 * 10**6),
        name="post",
    )(live_counts, slot_prompts, score_grads, pool_keys, own_keys, raw, recip, query_col)


def tree(terms):
    while len(terms) > 1:
        terms = [left + right for left, right in zip(terms[::2], terms[1::2])]
    return terms[0]


def add_kernel(keep_ref, came_ref, *refs, terms):
    tail = gain_rows(tree([ref[0:1, :] for ref in refs[:terms]]))
    size = tail.shape[1]
    own_ref, send_refs = refs[terms], refs[terms + 1:]
    blocks = len(send_refs) + 1
    shard = keep_ref.shape[0] // blocks
    for at in range(blocks):
        place = slice(at * shard, (at + 1) * shard)
        ref = send_refs[blocks - 1 - at] if at > 0 else own_ref
        total = keep_ref[place, :] + came_ref[place, :].astype(F32)
        for slab in range(keep_ref.shape[1] // size):
            ref[slab * shard:(slab + 1) * shard, :] = total[:, slab * size:(slab + 1) * size].astype(ref.dtype)
        ref[ref.shape[0] - TAIL:, :] = tail.astype(ref.dtype)


def add(keep, came, terms, blocks):
    size = terms[0].shape[1]
    shape = (keep.size // blocks // size + TAIL, size)
    return pl.pallas_call(
        functools.partial(add_kernel, terms=len(terms)),
        in_specs=[VMEM_SPEC] * (2 + len(terms)),
        out_specs=[VMEM_SPEC] * blocks,
        out_shape=[jax.ShapeDtypeStruct(shape, F32)] + [jax.ShapeDtypeStruct(shape, BF16)] * (blocks - 1),
        compiler_params=params(),
        name="add",
    )(keep, came, *terms)


def chips_kernel(*refs):
    parts = [gain_term(ref[ref.shape[0] - TAIL:, :]) for ref in refs[:-1]]
    total = tree(parts[:1] + parts[:0:-1])
    refs[-1][...] = jnp.broadcast_to(total, refs[-1].shape)


def sum_chips(blocks):
    return pl.pallas_call(
        chips_kernel,
        in_specs=[VMEM_SPEC] * len(blocks),
        out_specs=VMEM_SPEC,
        out_shape=jax.ShapeDtypeStruct((8, blocks[0].shape[1]), F32),
        compiler_params=params(),
        name="sum_chips",
    )(*blocks)


def last_kernel(*refs):
    terms, (qg_ref, kg_ref, query_ref, key_ref) = refs[:-4], refs[-4:]
    total = tree([ref[0:1, :] for ref in terms])
    query_ref[...] = total / qg_ref[...]
    key_ref[...] = total / kg_ref[...]


def gain_grads(terms, query_gain, key_gain):
    row = jax.ShapeDtypeStruct(query_gain.shape, F32)
    return pl.pallas_call(
        last_kernel,
        in_specs=[VMEM_SPEC] * (len(terms) + 2),
        out_specs=[VMEM_SPEC] * 2,
        out_shape=[row, row],
        compiler_params=params(),
        name="gain_grads",
    )(*terms, query_gain, key_gain)


def finish_kernel(*refs):
    parts, (raw_ref, kg_ref, key_ref, value_ref) = refs[:-4], refs[-4:]
    size = kg_ref.shape[1]
    shard, width = raw_ref.shape
    heads = width // size
    for slab in range(2 * heads):
        rows = slice(slab * shard, (slab + 1) * shard)
        total = parts[0][rows, :]
        for ref in parts[1:]:
            total = total + ref[rows, :].astype(F32)
        columns = slice(slab % heads * size, (slab % heads + 1) * size)
        if slab < heads:
            unit_rows, recip = unit(raw_ref[:, columns].astype(F32))
            key_ref[:, columns] = norm_back(total, unit_rows, recip, kg_ref[...])
        else:
            value_ref[:, columns] = total


def finish(blocks, raw, key_gain):
    shape = jax.ShapeDtypeStruct(raw.shape, F32)
    return pl.pallas_call(
        finish_kernel,
        in_specs=[VMEM_SPEC] * (len(blocks) + 2),
        out_specs=[VMEM_SPEC] * 2,
        out_shape=[shape, shape],
        compiler_params=params(),
        cost_estimate=cost(10**8, 10**6),
        name="finish",
    )(*blocks, raw, key_gain)


def swap(values, axis, step):
    return lax.ppermute(values, axis, [(i, i ^ step) for i in range(lax.axis_size(axis))])


def local(
    comp_queries, comp_keys, comp_values, prompt_keys, prompt_values,
    query_gain, key_gain, out_grad, live_counts, slot_prompts,
):
    grp, tp = lax.axis_size("grp"), lax.axis_size("tp")
    shard = prompt_keys.shape[0]
    size = query_gain.shape[0]
    by_permute = shard % 16 == 0 and grp > 1 and grp & (grp - 1) == 0 and tp & (tp - 1) == 0
    slots, width = slot_prompts.shape[0], comp_keys.shape[1]
    query_gain, key_gain = query_gain.reshape(1, size), key_gain.reshape(1, size)
    me = lax.axis_index("grp").astype(jnp.int32).reshape(1) if by_permute else jnp.zeros((1,), jnp.int32)
    mask, me, keys_in, values_in = lax.optimization_barrier((causal(), me, prompt_keys, prompt_values))
    mine = pack(keys_in, values_in, key_gain)
    raw, recip, queries, grads, query_col, query_rows = prepare(live_counts, comp_queries, out_grad, query_gain, slots, width)
    if by_permute:
        even = [mine] + [swap(mine, "grp", step) for step in range(2, grp, 2)]
        odd = [swap(mine, "grp", 1)] + [None] * (len(even) - 1)
        for at in range(len(even) - 1, 0, -1):
            if at == 1:
                even[at], query_col, odd[-1] = lax.optimization_barrier((even[at], query_col, odd[-1]))
            else:
                even[at], query_col = lax.optimization_barrier((even[at], query_col))
            odd[at] = swap(even[at], "grp", 1)
        pieces = [piece for pair in zip(even, odd) for piece in pair]
    else:
        pieces = [lax.all_gather(mine, "grp", axis=0, tiled=True)]
    att_t, score_grads, pool_keys, own_keys, own_acc, term, keep, *send = attention(
        live_counts, slot_prompts, me, queries, query_rows, grads, comp_keys, comp_values, key_gain, mask, pieces,
    )
    attended, key_grads, value_grads = turn(live_counts, att_t, own_acc, comp_keys, key_gain, comp_queries.shape)
    query_grads = post(
        live_counts, slot_prompts, score_grads, pool_keys, own_keys, raw, recip, query_col, comp_queries.shape,
    )
    if by_permute:
        came = swap(send[0], "grp", 1)
        terms = [term] + [swap(term, "tp", step) for step in range(1, tp)]
        terms, attended = lax.optimization_barrier((terms, attended))
        own, *blocks = add(keep, came, terms, grp // 2)
        blocks = [swap(block, "grp", grp - 2 - 2 * at) for at, block in enumerate(blocks)]
        blocks, query_grads = lax.optimization_barrier((blocks, query_grads))
        blocks = [own] + blocks
        total = sum_chips(blocks)
        terms = [total, swap(total, "grp", 1)]
    else:
        block = lax.psum_scatter(keep, "grp", scatter_dimension=0, tiled=True)
        blocks = [jnp.concatenate([block[:, at:at + size] for at in range(0, 2 * width, size)], axis=0)]
        terms = [lax.psum(term, ("grp", "tp"))]
    prompt_key_grads, prompt_value_grads = finish(blocks, prompt_keys, key_gain)
    query_gain_grad, key_gain_grad = gain_grads(terms, query_gain, key_gain)
    return (
        attended, query_grads, key_grads, value_grads, prompt_key_grads, prompt_value_grads,
        query_gain_grad.reshape(size), key_gain_grad.reshape(size),
    )


def solution(mesh):
    split, whole = P("grp", "tp"), P()
    return jax.shard_map(
        local,
        mesh=mesh,
        in_specs=(split, split, split, split, split, whole, whole, split, P("grp"), P("grp")),
        out_specs=(split, split, split, split, split, split, whole, whole),
        check_vma=False,
    )
```

```python
import functools
import math

import jax
import jax.numpy as jnp
from jax import lax
from jax.experimental import pallas as pl
from jax.experimental.pallas import tpu as pltpu
from jax.sharding import PartitionSpec as P

PL = 384
CL = 64
EPS = 1e-06
TAIL = 16
CHUNK = 512
VMEM_LIMIT = 24 * 1024 * 1024
F32 = jnp.float32
BF16 = jnp.bfloat16
SMEM_SPEC = pl.BlockSpec(memory_space=pltpu.SMEM)
VMEM_SPEC = pl.BlockSpec(memory_space=pltpu.VMEM)
HBM_SPEC = pl.BlockSpec(memory_space=pltpu.HBM)


def dot(left, right):
    return jnp.dot(left, right, preferred_element_type=F32)


def dot_nt(left, right):
    return lax.dot_general(left, right, (((1,), (1,)), ((), ())), preferred_element_type=F32)


def unit(raw):
    recip = lax.rsqrt(jnp.mean(raw * raw, axis=-1, keepdims=True) + EPS)
    return raw * recip, recip


def norm_back(upstream, unit_rows, recip, gain):
    scaled = upstream * gain
    return recip * (scaled - unit_rows * jnp.mean(unit_rows * scaled, axis=-1, keepdims=True))


def gain_rows(term):
    upper = term.astype(BF16).astype(F32)
    rows = jnp.concatenate([upper, term - upper, jnp.zeros((TAIL - 2, term.shape[1]), F32)], axis=0)
    return rows.astype(BF16)


def gain_term(rows):
    return rows[0:1].astype(F32) + rows[1:2].astype(F32)


def params(limit=VMEM_LIMIT):
    return pltpu.CompilerParams(vmem_limit_bytes=limit)


def cost(flops, size):
    return pl.CostEstimate(flops=flops, bytes_accessed=size, transcendentals=0)


def causal_kernel(mask_ref):
    key_no = lax.broadcasted_iota(jnp.int32, mask_ref.shape, 0)
    token_no = lax.broadcasted_iota(jnp.int32, mask_ref.shape, 1) % CL
    mask_ref[...] = jnp.where(key_no <= token_no, 0.0, -jnp.inf)


def causal():
    return pl.pallas_call(
        causal_kernel,
        out_specs=VMEM_SPEC,
        out_shape=jax.ShapeDtypeStruct((CL, CHUNK), F32),
        compiler_params=params(),
        cost_estimate=cost(4 * 10**9, 10**6),
        name="causal",
    )()


def pack_kernel(keys_ref, values_ref, kg_ref, out_ref):
    size, width = kg_ref.shape[1], keys_ref.shape[1]
    for head in range(width // size):
        columns = slice(head * size, (head + 1) * size)
        unit_rows, _ = unit(keys_ref[:, columns].astype(F32))
        out_ref[:, columns] = (unit_rows * kg_ref[...]).astype(BF16)
    out_ref[:, width:] = values_ref[...]


def pack(keys, values, key_gain):
    return pl.pallas_call(
        pack_kernel,
        in_specs=[VMEM_SPEC] * 3,
        out_specs=VMEM_SPEC,
        out_shape=jax.ShapeDtypeStruct((keys.shape[0], 2 * keys.shape[1]), BF16),
        compiler_params=params(),
        cost_estimate=cost(4 * 10**9, 10**6),
        name="pack",
    )(keys, values, key_gain)


def head_columns(head, group, size):
    return [slice((head * group + g) * size, (head * group + g + 1) * size) for g in range(group)]


def slot_rows(slot):
    return pl.ds(pl.multiple_of(slot * CL, CL), CL)


def prepare_kernel(live_ref, q_ref, do_ref, qg_ref, raw_ref, recip_ref, queries_ref, grads_ref, col_ref):
    size = col_ref.shape[0]
    heads = raw_ref.shape[1] // size
    group = q_ref.shape[1] // raw_ref.shape[1]
    column = jnp.broadcast_to(qg_ref[...], (size, size)).T
    for at in range(0, col_ref.shape[1], size):
        col_ref[:, at:at + size] = column

    def live(slot, carry):
        for head in range(heads):
            places = head_columns(head, group, size)
            rows = slice(head * size, (head + 1) * size)
            half = jnp.concatenate([q_ref[slot_rows(slot), place] for place in places], axis=0).T
            raw_ref[slot, rows, :] = half
            raw = half.astype(F32)
            recip = lax.rsqrt(jnp.mean(raw * raw, axis=0, keepdims=True) + EPS)
            recip_ref[slot, head:head + 1, :] = recip
            queries_ref[slot, rows, :] = (raw * recip * col_ref[...]).astype(BF16)
            grads_ref[slot, rows, :] = jnp.concatenate([do_ref[slot_rows(slot), place] for place in places], axis=0).T
        return carry

    lax.fori_loop(0, live_ref[0], live, 0)


def prepare(live_counts, queries, out_grad, query_gain, slots, width):
    size = query_gain.shape[1]
    lanes = queries.shape[1] // width * CL
    turned = jax.ShapeDtypeStruct((slots, width, lanes), BF16)
    return pl.pallas_call(
        prepare_kernel,
        in_specs=[SMEM_SPEC] + [VMEM_SPEC] * 3,
        out_specs=[VMEM_SPEC] * 5,
        out_shape=[
            turned, jax.ShapeDtypeStruct((slots, 8, lanes), F32), turned, turned,
            jax.ShapeDtypeStruct((size, lanes), F32),
        ],
        compiler_params=params(),
        cost_estimate=cost(2 * 10**9, 6 * queries.size),
        name="prepare",
    )(live_counts, queries, out_grad, query_gain)


def give_pieces(acc, me_ref, parts, keep_ref, send_ref, scale):
    if parts == 1:
        keep_ref[...] = acc[...] * scale
        return
    shard = acc.shape[0] // parts
    for piece_no in range(parts):
        rows = pl.ds(pl.multiple_of((me_ref[0] ^ piece_no) * shard, shard), shard)
        place = slice(piece_no // 2 * shard, (piece_no // 2 + 1) * shard)
        ref = keep_ref if piece_no % 2 == 0 else send_ref
        ref[place, :] = (acc[rows, :] * scale).astype(ref.dtype)


def piece_shapes(pool_rows, width, parts):
    if parts == 1:
        return [jax.ShapeDtypeStruct((pool_rows, width), F32)]
    return [jax.ShapeDtypeStruct((pool_rows // 2, width), kind) for kind in (F32, BF16)]


def attention_kernel(*refs, parts, heads):
    live_ref, prompt_ref, me_ref, queries_ref, grads_ref, ck_ref, cv_ref, kg_ref, mask_ref = refs[:9]
    pieces, refs = refs[9:9 + parts], refs[9 + parts:]
    att_ref, ds_ref, weights, grads, pool_keys, own_keys, own_acc, term_ref, keep_ref = refs[:9]
    send_ref, refs = (refs[9], refs[10:]) if parts > 1 else (None, refs[9:])
    acc, pool_values, pool_values_t, own_values_t = refs[:4]
    size = kg_ref.shape[1]
    width = heads * size
    slots, _, lanes = queries_ref.shape
    per_head = lanes // CHUNK
    count = heads * per_head
    scores, summed = refs[4:4 + count], refs[4 + count:]
    score_scale = 1.0 / math.sqrt(size)
    shard = pieces[0].shape[0]

    def columns(head):
        return slice(head * size, (head + 1) * size)

    def piece_rows(piece_no):
        return pl.ds(pl.multiple_of((me_ref[0] ^ piece_no) * shard, shard), shard)

    acc[...] = jnp.zeros_like(acc)
    own_acc[...] = jnp.zeros_like(own_acc)
    for piece_no, piece in enumerate(pieces):
        pool_keys[piece_rows(piece_no), :] = piece[:, :width]
        pool_values[piece_rows(piece_no), :] = piece[:, width:]
    for head in range(heads):
        pool_values_t[columns(head), :] = pool_values[:, columns(head)].T
        own_unit, _ = unit(ck_ref[:, columns(head)].astype(F32))
        own_keys[:, columns(head)] = (own_unit * kg_ref[...]).astype(BF16)
        for slot in range(slots):
            own_values_t[slot, head] = cv_ref[slot * CL:(slot + 1) * CL, columns(head)].T

    def prompt_rows(slot):
        return pl.ds(pl.multiple_of(prompt_ref[slot] * PL, PL), PL)

    def part(no):
        head = no // per_head
        return head, columns(head), slice(no % per_head * CHUNK, (no % per_head + 1) * CHUNK)

    def begin(slot, no):
        _, place, span = part(no)
        keys = jnp.concatenate([pool_keys[prompt_rows(slot), place], own_keys[slot_rows(slot), place]], axis=0)
        scores[no][...] = dot(keys, queries_ref[slot, place, span])

    def weigh(slot, no):
        head, place, span = part(no)
        prompt, own = scores[no][:PL, :], scores[no][PL:, :] + mask_ref[...]
        factor = score_scale * math.log2(math.e)
        high = jnp.maximum(jnp.max(prompt, axis=0, keepdims=True), jnp.max(own, axis=0, keepdims=True))
        both = jnp.concatenate([prompt, own], axis=0)
        half = jnp.exp2((both - high) * factor).astype(BF16)
        weights[slot, head, :, span] = half
        values_t = jnp.concatenate([pool_values_t[place, prompt_rows(slot)], own_values_t[slot, head]], axis=1)
        values_t = jnp.concatenate([values_t, jnp.ones((TAIL, PL + CL), BF16)], axis=0)
        summed[no][...] = dot(values_t, half)

    def back(slot, no):
        head, place, span = part(no)
        inverse = 1.0 / summed[no][size:size + 1, :]
        attended = (summed[no][:size, :] * inverse).astype(BF16)
        att_ref[slot, place, span] = attended
        scaled = (grads_ref[slot, place, span].astype(F32) * inverse).astype(BF16)
        grads[slot, place, span] = scaled
        delta = jnp.sum(scaled.astype(F32) * attended.astype(F32), axis=0, keepdims=True)
        values = jnp.concatenate([pool_values[prompt_rows(slot), place], cv_ref[slot_rows(slot), place]], axis=0)
        score_grad = weights[slot, head, :, span].astype(F32) * (dot(values, scaled) - delta)
        ds_ref[slot, head, :, span] = score_grad.astype(BF16)

    def close(slot, head):
        key_grad = dot_nt(ds_ref[slot, head], queries_ref[slot, columns(head), :])
        acc[prompt_rows(slot), columns(head)] += key_grad[:PL]
        own_acc[slot, head] = key_grad[PL:]

    def ticks(now, before):
        for tick in range(count):
            if now is not None:
                begin(now, tick)
            for number, stage in ((1, weigh), (2, back)):
                slot = now if tick >= number else before
                if slot is not None:
                    stage(slot, (tick - number) % count)
            wait = 3 if per_head > 1 else 2
            done = (tick - wait) % count
            slot = now if tick >= wait else before
            if slot is not None and done % per_head == per_head - 1:
                close(slot, done // per_head)

    def step(slot, carry):
        ticks(slot, slot - 1)
        return carry

    ticks(0, None)
    lax.fori_loop(1, live_ref[0], step, 0)
    ticks(None, live_ref[0] - 1)

    total = jnp.zeros((1, size), F32)
    for head in range(heads):
        own_grad = own_acc[:, head].reshape(slots * CL, size)
        total = total + jnp.sum(own_grad * own_keys[:, columns(head)].astype(F32), axis=0, keepdims=True)
        pool_term = acc[:, columns(head)] * pool_keys[:, columns(head)].astype(F32)
        total = total + jnp.sum(pool_term, axis=0, keepdims=True)
    term_ref[...] = jnp.broadcast_to(total * score_scale, term_ref.shape)
    give_pieces(acc, me_ref, parts, keep_ref, send_ref, score_scale)


def attention(live_counts, slot_prompts, me, queries, grads, keys, values, key_gain, mask, pieces):
    size = key_gain.shape[1]
    slots, width, lanes = queries.shape
    heads = width // size
    parts = len(pieces)
    pool_rows = parts * pieces[0].shape[0]
    count = heads * lanes // CHUNK
    span = PL + CL
    per_slot = jax.ShapeDtypeStruct((slots, heads, span, lanes), BF16)
    turned = jax.ShapeDtypeStruct(queries.shape, BF16)
    out_shape = [
        turned, per_slot, per_slot, turned,
        jax.ShapeDtypeStruct((pool_rows, width), BF16),
        jax.ShapeDtypeStruct(keys.shape, BF16),
        jax.ShapeDtypeStruct((slots, heads, CL, size), F32),
        jax.ShapeDtypeStruct((8, size), F32),
    ] + piece_shapes(pool_rows, width, parts)
    return pl.pallas_call(
        functools.partial(attention_kernel, parts=parts, heads=heads),
        in_specs=[SMEM_SPEC] * 3 + [VMEM_SPEC] * (6 + parts),
        out_specs=[VMEM_SPEC] * len(out_shape),
        out_shape=out_shape,
        scratch_shapes=[
            pltpu.VMEM((pool_rows, width), F32),
            pltpu.VMEM((pool_rows, width), BF16),
            pltpu.VMEM((width, pool_rows), BF16),
            pltpu.VMEM((slots, heads, size, CL), BF16),
        ]
        + [pltpu.VMEM((span, CHUNK), F32)] * count
        + [pltpu.VMEM((size + TAIL, CHUNK), F32)] * count,
        compiler_params=params(),
        cost_estimate=cost(3 * 10**9, 10**7),
        name="attention",
    )(live_counts, slot_prompts, me, queries, grads, keys, values, key_gain, mask, *pieces)


def values_kernel(live_ref, prompt_ref, me_ref, weights, grads, own_acc, keep_ref, *refs, parts):
    send_ref, acc = refs if parts > 1 else (None, refs[0])
    slots, heads, _, _ = weights.shape
    size = own_acc.shape[3]
    acc[...] = jnp.zeros_like(acc)
    own_acc[...] = jnp.zeros_like(own_acc)

    def live(slot, carry):
        rows = pl.ds(pl.multiple_of(prompt_ref[slot] * PL, PL), PL)
        for head in range(heads):
            columns = slice(head * size, (head + 1) * size)
            value_grad = dot_nt(weights[slot, head], grads[slot, columns, :])
            acc[rows, columns] += value_grad[:PL]
            own_acc[slot, head] = value_grad[PL:]
        return carry

    lax.fori_loop(0, live_ref[0], live, 0)
    give_pieces(acc, me_ref, parts, keep_ref, send_ref, 1.0)


def value_grads(live_counts, slot_prompts, me, weights, grads, pool_rows, parts):
    slots, heads, _, _ = weights.shape
    width = grads.shape[1]
    out_shape = [jax.ShapeDtypeStruct((slots, heads, CL, width // heads), F32)]
    out_shape += piece_shapes(pool_rows, width, parts)
    return pl.pallas_call(
        functools.partial(values_kernel, parts=parts),
        in_specs=[SMEM_SPEC] * 3 + [VMEM_SPEC] * 2,
        out_specs=[VMEM_SPEC] * len(out_shape),
        out_shape=out_shape,
        scratch_shapes=[pltpu.VMEM((pool_rows, width), F32)],
        compiler_params=params(),
        cost_estimate=cost(2 * 10**9, 10**6),
        name="values",
    )(live_counts, slot_prompts, me, weights, grads)


def copy_slots(live_ref, zeros, out, target, sems):
    slots = out.shape[0]

    def copy(source, slot):
        return pltpu.make_async_copy(source, target.at[slot_rows(slot), :], sems.at[slot])

    def dead(slot, carry):
        copy(zeros, slot).start()
        return carry

    def wait():
        for slot in range(slots):
            copy(zeros, slot).wait()

    zeros[...] = jnp.zeros_like(zeros)
    lax.fori_loop(live_ref[0], slots, dead, 0)
    return lambda slot: copy(out.at[slot], slot).start(), wait


def turn_kernel(
    live_ref, att_t_ref, own_keys, ck_ref, kg_ref, att_ref, dk_ref, att_out, zeros, dk_out, sems, own_sem,
):
    slots, width, _ = att_t_ref.shape
    size = kg_ref.shape[1]
    heads = width // size
    group = att_ref.shape[1] // width
    start, wait = copy_slots(live_ref, zeros, att_out, att_ref, sems)

    def live(slot, carry):
        for head in range(heads):
            attended = att_t_ref[slot, head * size:(head + 1) * size, :].T
            for g, place in enumerate(head_columns(head, group, size)):
                att_out[slot, :, place] = attended[g * CL:(g + 1) * CL]
        start(slot)
        return carry

    lax.fori_loop(0, live_ref[0], live, 0)
    for head in range(heads):
        columns = slice(head * size, (head + 1) * size)
        own_grad = own_keys[:, head].reshape(slots * CL, size) * (1.0 / math.sqrt(size))
        own_unit, own_recip = unit(ck_ref[:, columns].astype(F32))
        dk_out[:, columns] = norm_back(own_grad, own_unit, own_recip, kg_ref[...]).astype(BF16)
    own_copy = pltpu.make_async_copy(dk_out, dk_ref, own_sem)
    own_copy.start()
    own_copy.wait()
    wait()


def turn(live_counts, att_t, own_keys, keys, key_gain, shape):
    slots = att_t.shape[0]
    return pl.pallas_call(
        turn_kernel,
        in_specs=[SMEM_SPEC] + [VMEM_SPEC] * 4,
        out_specs=[HBM_SPEC] * 2,
        out_shape=[jax.ShapeDtypeStruct(shape, BF16), jax.ShapeDtypeStruct(keys.shape, BF16)],
        scratch_shapes=[
            pltpu.VMEM((slots, CL, shape[1]), BF16), pltpu.VMEM((CL, shape[1]), BF16), pltpu.VMEM(keys.shape, BF16),
            pltpu.SemaphoreType.DMA((slots,)), pltpu.SemaphoreType.DMA,
        ],
        compiler_params=params(),
        cost_estimate=cost(4 * 10**11, 2 * 10**6),
        name="turn",
    )(live_counts, att_t, own_keys, keys, key_gain)


def post_kernel(
    live_ref, prompt_ref, ds_ref, pool_keys, own_keys_ref, own_values, raw_ref, recip_ref, col_ref,
    dq_ref, dv_ref, dq_out, zeros, dv_out, sems, own_sem,
):
    slots, width, lanes = raw_ref.shape
    size = col_ref.shape[0]
    heads = width // size
    group = dq_ref.shape[1] // width
    score_scale = 1.0 / math.sqrt(size)
    start, wait = copy_slots(live_ref, zeros, dq_out, dq_ref, sems)
    for head in range(heads):
        dv_out[:, head * size:(head + 1) * size] = own_values[:, head].reshape(slots * CL, size).astype(BF16)
    own_copy = pltpu.make_async_copy(dv_out, dv_ref, own_sem)
    own_copy.start()

    def live(slot, carry):
        rows = pl.ds(pl.multiple_of(prompt_ref[slot] * PL, PL), PL)
        for head in range(heads):
            columns = slice(head * size, (head + 1) * size)
            keys_t = jnp.concatenate([pool_keys[rows, columns], own_keys_ref[slot_rows(slot), columns]], axis=0).T
            query_grad = dot(keys_t, ds_ref[slot, head]) * score_scale
            recip = recip_ref[slot, head:head + 1, :]
            query_unit = raw_ref[slot, columns, :].astype(F32) * recip
            scaled = query_grad * col_ref[...]
            mean = jnp.mean(query_unit * scaled, axis=0, keepdims=True)
            query_out = (recip * (scaled - query_unit * mean)).astype(BF16).T
            for g, place in enumerate(head_columns(head, group, size)):
                dq_out[slot, :, place] = query_out[g * CL:(g + 1) * CL]
        start(slot)
        return carry

    lax.fori_loop(0, live_ref[0], live, 0)
    own_copy.wait()
    wait()


def post(live_counts, slot_prompts, score_grads, pool_keys, own_keys, own_values, raw, recip, query_col, shape):
    slots = raw.shape[0]
    return pl.pallas_call(
        post_kernel,
        in_specs=[SMEM_SPEC] * 2 + [VMEM_SPEC] * 7,
        out_specs=[HBM_SPEC] * 2,
        out_shape=[jax.ShapeDtypeStruct(shape, BF16), jax.ShapeDtypeStruct(own_keys.shape, BF16)],
        scratch_shapes=[
            pltpu.VMEM((slots, CL, shape[1]), BF16), pltpu.VMEM((CL, shape[1]), BF16), pltpu.VMEM(own_keys.shape, BF16),
            pltpu.SemaphoreType.DMA((slots,)), pltpu.SemaphoreType.DMA,
        ],
        compiler_params=params(),
        cost_estimate=cost(3 * 10**9, 4 * 10**6),
        name="post",
    )(live_counts, slot_prompts, score_grads, pool_keys, own_keys, own_values, raw, recip, query_col)


def tree(terms):
    while len(terms) > 1:
        terms = [left + right for left, right in zip(terms[::2], terms[1::2])]
    return terms[0]


def add_kernel(*refs, terms):
    halves, refs = (refs[:2], refs[2:4]), refs[4:]
    tail = gain_rows(tree([ref[0:1, :] for ref in refs[:terms]]))
    size = tail.shape[1]
    own_ref, send_refs = refs[terms], refs[terms + 1:]
    blocks = len(send_refs) + 1
    rows, width = halves[0][0].shape
    shard = rows // blocks
    heads = width // size
    for at in range(blocks):
        place = slice(at * shard, (at + 1) * shard)
        ref = send_refs[blocks - 1 - at] if at > 0 else own_ref
        for slab in range(2 * heads):
            keep_ref, came_ref = halves[slab // heads]
            columns = slice(slab % heads * size, (slab % heads + 1) * size)
            total = keep_ref[place, columns] + came_ref[place, columns].astype(F32)
            ref[slab * shard:(slab + 1) * shard, :] = total.astype(ref.dtype)
        ref[2 * heads * shard:, :] = tail.astype(ref.dtype)


def add(keys, values, terms, blocks):
    size = terms[0].shape[1]
    shape = (2 * keys[0].size // blocks // size + TAIL, size)
    return pl.pallas_call(
        functools.partial(add_kernel, terms=len(terms)),
        in_specs=[VMEM_SPEC] * (4 + len(terms)),
        out_specs=[VMEM_SPEC] * blocks,
        out_shape=[jax.ShapeDtypeStruct(shape, F32)] + [jax.ShapeDtypeStruct(shape, BF16)] * (blocks - 1),
        compiler_params=params(),
        name="add",
    )(*keys, *values, *terms)


def chips_kernel(*refs):
    parts = [gain_term(ref[ref.shape[0] - TAIL:, :]) for ref in refs[:-1]]
    total = tree(parts[:1] + parts[:0:-1])
    refs[-1][...] = jnp.broadcast_to(total, refs[-1].shape)


def sum_chips(blocks):
    return pl.pallas_call(
        chips_kernel,
        in_specs=[VMEM_SPEC] * len(blocks),
        out_specs=VMEM_SPEC,
        out_shape=jax.ShapeDtypeStruct((8, blocks[0].shape[1]), F32),
        compiler_params=params(),
        name="sum_chips",
    )(*blocks)


def last_kernel(*refs):
    terms, (qg_ref, kg_ref, query_ref, key_ref) = refs[:-4], refs[-4:]
    total = tree([ref[0:1, :] for ref in terms])
    query_ref[...] = total / qg_ref[...]
    key_ref[...] = total / kg_ref[...]


def gain_grads(terms, query_gain, key_gain):
    row = jax.ShapeDtypeStruct(query_gain.shape, F32)
    return pl.pallas_call(
        last_kernel,
        in_specs=[VMEM_SPEC] * (len(terms) + 2),
        out_specs=[VMEM_SPEC] * 2,
        out_shape=[row, row],
        compiler_params=params(),
        name="gain_grads",
    )(*terms, query_gain, key_gain)


def finish_kernel(*refs):
    parts, (raw_ref, kg_ref, key_ref, value_ref) = refs[:-4], refs[-4:]
    size = kg_ref.shape[1]
    shard, width = raw_ref.shape
    heads = width // size
    for slab in range(2 * heads):
        rows = slice(slab * shard, (slab + 1) * shard)
        total = parts[0][rows, :]
        for ref in parts[1:]:
            total = total + ref[rows, :].astype(F32)
        columns = slice(slab % heads * size, (slab % heads + 1) * size)
        if slab < heads:
            unit_rows, recip = unit(raw_ref[:, columns].astype(F32))
            key_ref[:, columns] = norm_back(total, unit_rows, recip, kg_ref[...])
        else:
            value_ref[:, columns] = total


def finish(blocks, raw, key_gain):
    shape = jax.ShapeDtypeStruct(raw.shape, F32)
    return pl.pallas_call(
        finish_kernel,
        in_specs=[VMEM_SPEC] * (len(blocks) + 2),
        out_specs=[VMEM_SPEC] * 2,
        out_shape=[shape, shape],
        compiler_params=params(),
        cost_estimate=cost(10**8, 10**6),
        name="finish",
    )(*blocks, raw, key_gain)


def swap(values, axis, step):
    return lax.ppermute(values, axis, [(i, i ^ step) for i in range(lax.axis_size(axis))])


def local(
    comp_queries, comp_keys, comp_values, prompt_keys, prompt_values,
    query_gain, key_gain, out_grad, live_counts, slot_prompts,
):
    grp, tp = lax.axis_size("grp"), lax.axis_size("tp")
    shard = prompt_keys.shape[0]
    size = query_gain.shape[0]
    by_permute = shard % 16 == 0 and grp > 1 and grp & (grp - 1) == 0 and tp & (tp - 1) == 0
    slots, width = slot_prompts.shape[0], comp_keys.shape[1]
    query_gain, key_gain = query_gain.reshape(1, size), key_gain.reshape(1, size)
    me = lax.axis_index("grp").astype(jnp.int32).reshape(1) if by_permute else jnp.zeros((1,), jnp.int32)
    mask, me, keys_in, values_in = lax.optimization_barrier((causal(), me, prompt_keys, prompt_values))
    mine = pack(keys_in, values_in, key_gain)
    raw, recip, queries, grads, query_col = prepare(live_counts, comp_queries, out_grad, query_gain, slots, width)
    if by_permute:
        even = [mine] + [swap(mine, "grp", step) for step in range(2, grp, 2)]
        odd = [swap(mine, "grp", 1)] + [None] * (len(even) - 1)
        for at in range(len(even) - 1, 0, -1):
            if at == 1:
                even[at], query_col, odd[-1] = lax.optimization_barrier((even[at], query_col, odd[-1]))
            else:
                even[at], query_col = lax.optimization_barrier((even[at], query_col))
            odd[at] = swap(even[at], "grp", 1)
        pieces = [piece for pair in zip(even, odd) for piece in pair]
    else:
        pieces = [lax.all_gather(mine, "grp", axis=0, tiled=True)]
    att_t, score_grads, weights, grads, pool_keys, own_keys, own_key_acc, term, *key_pieces = attention(
        live_counts, slot_prompts, me, queries, grads, comp_keys, comp_values, key_gain, mask, pieces,
    )
    if by_permute:
        terms = [term] + [swap(term, "tp", step) for step in range(1, tp)]
    own_value_acc, *value_pieces = value_grads(
        live_counts, slot_prompts, me, weights, grads, pool_keys.shape[0], len(pieces),
    )
    attended, comp_key_grads = turn(live_counts, att_t, own_key_acc, comp_keys, key_gain, comp_queries.shape)
    query_grads, comp_value_grads = post(
        live_counts, slot_prompts, score_grads, pool_keys, own_keys, own_value_acc, raw, recip, query_col,
        comp_queries.shape,
    )
    if by_permute:
        key_pieces, value_pieces = ((keep, swap(send, "grp", 1)) for keep, send in (key_pieces, value_pieces))
        terms, attended = lax.optimization_barrier((terms, attended))
        own, *blocks = add(key_pieces, value_pieces, terms, grp // 2)
        blocks = [swap(block, "grp", grp - 2 - 2 * at) for at, block in enumerate(blocks)]
        blocks, query_grads = lax.optimization_barrier((blocks, query_grads))
        blocks = [own] + blocks
        total = sum_chips(blocks)
        terms = [total, swap(total, "grp", 1)]
    else:
        pool_grads = jnp.concatenate(key_pieces + value_pieces, axis=1)
        block = lax.psum_scatter(pool_grads, "grp", scatter_dimension=0, tiled=True)
        blocks = [jnp.concatenate([block[:, at:at + size] for at in range(0, 2 * width, size)], axis=0)]
        terms = [lax.psum(term, ("grp", "tp"))]
    prompt_key_grads, prompt_value_grads = finish(blocks, prompt_keys, key_gain)
    query_gain_grad, key_gain_grad = gain_grads(terms, query_gain, key_gain)
    return (
        attended, query_grads, comp_key_grads, comp_value_grads, prompt_key_grads, prompt_value_grads,
        query_gain_grad.reshape(size), key_gain_grad.reshape(size),
    )


def solution(mesh):
    split, whole = P("grp", "tp"), P()
    return jax.shard_map(
        local,
        mesh=mesh,
        in_specs=(split, split, split, split, split, whole, whole, split, P("grp"), P("grp")),
        out_specs=(split, split, split, split, split, split, whole, whole),
        check_vma=False,
    )
```

```python
import functools
import math

import jax
import jax.numpy as jnp
from jax import lax
from jax.experimental import pallas as pl
from jax.experimental.pallas import tpu as pltpu
from jax.sharding import PartitionSpec as P

PL = 384
CL = 64
EPS = 1e-06
TAIL = 16
CHUNK = 512
VMEM_LIMIT = 24 * 1024 * 1024
F32 = jnp.float32
BF16 = jnp.bfloat16
SMEM_SPEC = pl.BlockSpec(memory_space=pltpu.SMEM)
VMEM_SPEC = pl.BlockSpec(memory_space=pltpu.VMEM)
HBM_SPEC = pl.BlockSpec(memory_space=pltpu.HBM)


def dot(left, right):
    return jnp.dot(left, right, preferred_element_type=F32)


def dot_nt(left, right):
    return lax.dot_general(left, right, (((1,), (1,)), ((), ())), preferred_element_type=F32)


def unit(raw):
    recip = lax.rsqrt(jnp.mean(raw * raw, axis=-1, keepdims=True) + EPS)
    return raw * recip, recip


def norm_back(upstream, unit_rows, recip, gain):
    scaled = upstream * gain
    return recip * (scaled - unit_rows * jnp.mean(unit_rows * scaled, axis=-1, keepdims=True))


def gain_rows(term):
    upper = term.astype(BF16).astype(F32)
    rows = jnp.concatenate([upper, term - upper, jnp.zeros((TAIL - 2, term.shape[1]), F32)], axis=0)
    return rows.astype(BF16)


def gain_term(rows):
    return rows[0:1].astype(F32) + rows[1:2].astype(F32)


def params(limit=VMEM_LIMIT):
    return pltpu.CompilerParams(vmem_limit_bytes=limit)


def cost(flops, size):
    return pl.CostEstimate(flops=flops, bytes_accessed=size, transcendentals=0)


def causal_kernel(mask_ref):
    key_no = lax.broadcasted_iota(jnp.int32, mask_ref.shape, 0)
    token_no = lax.broadcasted_iota(jnp.int32, mask_ref.shape, 1) % CL
    mask_ref[...] = jnp.where(key_no <= token_no, 0.0, -jnp.inf)


def causal():
    return pl.pallas_call(
        causal_kernel,
        out_specs=VMEM_SPEC,
        out_shape=jax.ShapeDtypeStruct((CL, CHUNK), F32),
        compiler_params=params(),
        cost_estimate=cost(4 * 10**9, 10**6),
        name="causal",
    )()


def pack_kernel(keys_ref, values_ref, kg_ref, out_ref):
    size, width = kg_ref.shape[1], keys_ref.shape[1]
    for head in range(width // size):
        columns = slice(head * size, (head + 1) * size)
        unit_rows, _ = unit(keys_ref[:, columns].astype(F32))
        out_ref[:, columns] = (unit_rows * kg_ref[...]).astype(BF16)
    out_ref[:, width:] = values_ref[...]


def pack(keys, values, key_gain):
    return pl.pallas_call(
        pack_kernel,
        in_specs=[VMEM_SPEC] * 3,
        out_specs=VMEM_SPEC,
        out_shape=jax.ShapeDtypeStruct((keys.shape[0], 2 * keys.shape[1]), BF16),
        compiler_params=params(),
        cost_estimate=cost(4 * 10**9, 10**6),
        name="pack",
    )(keys, values, key_gain)


def head_columns(head, group, size):
    return [slice((head * group + g) * size, (head * group + g + 1) * size) for g in range(group)]


def slot_rows(slot):
    return pl.ds(pl.multiple_of(slot * CL, CL), CL)


def prepare_kernel(live_ref, q_ref, do_ref, qg_ref, raw_ref, recip_ref, queries_ref, grads_ref, col_ref, rows_ref):
    size = col_ref.shape[0]
    heads = raw_ref.shape[1] // size
    group = q_ref.shape[1] // raw_ref.shape[1]
    column = jnp.broadcast_to(qg_ref[...], (size, size)).T
    for at in range(0, col_ref.shape[1], size):
        col_ref[:, at:at + size] = column

    def live(slot, carry):
        for head in range(heads):
            places = head_columns(head, group, size)
            rows = slice(head * size, (head + 1) * size)
            half = jnp.concatenate([q_ref[slot_rows(slot), place] for place in places], axis=0).T
            raw_ref[slot, rows, :] = half
            raw = half.astype(F32)
            recip = lax.rsqrt(jnp.mean(raw * raw, axis=0, keepdims=True) + EPS)
            recip_ref[slot, head:head + 1, :] = recip
            queries = (raw * recip * col_ref[...]).astype(BF16)
            queries_ref[slot, rows, :] = queries
            rows_ref[slot, head] = queries.T
            grads_ref[slot, rows, :] = jnp.concatenate([do_ref[slot_rows(slot), place] for place in places], axis=0).T
        return carry

    lax.fori_loop(0, live_ref[0], live, 0)


def prepare(live_counts, queries, out_grad, query_gain, slots, width):
    size = query_gain.shape[1]
    lanes = queries.shape[1] // width * CL
    turned = jax.ShapeDtypeStruct((slots, width, lanes), BF16)
    return pl.pallas_call(
        prepare_kernel,
        in_specs=[SMEM_SPEC] + [VMEM_SPEC] * 3,
        out_specs=[VMEM_SPEC] * 6,
        out_shape=[
            turned, jax.ShapeDtypeStruct((slots, 8, lanes), F32), turned, turned,
            jax.ShapeDtypeStruct((size, lanes), F32),
            jax.ShapeDtypeStruct((slots, width // size, lanes, size), BF16),
        ],
        compiler_params=params(),
        cost_estimate=cost(2 * 10**9, 6 * queries.size),
        name="prepare",
    )(live_counts, queries, out_grad, query_gain)


def attention_kernel(*refs, parts, heads):
    live_ref, prompt_ref, me_ref, queries_ref, query_rows, grads_ref, ck_ref, cv_ref, kg_ref, mask_ref = refs[:10]
    pieces, refs = refs[10:10 + parts], refs[10 + parts:]
    att_ref, ds_ref, pool_keys, own_keys, own_acc, term_ref, keep_ref = refs[:7]
    send_ref, refs = (refs[7], refs[8:]) if parts > 1 else (None, refs[7:])
    acc, pool_values, pool_values_t, own_values_t = refs[:4]
    size = kg_ref.shape[1]
    width = heads * size
    slots, _, lanes = queries_ref.shape
    per_head = lanes // CHUNK
    count = heads * per_head
    weights, grads = refs[4:4 + heads], refs[4 + heads:4 + 2 * heads]
    scores, summed = refs[4 + 2 * heads:4 + 2 * heads + count], refs[4 + 2 * heads + count:]
    score_scale = 1.0 / math.sqrt(size)
    shard = pieces[0].shape[0]

    def columns(head):
        return slice(head * size, (head + 1) * size)

    def piece_rows(piece_no):
        return pl.ds(pl.multiple_of((me_ref[0] ^ piece_no) * shard, shard), shard)

    acc[...] = jnp.zeros_like(acc)
    own_acc[...] = jnp.zeros_like(own_acc)
    for piece_no, piece in enumerate(pieces):
        pool_keys[piece_rows(piece_no), :] = piece[:, :width]
        pool_values[piece_rows(piece_no), :] = piece[:, width:]
    for head in range(heads):
        pool_values_t[columns(head), :] = pool_values[:, columns(head)].T
        own_unit, _ = unit(ck_ref[:, columns(head)].astype(F32))
        own_keys[:, columns(head)] = (own_unit * kg_ref[...]).astype(BF16)
        for slot in range(slots):
            own_values_t[slot, head] = cv_ref[slot * CL:(slot + 1) * CL, columns(head)].T

    def prompt_rows(slot):
        return pl.ds(pl.multiple_of(prompt_ref[slot] * PL, PL), PL)

    def part(no):
        head = no // per_head
        return head, columns(head), slice(no % per_head * CHUNK, (no % per_head + 1) * CHUNK)

    def begin(slot, no):
        _, place, span = part(no)
        keys = jnp.concatenate([pool_keys[prompt_rows(slot), place], own_keys[slot_rows(slot), place]], axis=0)
        scores[no][...] = dot(keys, queries_ref[slot, place, span])

    def weigh(slot, no):
        head, place, span = part(no)
        prompt, own = scores[no][:PL, :], scores[no][PL:, :] + mask_ref[...]
        factor = score_scale * math.log2(math.e)
        high = jnp.maximum(jnp.max(prompt, axis=0, keepdims=True), jnp.max(own, axis=0, keepdims=True))
        both = jnp.concatenate([prompt, own], axis=0)
        half = jnp.exp2((both - high) * factor).astype(BF16)
        weights[head][:, span] = half
        values_t = jnp.concatenate([pool_values_t[place, prompt_rows(slot)], own_values_t[slot, head]], axis=1)
        values_t = jnp.concatenate([values_t, jnp.ones((TAIL, PL + CL), BF16)], axis=0)
        summed[no][...] = dot(values_t, half)

    def back(slot, no):
        head, place, span = part(no)
        inverse = 1.0 / summed[no][size:size + 1, :]
        attended = (summed[no][:size, :] * inverse).astype(BF16)
        att_ref[slot, place, span] = attended
        scaled = (grads_ref[slot, place, span].astype(F32) * inverse).astype(BF16)
        grads[head][:, span] = scaled
        delta = jnp.sum(scaled.astype(F32) * attended.astype(F32), axis=0, keepdims=True)
        values = jnp.concatenate([pool_values[prompt_rows(slot), place], cv_ref[slot_rows(slot), place]], axis=0)
        score_grad = weights[head][:, span].astype(F32) * (dot(values, scaled) - delta)
        ds_ref[slot, head, :, span] = score_grad.astype(BF16)

    def close(slot, head):
        value_grad = dot_nt(weights[head][...], grads[head][...])
        key_grad = dot(ds_ref[slot, head], query_rows[slot, head])
        acc[prompt_rows(slot), columns(head)] += key_grad[:PL]
        acc[prompt_rows(slot), width + head * size:width + (head + 1) * size] += value_grad[:PL]
        own_acc[slot, head, 0] = key_grad[PL:]
        own_acc[slot, head, 1] = value_grad[PL:]

    def ticks(now, before):
        for tick in range(count):
            if now is not None:
                begin(now, tick)
            for number, stage in ((1, weigh), (2, back)):
                slot = now if tick >= number else before
                if slot is not None:
                    stage(slot, (tick - number) % count)
            wait = 3 if per_head > 1 else 2
            done = (tick - wait) % count
            slot = now if tick >= wait else before
            if slot is not None and done % per_head == per_head - 1:
                close(slot, done // per_head)

    def step(slot, carry):
        ticks(slot, slot - 1)
        return carry

    ticks(0, None)
    lax.fori_loop(1, live_ref[0], step, 0)
    ticks(None, live_ref[0] - 1)

    total = jnp.zeros((1, size), F32)
    for head in range(heads):
        own_grad = own_acc[:, head, 0].reshape(slots * CL, size)
        total = total + jnp.sum(own_grad * own_keys[:, columns(head)].astype(F32), axis=0, keepdims=True)
        pool_term = acc[:, columns(head)] * pool_keys[:, columns(head)].astype(F32)
        total = total + jnp.sum(pool_term, axis=0, keepdims=True)
    term_ref[...] = jnp.broadcast_to(total * score_scale, term_ref.shape)
    if parts == 1:
        keep_ref[:, :width] = acc[:, :width] * score_scale
        keep_ref[:, width:] = acc[:, width:]
    else:
        for piece_no in range(parts):
            place = slice(piece_no // 2 * shard, (piece_no // 2 + 1) * shard)
            ref = keep_ref if piece_no % 2 == 0 else send_ref
            ref[place, :width] = (acc[piece_rows(piece_no), :width] * score_scale).astype(ref.dtype)
            ref[place, width:] = acc[piece_rows(piece_no), width:].astype(ref.dtype)


def attention(live_counts, slot_prompts, me, queries, query_rows, grads, keys, values, key_gain, mask, pieces):
    size = key_gain.shape[1]
    slots, width, lanes = queries.shape
    heads = width // size
    parts = len(pieces)
    pool_rows = parts * pieces[0].shape[0]
    count = heads * lanes // CHUNK
    span = PL + CL
    out_shape = [
        jax.ShapeDtypeStruct(queries.shape, BF16),
        jax.ShapeDtypeStruct((slots, heads, span, lanes), BF16),
        jax.ShapeDtypeStruct((pool_rows, width), BF16),
        jax.ShapeDtypeStruct(keys.shape, BF16),
        jax.ShapeDtypeStruct((slots, heads, 2, CL, size), F32),
        jax.ShapeDtypeStruct((8, size), F32),
    ]
    if parts > 1:
        half = (pool_rows // 2, 2 * width)
        out_shape += [jax.ShapeDtypeStruct(half, F32), jax.ShapeDtypeStruct(half, BF16)]
    else:
        out_shape += [jax.ShapeDtypeStruct((pool_rows, 2 * width), F32)]
    return pl.pallas_call(
        functools.partial(attention_kernel, parts=parts, heads=heads),
        in_specs=[SMEM_SPEC] * 3 + [VMEM_SPEC] * (7 + parts),
        out_specs=[VMEM_SPEC] * len(out_shape),
        out_shape=out_shape,
        scratch_shapes=[
            pltpu.VMEM((pool_rows, 2 * width), F32),
            pltpu.VMEM((pool_rows, width), BF16),
            pltpu.VMEM((width, pool_rows), BF16),
            pltpu.VMEM((slots, heads, size, CL), BF16),
        ]
        + [pltpu.VMEM((span, lanes), BF16)] * heads
        + [pltpu.VMEM((size, lanes), BF16)] * heads
        + [pltpu.VMEM((span, CHUNK), F32)] * count
        + [pltpu.VMEM((size + TAIL, CHUNK), F32)] * count,
        compiler_params=params(),
        cost_estimate=cost(3 * 10**9, 10**7),
        name="attention",
    )(live_counts, slot_prompts, me, queries, query_rows, grads, keys, values, key_gain, mask, *pieces)


def copy_slots(live_ref, zeros, out, target, sems):
    slots = out.shape[0]

    def copy(source, slot):
        return pltpu.make_async_copy(source, target.at[slot_rows(slot), :], sems.at[slot])

    def dead(slot, carry):
        copy(zeros, slot).start()
        return carry

    def wait():
        for slot in range(slots):
            copy(zeros, slot).wait()

    zeros[...] = jnp.zeros_like(zeros)
    lax.fori_loop(live_ref[0], slots, dead, 0)
    return lambda slot: copy(out.at[slot], slot).start(), wait


def turn_kernel(
    live_ref, att_t_ref, own_acc, ck_ref, kg_ref, att_ref, dk_ref, dv_ref, att_out, zeros, dk_out, dv_out, sems, own_sems,
):
    slots, width, _ = att_t_ref.shape
    size = kg_ref.shape[1]
    heads = width // size
    group = att_ref.shape[1] // width
    start, wait = copy_slots(live_ref, zeros, att_out, att_ref, sems)

    def live(slot, carry):
        for head in range(heads):
            attended = att_t_ref[slot, head * size:(head + 1) * size, :].T
            for g, place in enumerate(head_columns(head, group, size)):
                att_out[slot, :, place] = attended[g * CL:(g + 1) * CL]
        start(slot)
        return carry

    lax.fori_loop(0, live_ref[0], live, 0)
    for head in range(heads):
        columns = slice(head * size, (head + 1) * size)
        own_grad = own_acc[:, head, 0].reshape(slots * CL, size) * (1.0 / math.sqrt(size))
        own_unit, own_recip = unit(ck_ref[:, columns].astype(F32))
        dk_out[:, columns] = norm_back(own_grad, own_unit, own_recip, kg_ref[...]).astype(BF16)
        dv_out[:, columns] = own_acc[:, head, 1].reshape(slots * CL, size).astype(BF16)
    own_copies = [
        pltpu.make_async_copy(dk_out, dk_ref, own_sems.at[0]),
        pltpu.make_async_copy(dv_out, dv_ref, own_sems.at[1]),
    ]
    for copy in own_copies:
        copy.start()
    for copy in own_copies:
        copy.wait()
    wait()


def turn(live_counts, att_t, own_acc, keys, key_gain, shape):
    slots = att_t.shape[0]
    own = jax.ShapeDtypeStruct(keys.shape, BF16)
    own_slab = pltpu.VMEM(keys.shape, BF16)
    return pl.pallas_call(
        turn_kernel,
        in_specs=[SMEM_SPEC] + [VMEM_SPEC] * 4,
        out_specs=[HBM_SPEC] * 3,
        out_shape=[jax.ShapeDtypeStruct(shape, BF16), own, own],
        scratch_shapes=[
            pltpu.VMEM((slots, CL, shape[1]), BF16), pltpu.VMEM((CL, shape[1]), BF16), own_slab, own_slab,
            pltpu.SemaphoreType.DMA((slots,)), pltpu.SemaphoreType.DMA((2,)),
        ],
        compiler_params=params(),
        cost_estimate=cost(6 * 10**9, 2 * 10**6),
        name="turn",
    )(live_counts, att_t, own_acc, keys, key_gain)


def post_kernel(
    live_ref, prompt_ref, ds_ref, pool_keys, own_keys_ref, raw_ref, recip_ref, col_ref, dq_ref, dq_out, zeros, sems,
):
    slots, width, lanes = raw_ref.shape
    size = col_ref.shape[0]
    heads = width // size
    group = dq_ref.shape[1] // width
    score_scale = 1.0 / math.sqrt(size)
    start, wait = copy_slots(live_ref, zeros, dq_out, dq_ref, sems)

    def live(slot, carry):
        rows = pl.ds(pl.multiple_of(prompt_ref[slot] * PL, PL), PL)
        for head in range(heads):
            columns = slice(head * size, (head + 1) * size)
            keys_t = jnp.concatenate([pool_keys[rows, columns], own_keys_ref[slot_rows(slot), columns]], axis=0).T
            query_grad = dot(keys_t, ds_ref[slot, head]) * score_scale
            recip = recip_ref[slot, head:head + 1, :]
            query_unit = raw_ref[slot, columns, :].astype(F32) * recip
            scaled = query_grad * col_ref[...]
            mean = jnp.mean(query_unit * scaled, axis=0, keepdims=True)
            query_out = (recip * (scaled - query_unit * mean)).astype(BF16).T
            for g, place in enumerate(head_columns(head, group, size)):
                dq_out[slot, :, place] = query_out[g * CL:(g + 1) * CL]
        start(slot)
        return carry

    lax.fori_loop(0, live_ref[0], live, 0)
    wait()


def post(live_counts, slot_prompts, score_grads, pool_keys, own_keys, raw, recip, query_col, shape):
    slots = raw.shape[0]
    return pl.pallas_call(
        post_kernel,
        in_specs=[SMEM_SPEC] * 2 + [VMEM_SPEC] * 6,
        out_specs=HBM_SPEC,
        out_shape=jax.ShapeDtypeStruct(shape, BF16),
        scratch_shapes=[
            pltpu.VMEM((slots, CL, shape[1]), BF16), pltpu.VMEM((CL, shape[1]), BF16),
            pltpu.SemaphoreType.DMA((slots,)),
        ],
        compiler_params=params(),
        cost_estimate=cost(3 * 10**9, 4 * 10**6),
        name="post",
    )(live_counts, slot_prompts, score_grads, pool_keys, own_keys, raw, recip, query_col)


def tree(terms):
    while len(terms) > 1:
        terms = [left + right for left, right in zip(terms[::2], terms[1::2])]
    return terms[0]


def add_kernel(keep_ref, came_ref, *refs, terms):
    tail = gain_rows(tree([ref[0:1, :] for ref in refs[:terms]]))
    size = tail.shape[1]
    own_ref, send_refs = refs[terms], refs[terms + 1:]
    blocks = len(send_refs) + 1
    shard = keep_ref.shape[0] // blocks
    for at in range(blocks):
        place = slice(at * shard, (at + 1) * shard)
        ref = send_refs[blocks - 1 - at] if at > 0 else own_ref
        total = keep_ref[place, :] + came_ref[place, :].astype(F32)
        for slab in range(keep_ref.shape[1] // size):
            ref[slab * shard:(slab + 1) * shard, :] = total[:, slab * size:(slab + 1) * size].astype(ref.dtype)
        ref[ref.shape[0] - TAIL:, :] = tail.astype(ref.dtype)


def add(keep, came, terms, blocks):
    size = terms[0].shape[1]
    shape = (keep.size // blocks // size + TAIL, size)
    return pl.pallas_call(
        functools.partial(add_kernel, terms=len(terms)),
        in_specs=[VMEM_SPEC] * (2 + len(terms)),
        out_specs=[VMEM_SPEC] * blocks,
        out_shape=[jax.ShapeDtypeStruct(shape, F32)] + [jax.ShapeDtypeStruct(shape, BF16)] * (blocks - 1),
        compiler_params=params(),
        name="add",
    )(keep, came, *terms)


def chips_kernel(*refs):
    parts = [gain_term(ref[ref.shape[0] - TAIL:, :]) for ref in refs[:-1]]
    total = tree(parts[:1] + parts[:0:-1])
    refs[-1][...] = jnp.broadcast_to(total, refs[-1].shape)


def sum_chips(blocks):
    return pl.pallas_call(
        chips_kernel,
        in_specs=[VMEM_SPEC] * len(blocks),
        out_specs=VMEM_SPEC,
        out_shape=jax.ShapeDtypeStruct((8, blocks[0].shape[1]), F32),
        compiler_params=params(),
        name="sum_chips",
    )(*blocks)


def last_kernel(*refs):
    terms, (qg_ref, kg_ref, query_ref, key_ref) = refs[:-4], refs[-4:]
    total = tree([ref[0:1, :] for ref in terms])
    query_ref[...] = total / qg_ref[...]
    key_ref[...] = total / kg_ref[...]


def gain_grads(terms, query_gain, key_gain):
    row = jax.ShapeDtypeStruct(query_gain.shape, F32)
    return pl.pallas_call(
        last_kernel,
        in_specs=[VMEM_SPEC] * (len(terms) + 2),
        out_specs=[VMEM_SPEC] * 2,
        out_shape=[row, row],
        compiler_params=params(),
        name="gain_grads",
    )(*terms, query_gain, key_gain)


def finish_kernel(*refs):
    parts, (raw_ref, kg_ref, key_ref, value_ref) = refs[:-4], refs[-4:]
    size = kg_ref.shape[1]
    shard, width = raw_ref.shape
    heads = width // size
    for slab in range(2 * heads):
        rows = slice(slab * shard, (slab + 1) * shard)
        total = parts[0][rows, :]
        for ref in parts[1:]:
            total = total + ref[rows, :].astype(F32)
        columns = slice(slab % heads * size, (slab % heads + 1) * size)
        if slab < heads:
            unit_rows, recip = unit(raw_ref[:, columns].astype(F32))
            key_ref[:, columns] = norm_back(total, unit_rows, recip, kg_ref[...])
        else:
            value_ref[:, columns] = total


def finish(blocks, raw, key_gain):
    shape = jax.ShapeDtypeStruct(raw.shape, F32)
    return pl.pallas_call(
        finish_kernel,
        in_specs=[VMEM_SPEC] * (len(blocks) + 2),
        out_specs=[VMEM_SPEC] * 2,
        out_shape=[shape, shape],
        compiler_params=params(),
        cost_estimate=cost(10**8, 10**6),
        name="finish",
    )(*blocks, raw, key_gain)


def swap(values, axis, step):
    return lax.ppermute(values, axis, [(i, i ^ step) for i in range(lax.axis_size(axis))])


def local(
    comp_queries, comp_keys, comp_values, prompt_keys, prompt_values,
    query_gain, key_gain, out_grad, live_counts, slot_prompts,
):
    grp, tp = lax.axis_size("grp"), lax.axis_size("tp")
    shard = prompt_keys.shape[0]
    size = query_gain.shape[0]
    by_permute = shard % 16 == 0 and grp > 1 and grp & (grp - 1) == 0 and tp & (tp - 1) == 0
    slots, width = slot_prompts.shape[0], comp_keys.shape[1]
    query_gain, key_gain = query_gain.reshape(1, size), key_gain.reshape(1, size)
    me = lax.axis_index("grp").astype(jnp.int32).reshape(1) if by_permute else jnp.zeros((1,), jnp.int32)
    mask, me, keys_in, values_in = lax.optimization_barrier((causal(), me, prompt_keys, prompt_values))
    mine = pack(keys_in, values_in, key_gain)
    raw, recip, queries, grads, query_col, query_rows = prepare(live_counts, comp_queries, out_grad, query_gain, slots, width)
    if by_permute:
        even = [mine] + [swap(mine, "grp", step) for step in range(2, grp, 2)]
        odd = [swap(mine, "grp", 1)] + [None] * (len(even) - 1)
        for at in range(len(even) - 1, 0, -1):
            if at == 1:
                even[at], query_col, odd[-1] = lax.optimization_barrier((even[at], query_col, odd[-1]))
            else:
                even[at], query_col = lax.optimization_barrier((even[at], query_col))
            odd[at] = swap(even[at], "grp", 1)
        pieces = [piece for pair in zip(even, odd) for piece in pair]
    else:
        pieces = [lax.all_gather(mine, "grp", axis=0, tiled=True)]
    att_t, score_grads, pool_keys, own_keys, own_acc, term, keep, *send = attention(
        live_counts, slot_prompts, me, queries, query_rows, grads, comp_keys, comp_values, key_gain, mask, pieces,
    )
    attended, key_grads, value_grads = turn(live_counts, att_t, own_acc, comp_keys, key_gain, comp_queries.shape)
    query_grads = post(
        live_counts, slot_prompts, score_grads, pool_keys, own_keys, raw, recip, query_col, comp_queries.shape,
    )
    if by_permute:
        came = swap(send[0], "grp", 1)
        terms = [term] + [swap(term, "tp", step) for step in range(1, tp)]
        terms, attended = lax.optimization_barrier((terms, attended))
        own, *blocks = add(keep, came, terms, grp // 2)
        blocks = [swap(block, "grp", grp - 2 - 2 * at) for at, block in enumerate(blocks)]
        blocks, query_grads = lax.optimization_barrier((blocks, query_grads))
        blocks = [own] + blocks
        total = sum_chips(blocks)
        terms = [total, swap(total, "grp", 1)]
    else:
        block = lax.psum_scatter(keep, "grp", scatter_dimension=0, tiled=True)
        blocks = [jnp.concatenate([block[:, at:at + size] for at in range(0, 2 * width, size)], axis=0)]
        terms = [lax.psum(term, ("grp", "tp"))]
    prompt_key_grads, prompt_value_grads = finish(blocks, prompt_keys, key_gain)
    query_gain_grad, key_gain_grad = gain_grads(terms, query_gain, key_gain)
    return (
        attended, query_grads, key_grads, value_grads, prompt_key_grads, prompt_value_grads,
        query_gain_grad.reshape(size), key_gain_grad.reshape(size),
    )


def solution(mesh):
    split, whole = P("grp", "tp"), P()
    return jax.shard_map(
        local,
        mesh=mesh,
        in_specs=(split, split, split, split, split, whole, whole, split, P("grp"), P("grp")),
        out_specs=(split, split, split, split, split, split, whole, whole),
        check_vma=False,
    )
```

```python
import functools
import math

import jax
import jax.numpy as jnp
from jax import lax
from jax.experimental import pallas as pl
from jax.experimental.pallas import tpu as pltpu
from jax.sharding import PartitionSpec as P

PL = 384
CL = 64
EPS = 1e-06
TAIL = 16
CHUNK = 512
VMEM_LIMIT = 24 * 1024 * 1024
F32 = jnp.float32
BF16 = jnp.bfloat16
SMEM_SPEC = pl.BlockSpec(memory_space=pltpu.SMEM)
VMEM_SPEC = pl.BlockSpec(memory_space=pltpu.VMEM)
HBM_SPEC = pl.BlockSpec(memory_space=pltpu.HBM)


def dot(left, right):
    return jnp.dot(left, right, preferred_element_type=F32)


def dot_nt(left, right):
    return lax.dot_general(left, right, (((1,), (1,)), ((), ())), preferred_element_type=F32)


def unit(raw):
    recip = lax.rsqrt(jnp.mean(raw * raw, axis=-1, keepdims=True) + EPS)
    return raw * recip, recip


def norm_back(upstream, unit_rows, recip, gain):
    scaled = upstream * gain
    return recip * (scaled - unit_rows * jnp.mean(unit_rows * scaled, axis=-1, keepdims=True))


def gain_rows(term):
    upper = term.astype(BF16).astype(F32)
    rows = jnp.concatenate([upper, term - upper, jnp.zeros((TAIL - 2, term.shape[1]), F32)], axis=0)
    return rows.astype(BF16)


def gain_term(rows):
    return rows[0:1].astype(F32) + rows[1:2].astype(F32)


def params(limit=VMEM_LIMIT):
    return pltpu.CompilerParams(vmem_limit_bytes=limit)


def cost(flops, size):
    return pl.CostEstimate(flops=flops, bytes_accessed=size, transcendentals=0)


def causal_kernel(mask_ref):
    key_no = lax.broadcasted_iota(jnp.int32, mask_ref.shape, 0)
    token_no = lax.broadcasted_iota(jnp.int32, mask_ref.shape, 1) % CL
    mask_ref[...] = jnp.where(key_no <= token_no, 0.0, -jnp.inf)


def causal():
    return pl.pallas_call(
        causal_kernel,
        out_specs=VMEM_SPEC,
        out_shape=jax.ShapeDtypeStruct((CL, CHUNK), F32),
        compiler_params=params(),
        cost_estimate=cost(4 * 10**9, 10**6),
        name="causal",
    )()


def pack_kernel(keys_ref, values_ref, kg_ref, out_ref):
    size, width = kg_ref.shape[1], keys_ref.shape[1]
    for head in range(width // size):
        columns = slice(head * size, (head + 1) * size)
        unit_rows, _ = unit(keys_ref[:, columns].astype(F32))
        out_ref[:, columns] = (unit_rows * kg_ref[...]).astype(BF16)
    out_ref[:, width:] = values_ref[...]


def pack(keys, values, key_gain):
    return pl.pallas_call(
        pack_kernel,
        in_specs=[VMEM_SPEC] * 3,
        out_specs=VMEM_SPEC,
        out_shape=jax.ShapeDtypeStruct((keys.shape[0], 2 * keys.shape[1]), BF16),
        compiler_params=params(),
        cost_estimate=cost(4 * 10**9, 10**6),
        name="pack",
    )(keys, values, key_gain)


def head_columns(head, group, size):
    return [slice((head * group + g) * size, (head * group + g + 1) * size) for g in range(group)]


def slot_rows(slot):
    return pl.ds(pl.multiple_of(slot * CL, CL), CL)


def prepare_kernel(live_ref, q_ref, do_ref, qg_ref, raw_ref, recip_ref, queries_ref, grads_ref, col_ref):
    size = col_ref.shape[0]
    heads = raw_ref.shape[1] // size
    group = q_ref.shape[1] // raw_ref.shape[1]
    column = jnp.broadcast_to(qg_ref[...], (size, size)).T
    for at in range(0, col_ref.shape[1], size):
        col_ref[:, at:at + size] = column

    def live(slot, carry):
        for head in range(heads):
            places = head_columns(head, group, size)
            rows = slice(head * size, (head + 1) * size)
            half = jnp.concatenate([q_ref[slot_rows(slot), place] for place in places], axis=0).T
            raw_ref[slot, rows, :] = half
            raw = half.astype(F32)
            recip = lax.rsqrt(jnp.mean(raw * raw, axis=0, keepdims=True) + EPS)
            recip_ref[slot, head:head + 1, :] = recip
            queries_ref[slot, rows, :] = (raw * recip * col_ref[...]).astype(BF16)
            grads_ref[slot, rows, :] = jnp.concatenate([do_ref[slot_rows(slot), place] for place in places], axis=0).T
        return carry

    lax.fori_loop(0, live_ref[0], live, 0)


def prepare(live_counts, queries, out_grad, query_gain, slots, width):
    size = query_gain.shape[1]
    lanes = queries.shape[1] // width * CL
    turned = jax.ShapeDtypeStruct((slots, width, lanes), BF16)
    return pl.pallas_call(
        prepare_kernel,
        in_specs=[SMEM_SPEC] + [VMEM_SPEC] * 3,
        out_specs=[VMEM_SPEC] * 5,
        out_shape=[
            turned, jax.ShapeDtypeStruct((slots, 8, lanes), F32), turned, turned,
            jax.ShapeDtypeStruct((size, lanes), F32),
        ],
        compiler_params=params(),
        cost_estimate=cost(2 * 10**9, 6 * queries.size),
        name="prepare",
    )(live_counts, queries, out_grad, query_gain)


def give_pieces(acc, me_ref, parts, keep_ref, send_ref, scale):
    if parts == 1:
        keep_ref[...] = acc[...] * scale
        return
    shard = acc.shape[0] // parts
    for piece_no in range(parts):
        rows = pl.ds(pl.multiple_of((me_ref[0] ^ piece_no) * shard, shard), shard)
        place = slice(piece_no // 2 * shard, (piece_no // 2 + 1) * shard)
        ref = keep_ref if piece_no % 2 == 0 else send_ref
        ref[place, :] = (acc[rows, :] * scale).astype(ref.dtype)


def piece_shapes(pool_rows, width, parts):
    if parts == 1:
        return [jax.ShapeDtypeStruct((pool_rows, width), F32)]
    return [jax.ShapeDtypeStruct((pool_rows // 2, width), kind) for kind in (F32, BF16)]


def attention_kernel(*refs, parts, heads):
    live_ref, prompt_ref, me_ref, queries_ref, grads_ref, ck_ref, cv_ref, kg_ref, mask_ref = refs[:9]
    pieces, refs = refs[9:9 + parts], refs[9 + parts:]
    att_ref, ds_ref, weights, grads, pool_keys, own_keys, own_acc, term_ref, keep_ref = refs[:9]
    send_ref, refs = (refs[9], refs[10:]) if parts > 1 else (None, refs[9:])
    acc, pool_values, pool_values_t, own_values_t = refs[:4]
    size = kg_ref.shape[1]
    width = heads * size
    slots, _, lanes = queries_ref.shape
    per_head = lanes // CHUNK
    count = heads * per_head
    scores, summed = refs[4:4 + count], refs[4 + count:]
    score_scale = 1.0 / math.sqrt(size)
    shard = pieces[0].shape[0]

    def columns(head):
        return slice(head * size, (head + 1) * size)

    def piece_rows(piece_no):
        return pl.ds(pl.multiple_of((me_ref[0] ^ piece_no) * shard, shard), shard)

    acc[...] = jnp.zeros_like(acc)
    own_acc[...] = jnp.zeros_like(own_acc)
    for piece_no, piece in enumerate(pieces):
        pool_keys[piece_rows(piece_no), :] = piece[:, :width]
        pool_values[piece_rows(piece_no), :] = piece[:, width:]
    for head in range(heads):
        pool_values_t[columns(head), :] = pool_values[:, columns(head)].T
        own_unit, _ = unit(ck_ref[:, columns(head)].astype(F32))
        own_keys[:, columns(head)] = (own_unit * kg_ref[...]).astype(BF16)
        for slot in range(slots):
            own_values_t[slot, head] = cv_ref[slot * CL:(slot + 1) * CL, columns(head)].T

    def prompt_rows(slot):
        return pl.ds(pl.multiple_of(prompt_ref[slot] * PL, PL), PL)

    def part(no):
        head = no // per_head
        return head, columns(head), slice(no % per_head * CHUNK, (no % per_head + 1) * CHUNK)

    def begin(slot, no):
        _, place, span = part(no)
        keys = jnp.concatenate([pool_keys[prompt_rows(slot), place], own_keys[slot_rows(slot), place]], axis=0)
        scores[no][...] = dot(keys, queries_ref[slot, place, span])

    def weigh(slot, no):
        head, place, span = part(no)
        prompt, own = scores[no][:PL, :], scores[no][PL:, :] + mask_ref[...]
        factor = score_scale * math.log2(math.e)
        high = jnp.maximum(jnp.max(prompt, axis=0, keepdims=True), jnp.max(own, axis=0, keepdims=True))
        both = jnp.concatenate([prompt, own], axis=0)
        half = jnp.exp2((both - high) * factor).astype(BF16)
        weights[slot, head, :, span] = half
        values_t = jnp.concatenate([pool_values_t[place, prompt_rows(slot)], own_values_t[slot, head]], axis=1)
        values_t = jnp.concatenate([values_t, jnp.ones((TAIL, PL + CL), BF16)], axis=0)
        summed[no][...] = dot(values_t, half)

    def back(slot, no):
        head, place, span = part(no)
        inverse = 1.0 / summed[no][size:size + 1, :]
        attended = (summed[no][:size, :] * inverse).astype(BF16)
        att_ref[slot, place, span] = attended
        scaled = (grads_ref[slot, place, span].astype(F32) * inverse).astype(BF16)
        grads[slot, place, span] = scaled
        delta = jnp.sum(scaled.astype(F32) * attended.astype(F32), axis=0, keepdims=True)
        values = jnp.concatenate([pool_values[prompt_rows(slot), place], cv_ref[slot_rows(slot), place]], axis=0)
        score_grad = weights[slot, head, :, span].astype(F32) * (dot(values, scaled) - delta)
        ds_ref[slot, head, :, span] = score_grad.astype(BF16)

    def close(slot, head):
        key_grad = dot_nt(ds_ref[slot, head], queries_ref[slot, columns(head), :])
        acc[prompt_rows(slot), columns(head)] += key_grad[:PL]
        own_acc[slot, head] = key_grad[PL:]

    def ticks(now, before):
        for tick in range(count):
            if now is not None:
                begin(now, tick)
            for number, stage in ((1, weigh), (2, back)):
                slot = now if tick >= number else before
                if slot is not None:
                    stage(slot, (tick - number) % count)
            wait = 3 if per_head > 1 else 2
            done = (tick - wait) % count
            slot = now if tick >= wait else before
            if slot is not None and done % per_head == per_head - 1:
                close(slot, done // per_head)

    def step(slot, carry):
        ticks(slot, slot - 1)
        return carry

    ticks(0, None)
    lax.fori_loop(1, live_ref[0], step, 0)
    ticks(None, live_ref[0] - 1)

    total = jnp.zeros((1, size), F32)
    for head in range(heads):
        own_grad = own_acc[:, head].reshape(slots * CL, size)
        total = total + jnp.sum(own_grad * own_keys[:, columns(head)].astype(F32), axis=0, keepdims=True)
        pool_term = acc[:, columns(head)] * pool_keys[:, columns(head)].astype(F32)
        total = total + jnp.sum(pool_term, axis=0, keepdims=True)
    term_ref[...] = jnp.broadcast_to(total * score_scale, term_ref.shape)
    give_pieces(acc, me_ref, parts, keep_ref, send_ref, score_scale)


def attention(live_counts, slot_prompts, me, queries, grads, keys, values, key_gain, mask, pieces):
    size = key_gain.shape[1]
    slots, width, lanes = queries.shape
    heads = width // size
    parts = len(pieces)
    pool_rows = parts * pieces[0].shape[0]
    count = heads * lanes // CHUNK
    span = PL + CL
    per_slot = jax.ShapeDtypeStruct((slots, heads, span, lanes), BF16)
    turned = jax.ShapeDtypeStruct(queries.shape, BF16)
    out_shape = [
        turned, per_slot, per_slot, turned,
        jax.ShapeDtypeStruct((pool_rows, width), BF16),
        jax.ShapeDtypeStruct(keys.shape, BF16),
        jax.ShapeDtypeStruct((slots, heads, CL, size), F32),
        jax.ShapeDtypeStruct((8, size), F32),
    ] + piece_shapes(pool_rows, width, parts)
    return pl.pallas_call(
        functools.partial(attention_kernel, parts=parts, heads=heads),
        in_specs=[SMEM_SPEC] * 3 + [VMEM_SPEC] * (6 + parts),
        out_specs=[VMEM_SPEC] * len(out_shape),
        out_shape=out_shape,
        scratch_shapes=[
            pltpu.VMEM((pool_rows, width), F32),
            pltpu.VMEM((pool_rows, width), BF16),
            pltpu.VMEM((width, pool_rows), BF16),
            pltpu.VMEM((slots, heads, size, CL), BF16),
        ]
        + [pltpu.VMEM((span, CHUNK), F32)] * count
        + [pltpu.VMEM((size + TAIL, CHUNK), F32)] * count,
        compiler_params=params(),
        cost_estimate=cost(3 * 10**9, 10**7),
        name="attention",
    )(live_counts, slot_prompts, me, queries, grads, keys, values, key_gain, mask, *pieces)


def values_kernel(live_ref, prompt_ref, me_ref, weights, grads, own_acc, keep_ref, *refs, parts):
    send_ref, acc = refs if parts > 1 else (None, refs[0])
    slots, heads, _, _ = weights.shape
    size = own_acc.shape[3]
    acc[...] = jnp.zeros_like(acc)
    own_acc[...] = jnp.zeros_like(own_acc)

    def live(slot, carry):
        rows = pl.ds(pl.multiple_of(prompt_ref[slot] * PL, PL), PL)
        for head in range(heads):
            columns = slice(head * size, (head + 1) * size)
            value_grad = dot_nt(weights[slot, head], grads[slot, columns, :])
            acc[rows, columns] += value_grad[:PL]
            own_acc[slot, head] = value_grad[PL:]
        return carry

    lax.fori_loop(0, live_ref[0], live, 0)
    give_pieces(acc, me_ref, parts, keep_ref, send_ref, 1.0)


def value_grads(live_counts, slot_prompts, me, weights, grads, pool_rows, parts):
    slots, heads, _, _ = weights.shape
    width = grads.shape[1]
    out_shape = [jax.ShapeDtypeStruct((slots, heads, CL, width // heads), F32)]
    out_shape += piece_shapes(pool_rows, width, parts)
    return pl.pallas_call(
        functools.partial(values_kernel, parts=parts),
        in_specs=[SMEM_SPEC] * 3 + [VMEM_SPEC] * 2,
        out_specs=[VMEM_SPEC] * len(out_shape),
        out_shape=out_shape,
        scratch_shapes=[pltpu.VMEM((pool_rows, width), F32)],
        compiler_params=params(),
        cost_estimate=cost(2 * 10**9, 10**6),
        name="values",
    )(live_counts, slot_prompts, me, weights, grads)


def copy_slots(live_ref, zeros, out, target, sems):
    slots = out.shape[0]

    def copy(source, slot):
        return pltpu.make_async_copy(source, target.at[slot_rows(slot), :], sems.at[slot])

    def dead(slot, carry):
        copy(zeros, slot).start()
        return carry

    def wait():
        for slot in range(slots):
            copy(zeros, slot).wait()

    zeros[...] = jnp.zeros_like(zeros)
    lax.fori_loop(live_ref[0], slots, dead, 0)
    return lambda slot: copy(out.at[slot], slot).start(), wait


def turn_kernel(
    live_ref, att_t_ref, own_keys, ck_ref, kg_ref, att_ref, dk_ref, att_out, zeros, dk_out, sems, own_sem,
):
    slots, width, _ = att_t_ref.shape
    size = kg_ref.shape[1]
    heads = width // size
    group = att_ref.shape[1] // width
    start, wait = copy_slots(live_ref, zeros, att_out, att_ref, sems)

    def live(slot, carry):
        for head in range(heads):
            attended = att_t_ref[slot, head * size:(head + 1) * size, :].T
            for g, place in enumerate(head_columns(head, group, size)):
                att_out[slot, :, place] = attended[g * CL:(g + 1) * CL]
        start(slot)
        return carry

    lax.fori_loop(0, live_ref[0], live, 0)
    for head in range(heads):
        columns = slice(head * size, (head + 1) * size)
        own_grad = own_keys[:, head].reshape(slots * CL, size) * (1.0 / math.sqrt(size))
        own_unit, own_recip = unit(ck_ref[:, columns].astype(F32))
        dk_out[:, columns] = norm_back(own_grad, own_unit, own_recip, kg_ref[...]).astype(BF16)
    own_copy = pltpu.make_async_copy(dk_out, dk_ref, own_sem)
    own_copy.start()
    own_copy.wait()
    wait()


def turn(live_counts, att_t, own_keys, keys, key_gain, shape):
    slots = att_t.shape[0]
    return pl.pallas_call(
        turn_kernel,
        in_specs=[SMEM_SPEC] + [VMEM_SPEC] * 4,
        out_specs=[HBM_SPEC] * 2,
        out_shape=[jax.ShapeDtypeStruct(shape, BF16), jax.ShapeDtypeStruct(keys.shape, BF16)],
        scratch_shapes=[
            pltpu.VMEM((slots, CL, shape[1]), BF16), pltpu.VMEM((CL, shape[1]), BF16), pltpu.VMEM(keys.shape, BF16),
            pltpu.SemaphoreType.DMA((slots,)), pltpu.SemaphoreType.DMA,
        ],
        compiler_params=params(),
        cost_estimate=cost(6 * 10**9, 2 * 10**6),
        name="turn",
    )(live_counts, att_t, own_keys, keys, key_gain)


def post_kernel(
    live_ref, prompt_ref, ds_ref, pool_keys, own_keys_ref, own_values, raw_ref, recip_ref, col_ref,
    dq_ref, dv_ref, dq_out, zeros, dv_out, sems, own_sem,
):
    slots, width, lanes = raw_ref.shape
    size = col_ref.shape[0]
    heads = width // size
    group = dq_ref.shape[1] // width
    score_scale = 1.0 / math.sqrt(size)
    start, wait = copy_slots(live_ref, zeros, dq_out, dq_ref, sems)
    for head in range(heads):
        dv_out[:, head * size:(head + 1) * size] = own_values[:, head].reshape(slots * CL, size).astype(BF16)
    own_copy = pltpu.make_async_copy(dv_out, dv_ref, own_sem)
    own_copy.start()

    def live(slot, carry):
        rows = pl.ds(pl.multiple_of(prompt_ref[slot] * PL, PL), PL)
        for head in range(heads):
            columns = slice(head * size, (head + 1) * size)
            keys_t = jnp.concatenate([pool_keys[rows, columns], own_keys_ref[slot_rows(slot), columns]], axis=0).T
            query_grad = dot(keys_t, ds_ref[slot, head]) * score_scale
            recip = recip_ref[slot, head:head + 1, :]
            query_unit = raw_ref[slot, columns, :].astype(F32) * recip
            scaled = query_grad * col_ref[...]
            mean = jnp.mean(query_unit * scaled, axis=0, keepdims=True)
            query_out = (recip * (scaled - query_unit * mean)).astype(BF16).T
            for g, place in enumerate(head_columns(head, group, size)):
                dq_out[slot, :, place] = query_out[g * CL:(g + 1) * CL]
        start(slot)
        return carry

    lax.fori_loop(0, live_ref[0], live, 0)
    own_copy.wait()
    wait()


def post(live_counts, slot_prompts, score_grads, pool_keys, own_keys, own_values, raw, recip, query_col, shape):
    slots = raw.shape[0]
    return pl.pallas_call(
        post_kernel,
        in_specs=[SMEM_SPEC] * 2 + [VMEM_SPEC] * 7,
        out_specs=[HBM_SPEC] * 2,
        out_shape=[jax.ShapeDtypeStruct(shape, BF16), jax.ShapeDtypeStruct(own_keys.shape, BF16)],
        scratch_shapes=[
            pltpu.VMEM((slots, CL, shape[1]), BF16), pltpu.VMEM((CL, shape[1]), BF16), pltpu.VMEM(own_keys.shape, BF16),
            pltpu.SemaphoreType.DMA((slots,)), pltpu.SemaphoreType.DMA,
        ],
        compiler_params=params(),
        cost_estimate=cost(3 * 10**9, 4 * 10**6),
        name="post",
    )(live_counts, slot_prompts, score_grads, pool_keys, own_keys, own_values, raw, recip, query_col)


def tree(terms):
    while len(terms) > 1:
        terms = [left + right for left, right in zip(terms[::2], terms[1::2])]
    return terms[0]


def add_kernel(*refs, terms):
    halves, refs = (refs[:2], refs[2:4]), refs[4:]
    tail = gain_rows(tree([ref[0:1, :] for ref in refs[:terms]]))
    size = tail.shape[1]
    own_ref, send_refs = refs[terms], refs[terms + 1:]
    blocks = len(send_refs) + 1
    rows, width = halves[0][0].shape
    shard = rows // blocks
    heads = width // size
    for at in range(blocks):
        place = slice(at * shard, (at + 1) * shard)
        ref = send_refs[blocks - 1 - at] if at > 0 else own_ref
        for slab in range(2 * heads):
            keep_ref, came_ref = halves[slab // heads]
            columns = slice(slab % heads * size, (slab % heads + 1) * size)
            total = keep_ref[place, columns] + came_ref[place, columns].astype(F32)
            ref[slab * shard:(slab + 1) * shard, :] = total.astype(ref.dtype)
        ref[2 * heads * shard:, :] = tail.astype(ref.dtype)


def add(keys, values, terms, blocks):
    size = terms[0].shape[1]
    shape = (2 * keys[0].size // blocks // size + TAIL, size)
    return pl.pallas_call(
        functools.partial(add_kernel, terms=len(terms)),
        in_specs=[VMEM_SPEC] * (4 + len(terms)),
        out_specs=[VMEM_SPEC] * blocks,
        out_shape=[jax.ShapeDtypeStruct(shape, F32)] + [jax.ShapeDtypeStruct(shape, BF16)] * (blocks - 1),
        compiler_params=params(),
        name="add",
    )(*keys, *values, *terms)


def chips_kernel(*refs):
    parts = [gain_term(ref[ref.shape[0] - TAIL:, :]) for ref in refs[:-1]]
    total = tree(parts[:1] + parts[:0:-1])
    refs[-1][...] = jnp.broadcast_to(total, refs[-1].shape)


def sum_chips(blocks):
    return pl.pallas_call(
        chips_kernel,
        in_specs=[VMEM_SPEC] * len(blocks),
        out_specs=VMEM_SPEC,
        out_shape=jax.ShapeDtypeStruct((8, blocks[0].shape[1]), F32),
        compiler_params=params(),
        name="sum_chips",
    )(*blocks)


def last_kernel(*refs):
    terms, (qg_ref, kg_ref, query_ref, key_ref) = refs[:-4], refs[-4:]
    total = tree([ref[0:1, :] for ref in terms])
    query_ref[...] = total / qg_ref[...]
    key_ref[...] = total / kg_ref[...]


def gain_grads(terms, query_gain, key_gain):
    row = jax.ShapeDtypeStruct(query_gain.shape, F32)
    return pl.pallas_call(
        last_kernel,
        in_specs=[VMEM_SPEC] * (len(terms) + 2),
        out_specs=[VMEM_SPEC] * 2,
        out_shape=[row, row],
        compiler_params=params(),
        name="gain_grads",
    )(*terms, query_gain, key_gain)


def finish_kernel(*refs):
    parts, (raw_ref, kg_ref, key_ref, value_ref) = refs[:-4], refs[-4:]
    size = kg_ref.shape[1]
    shard, width = raw_ref.shape
    heads = width // size
    for slab in range(2 * heads):
        rows = slice(slab * shard, (slab + 1) * shard)
        total = parts[0][rows, :]
        for ref in parts[1:]:
            total = total + ref[rows, :].astype(F32)
        columns = slice(slab % heads * size, (slab % heads + 1) * size)
        if slab < heads:
            unit_rows, recip = unit(raw_ref[:, columns].astype(F32))
            key_ref[:, columns] = norm_back(total, unit_rows, recip, kg_ref[...])
        else:
            value_ref[:, columns] = total


def finish(blocks, raw, key_gain):
    shape = jax.ShapeDtypeStruct(raw.shape, F32)
    return pl.pallas_call(
        finish_kernel,
        in_specs=[VMEM_SPEC] * (len(blocks) + 2),
        out_specs=[VMEM_SPEC] * 2,
        out_shape=[shape, shape],
        compiler_params=params(),
        cost_estimate=cost(10**8, 10**6),
        name="finish",
    )(*blocks, raw, key_gain)


def swap(values, axis, step):
    return lax.ppermute(values, axis, [(i, i ^ step) for i in range(lax.axis_size(axis))])


def local(
    comp_queries, comp_keys, comp_values, prompt_keys, prompt_values,
    query_gain, key_gain, out_grad, live_counts, slot_prompts,
):
    grp, tp = lax.axis_size("grp"), lax.axis_size("tp")
    shard = prompt_keys.shape[0]
    size = query_gain.shape[0]
    by_permute = shard % 16 == 0 and grp > 1 and grp & (grp - 1) == 0 and tp & (tp - 1) == 0
    slots, width = slot_prompts.shape[0], comp_keys.shape[1]
    query_gain, key_gain = query_gain.reshape(1, size), key_gain.reshape(1, size)
    me = lax.axis_index("grp").astype(jnp.int32).reshape(1) if by_permute else jnp.zeros((1,), jnp.int32)
    mask, me, keys_in, values_in = lax.optimization_barrier((causal(), me, prompt_keys, prompt_values))
    mine = pack(keys_in, values_in, key_gain)
    raw, recip, queries, grads, query_col = prepare(live_counts, comp_queries, out_grad, query_gain, slots, width)
    if by_permute:
        even = [mine] + [swap(mine, "grp", step) for step in range(2, grp, 2)]
        odd = [swap(mine, "grp", 1)] + [None] * (len(even) - 1)
        for at in range(len(even) - 1, 0, -1):
            if at == 1:
                even[at], query_col, odd[-1] = lax.optimization_barrier((even[at], query_col, odd[-1]))
            else:
                even[at], query_col = lax.optimization_barrier((even[at], query_col))
            odd[at] = swap(even[at], "grp", 1)
        pieces = [piece for pair in zip(even, odd) for piece in pair]
    else:
        pieces = [lax.all_gather(mine, "grp", axis=0, tiled=True)]
    att_t, score_grads, weights, grads, pool_keys, own_keys, own_key_acc, term, *key_pieces = attention(
        live_counts, slot_prompts, me, queries, grads, comp_keys, comp_values, key_gain, mask, pieces,
    )
    if by_permute:
        terms = [term] + [swap(term, "tp", step) for step in range(1, tp)]
    own_value_acc, *value_pieces = value_grads(
        live_counts, slot_prompts, me, weights, grads, pool_keys.shape[0], len(pieces),
    )
    attended, comp_key_grads = turn(live_counts, att_t, own_key_acc, comp_keys, key_gain, comp_queries.shape)
    query_grads, comp_value_grads = post(
        live_counts, slot_prompts, score_grads, pool_keys, own_keys, own_value_acc, raw, recip, query_col,
        comp_queries.shape,
    )
    if by_permute:
        key_pieces, value_pieces = ((keep, swap(send, "grp", 1)) for keep, send in (key_pieces, value_pieces))
        terms, attended = lax.optimization_barrier((terms, attended))
        own, *blocks = add(key_pieces, value_pieces, terms, grp // 2)
        blocks = [swap(block, "grp", grp - 2 - 2 * at) for at, block in enumerate(blocks)]
        blocks, query_grads = lax.optimization_barrier((blocks, query_grads))
        blocks = [own] + blocks
        total = sum_chips(blocks)
        terms = [total, swap(total, "grp", 1)]
    else:
        pool_grads = jnp.concatenate(key_pieces + value_pieces, axis=1)
        block = lax.psum_scatter(pool_grads, "grp", scatter_dimension=0, tiled=True)
        blocks = [jnp.concatenate([block[:, at:at + size] for at in range(0, 2 * width, size)], axis=0)]
        terms = [lax.psum(term, ("grp", "tp"))]
    prompt_key_grads, prompt_value_grads = finish(blocks, prompt_keys, key_gain)
    query_gain_grad, key_gain_grad = gain_grads(terms, query_gain, key_gain)
    return (
        attended, query_grads, comp_key_grads, comp_value_grads, prompt_key_grads, prompt_value_grads,
        query_gain_grad.reshape(size), key_gain_grad.reshape(size),
    )


def solution(mesh):
    split, whole = P("grp", "tp"), P()
    return jax.shard_map(
        local,
        mesh=mesh,
        in_specs=(split, split, split, split, split, whole, whole, split, P("grp"), P("grp")),
        out_specs=(split, split, split, split, split, split, whole, whole),
        check_vma=False,
    )
```
